512 devices in a mesh: gx: 32 (over x_lo, z, core), gy: 16 (over y, x_hi).
Axes of the slice: x: 4 (x_hi: 2, x_lo: 2; x = x_hi * 2 + x_lo), y: 8, z: 8, core: 2. Of those that a mesh axis runs over, the one named last changes fastest.
Arguments:
- concentration: float32 [3, 512, 256, 128], P(None, 'gx', 'gy'), may hold values from 0.2 to 2
- potential: float32 [512, 256, 128], P('gx', 'gy'), may hold values from -3 to 3
- permittivity: float32 [512, 256, 128], P('gx', 'gy'), may hold values from 0.5 to 4
- records: float32 [65536, 4, 128], P(('gx', 'gy')), may hold values from -3 to 3
- colloid_count: int32 [512], P(('gx', 'gy')), may hold values from 64 to 128, as said below
- move_slots: int32 [512, 4, 16], P(('gx', 'gy')), may hold values from 0 to 127, as said below
- move_count: int32 [512, 4], P(('gx', 'gy')), may hold values from 8 to 16, as said below
- own_nodes: int32 [65536, 128], P(('gx', 'gy')), may hold values from 0 to 41471, as said below
- arrive_nodes: int32 [512, 4, 16, 128], P(('gx', 'gy')), may hold values from 0 to 41471, as said below
Outputs:
- concentration_next: float32 [3, 512, 256, 128], P(None, 'gx', 'gy')
- potential_next: float32 [512, 256, 128], P('gx', 'gy')
- body_force: float32 [3, 512, 256, 128], P(None, 'gx', 'gy')
The draws below stay inside these ranges and needn't reach their ends.
Inputs may be any that keep to these rules, and one draw needn't show every extreme that they name: `colloid_count`: every brick has at least 64 live slots; some brick has all 128. `move_slots`: the slots of one brick named across all four directions are distinct and below that brick's colloid_count; entries at k >= move_count are ignored. `move_count`: in every direction some brick sends exactly 16. `own_nodes`: index ((x+1)(18) + (y+1)) * 128 + z of a cell of the brick extended by one cell on each side of its first two dimensions, x from -1 to 16 and y from -1 to 16. `arrive_nodes`: same form as own_nodes, for the receiving brick.
All inputs are finite; a program needn't handle non-finite values.
Results may differ from the reference program's by a relative error of at most 0.00002.
Values sent between devices are 32-bit elements; how exact they have to be, the bound alone decides.
No kernel may reach another device: no remote copies, remote signals or barrier semaphores. Data moves between devices by JAX's collectives and lax.ppermute only.
A program may use at most 128 MiB of HBM per device.

```python
import math
import jax
import jax.numpy as jnp

BX = 16
BY = 16
NZ = 128
C_DEV = 128
S = 128
SWEEPS = 8
M = 16
DEVS = 512
COLLOIDS = 65536
NX = 512
NY = 256
N_GX = 32
N_GY = 16


def mover_lists(key):
    subkeys = jax.random.split(key, 5)
    live_counts = jax.random.randint(subkeys[0], (DEVS,), C_DEV // 2, C_DEV + 1)
    fullest = jax.random.randint(subkeys[1], (), 0, DEVS)
    live_counts = live_counts.at[fullest].set(C_DEV)
    scores = jax.random.randint(subkeys[2], (DEVS, C_DEV), 1, 1 << 20)
    scores = scores.at[fullest, C_DEV - 1].set(0)
    slot_ids = jnp.arange(C_DEV, dtype=jnp.int32)[None, :]
    ranked = jnp.where(slot_ids < live_counts[:, None], scores, 1 << 20) * C_DEV + slot_ids
    ranking = jnp.argsort(ranked, axis=1).astype(jnp.int32)
    mover_slots = ranking[:, :4 * M].reshape(DEVS, 4, M)
    mover_counts = jax.random.randint(subkeys[3], (DEVS, 4), M // 2, M + 1)
    busiest = jax.random.randint(subkeys[4], (4,), 0, DEVS)
    mover_counts = mover_counts.at[busiest, jnp.arange(4)].set(M)
    return (live_counts, mover_slots, mover_counts)


def surface_cells(key, leading):
    subkeys = jax.random.split(key, 8)
    centre_x = jax.random.randint(subkeys[0], leading + (1,), 0, BX)
    centre_y = jax.random.randint(subkeys[1], leading + (1,), 0, BY)
    centre_z = jax.random.randint(subkeys[2], leading + (1,), 0, NZ)
    step_x = jax.random.randint(subkeys[3], leading + (S,), -1, 2)
    step_y = jax.random.randint(subkeys[4], leading + (S,), -1, 2)
    step_z = jax.random.randint(subkeys[5], leading + (S,), -3, 4)
    cells = ((centre_x + 1 + step_x) * (BY + 2) + (centre_y + 1 + step_y)) * NZ + (centre_z + step_z) % NZ
    flat_cells = cells.reshape(-1)
    entries = flat_cells.shape[0]
    corner_at = jax.random.randint(subkeys[6], (), 0, entries)
    anchor_at = (corner_at + 1 + jax.random.randint(subkeys[7], (), 0, entries - 1)) % entries
    flat_cells = flat_cells.at[corner_at].set((BX + 2) * (BY + 2) * NZ - 1)
    flat_cells = flat_cells.at[anchor_at].set(0)
    return flat_cells.reshape(cells.shape).astype(jnp.int32)


def draw_colloid_count(key, part):
    live_counts, mover_slots, mover_counts = mover_lists(key)
    return live_counts.astype(jnp.int32)


def draw_move_slots(key, part):
    live_counts, mover_slots, mover_counts = mover_lists(key)
    return mover_slots.astype(jnp.int32)


def draw_move_count(key, part):
    live_counts, mover_slots, mover_counts = mover_lists(key)
    return mover_counts.astype(jnp.int32)


def draw_own_nodes(key, part):
    key = jax.random.fold_in(key, 4)
    return surface_cells(key, (COLLOIDS,))


def draw_arrive_nodes(key, part):
    key = jax.random.fold_in(key, 5)
    return surface_cells(key, (DEVS, 4, M))


def steps_of(stream_key, extent, cuts, least, top_value):
    gain, own = 1.0, jax.random.fold_in(stream_key, 6)
    for position, blocks in cuts:
        steps = jnp.exp(jax.random.uniform(jax.random.fold_in(own, position), (blocks,), jnp.float32, least / len(cuts), top_value / len(cuts)))
        gain = gain * jnp.repeat(steps, extent[position] // blocks).reshape([-1 if axis == position else 1 for axis in range(len(extent))])
    return gain


def gaussian(stream_key, shape, spread, bound, cuts=(), kind=jnp.bfloat16):
    drawn = spread * jax.random.normal(stream_key, shape, jnp.float32)
    if cuts:
        drawn = drawn * steps_of(stream_key, shape, cuts, -0.22, 0.18)
    return jnp.clip(drawn, -bound, bound).astype(kind)


def setup_inputs(seed: int = 0) -> dict:
    key_of = jax.random.split(jax.random.key(seed), 10)
    return {
        "concentration": jnp.clip(0.2 + 1.8 * jax.random.uniform(key_of[0], (3, NX, NY, NZ), jnp.float32) ** steps_of(key_of[0], (3, NX, NY, NZ), ((1, 32), (2, 16)), -0.2, 0.2), 0.2, 2.0),
        "potential": gaussian(key_of[1], (NX, NY, NZ), 0.5, 3.0, ((0, 32), (1, 16)), jnp.float32),
        "permittivity": jnp.clip(jnp.exp(math.log(4.0) - 2.0794415 * jax.random.uniform(key_of[2], (NX, NY, NZ), jnp.float32) ** steps_of(key_of[2], (NX, NY, NZ), ((0, 32), (1, 16)), -0.2, 0.2)), 0.5, 4.0),
        "records": gaussian(key_of[3], (COLLOIDS, 4, S), 0.5, 3.0, ((0, 512),), jnp.float32),
        "colloid_count": draw_colloid_count(jax.random.fold_in(key_of[9], 71), 0),
        "move_slots": draw_move_slots(jax.random.fold_in(key_of[9], 71), 0),
        "move_count": draw_move_count(jax.random.fold_in(key_of[9], 71), 0),
        "own_nodes": draw_own_nodes(jax.random.fold_in(key_of[9], 71), 0),
        "arrive_nodes": draw_arrive_nodes(jax.random.fold_in(key_of[9], 71), 0),
    }


diffusion = (1.0, 0.7, 0.45)
valence = (1.0, -1.0, 2.0)
time_step = 0.05
screening = 0.05


def species_table(numbers):
    return jnp.array(numbers, dtype=jnp.float32).reshape(3, 1, 1, 1)


def face_flux(upper, lower, upper_pot, lower_pot):
    return -species_table(diffusion) * ((upper - lower) + species_table(valence) * 0.5 * (upper + lower) * (upper_pot - lower_pot))


def jacobi_global(current, permit, density):
    x_up = 0.5 * (permit + jnp.roll(permit, -1, 0))
    x_down = 0.5 * (permit + jnp.roll(permit, 1, 0))
    y_up = 0.5 * (permit + jnp.roll(permit, -1, 1))
    y_down = 0.5 * (permit + jnp.roll(permit, 1, 1))
    z_up = 0.5 * (permit + jnp.roll(permit, -1, 2))
    z_down = 0.5 * (permit + jnp.roll(permit, 1, 2))
    numer = x_up * jnp.roll(current, -1, 0) + x_down * jnp.roll(current, 1, 0) + y_up * jnp.roll(current, -1, 1) + y_down * jnp.roll(current, 1, 1) + z_up * jnp.roll(current, -1, 2) + z_down * jnp.roll(current, 1, 2) + density
    denom = x_up + x_down + y_up + y_down + z_up + z_down + screening
    return numer / denom


def reference(concentration, potential, permittivity, records, colloid_count, move_slots, move_count, own_nodes, arrive_nodes):
    grid_x = N_GX
    grid_y = N_GY
    wide_y = BY + 2
    colloid_rows = records.reshape(grid_x, grid_y, C_DEV, 4, S)
    live_counts = colloid_count.reshape(grid_x, grid_y)
    mover_slots = move_slots.reshape(grid_x, grid_y, 4, M)
    mover_counts = move_count.reshape(grid_x, grid_y, 4)
    slot_ids = jnp.arange(C_DEV, dtype=jnp.int32)
    slot_valid = jnp.arange(M, dtype=jnp.int32)[None, None, None, :] < mover_counts[..., None]
    leaving = jnp.any((mover_slots[..., None] == slot_ids) & slot_valid[..., None], axis=(2, 3))
    staying = (slot_ids < live_counts[..., None]) & jnp.logical_not(leaving)
    kept_rows = jnp.where(staying[..., None, None], colloid_rows, 0.0)
    picked_rows = jax.vmap(jax.vmap(lambda table, index: table[index]))(colloid_rows, mover_slots.reshape(grid_x, grid_y, 4 * M))
    picked_rows = picked_rows.reshape(grid_x, grid_y, 4, M, 4, S)
    sent_rows = jnp.where(slot_valid[..., None, None], picked_rows, 0.0)
    arrived_rows = jnp.stack([jnp.roll(sent_rows[:, :, 0], 1, axis=0), jnp.roll(sent_rows[:, :, 1], -1, axis=0), jnp.roll(sent_rows[:, :, 2], 1, axis=1), jnp.roll(sent_rows[:, :, 3], -1, axis=1)], axis=2)
    all_rows = jnp.concatenate([kept_rows, arrived_rows.reshape(grid_x, grid_y, 4 * M, 4, S)], axis=2)
    node_cells = jnp.concatenate([own_nodes.reshape(grid_x, grid_y, C_DEV, S), arrive_nodes.reshape(grid_x, grid_y, 4 * M, S)], axis=2)
    cell_x = node_cells // (wide_y * NZ)
    cell_y = (node_cells // NZ) % wide_y
    cell_z = node_cells % NZ
    brick_x = jnp.arange(grid_x, dtype=jnp.int32)[:, None, None, None] * BX
    brick_y = jnp.arange(grid_y, dtype=jnp.int32)[None, :, None, None] * BY
    global_x = (brick_x + cell_x - 1) % NX
    global_y = (brick_y + cell_y - 1) % NY
    flat_cells = ((global_x * NY + global_y) * NZ + cell_z).reshape(-1)
    spread_grid = jnp.zeros((4, NX * NY * NZ), jnp.float32).at[:, flat_cells].add(jnp.moveaxis(all_rows, 3, 0).reshape(4, -1))
    colloid_charge = spread_grid[0].reshape(NX, NY, NZ)
    body_force = spread_grid[1:].reshape(3, NX, NY, NZ)
    divergence = []
    for axis_index in range(3):
        flux = face_flux(jnp.roll(concentration, -1, axis_index + 1), concentration, jnp.roll(potential, -1, axis_index), potential)
        divergence.append(flux - jnp.roll(flux, 1, axis_index + 1))
    concentration_next = concentration - time_step * ((divergence[0] + divergence[1]) + divergence[2])
    charge_density = jnp.sum(species_table(valence) * concentration_next, axis=0) + colloid_charge
    current = potential
    for sweep_index in range(SWEEPS):
        current = jacobi_global(current, permittivity, charge_density)
    return concentration_next, current, body_force
```

```python
import jax
import jax.numpy as jnp
from jax import lax
from jax.experimental import pallas as pl
from jax.experimental.pallas import tpu as pltpu
from jax.sharding import PartitionSpec as P

SWEEPS = 8
DIFFUSION = (1.0, 0.7, 0.45)
VALENCE = (1.0, -1.0, 2.0)
TIME_STEP = 0.05
SCREENING = 0.05

F32 = jnp.float32
BF16 = jnp.bfloat16
BX, BY, NZ = 16, 16, 128
SLOTS, MOVERS, CHANNELS, NODES = 128, 16, 4, 128
W = 8
EXT = BX + 2 * W
WIDE = BX + 2
PAIRS = WIDE * WIDE // 2
ROWS = PAIRS * 2 * CHANNELS
GROUP = 8
KEPT = SLOTS - 4 * 8

T_REC, T_CONC, T_POT, T_EPS, T_A = 0, 8, 14, 30, 46
T_DY, T_FY, T_BY = 0, 18, 25
T_DX, T_FX, T_CX, T_BX = 0, 32, 38, 70

VMEM = pl.BlockSpec(memory_space=pltpu.VMEM)
SMEM = pl.BlockSpec(memory_space=pltpu.SMEM)


def parity(axis):
    return lax.rem(lax.axis_index(axis), 2)


def swap(block, axis, odd):
    count = lax.axis_size(axis)
    route = [(i, (((i - odd) % count ^ 1) + odd) % count) for i in range(count)]
    return lax.ppermute(block, axis, route)


def pack_kernel(conc, pot, eps, rec, slots, counts, *outs):
    for axis, odd, out in (("gx", 0, outs[0]), ("gx", 1, outs[1]), ("gy", 0, outs[2]), ("gy", 1, outs[3])):
        p = parity(axis)
        up = 1 - p if odd == 0 else p
        way = (1 if axis == "gx" else 3) - up
        number = counts[0, way]
        for k in range(MOVERS):
            row = rec[slots[0, way, k]]
            out[T_REC + k // 2, (k % 2) * 4 : (k % 2) * 4 + 4] = jnp.where(k < number, row, 0.0)
        if axis == "gx":
            out[T_CONC:T_POT] = conc[:, up * (BX - 1)].reshape(6, 8, NZ)
            out[T_POT:T_EPS] = pot[pl.ds(up * W, W)].reshape(16, 8, NZ)
            out[T_EPS:T_A] = eps[pl.ds(up * W, W)].reshape(16, 8, NZ)
        else:
            for s in range(3):
                face = jnp.where(up == 1, conc[s, :, BY - 1], conc[s, :, 0])
                out[T_CONC + 2 * s : T_CONC + 2 * s + 2] = face.reshape(2, 8, NZ)
            start = pl.multiple_of(up * W, W)
            out[T_POT:T_EPS] = pot[:, pl.ds(start, W)]
            out[T_EPS:T_A] = eps[:, pl.ds(start, W)]


def hot_group(rows_of, a_s, b_s):
    sub = lax.broadcasted_iota(jnp.int32, (16, NODES), 0)
    second = (sub >= 8).astype(F32)
    subf = sub.astype(F32)
    for g in range(GROUP):
        cell, value = rows_of(g)
        half = (cell >= PAIRS * NZ).astype(jnp.int32)
        high = ((cell - half * (PAIRS * NZ)) >> 7).astype(F32)
        low = ((cell & (NZ - 1)) + half * NZ).astype(F32)
        high = (jnp.broadcast_to(high, (16, NODES)) - second).astype(BF16)
        low = (jnp.broadcast_to(low, (16, NODES)) - subf).astype(BF16)
        lead = value.astype(BF16).astype(F32)
        rest = value - lead
        parts = jnp.concatenate([lead, rest, lead, rest], axis=0).astype(BF16)
        lanes = slice(g * NODES, (g + 1) * NODES)
        for m in range(ROWS // 16):
            a_s[m * 16 : (m + 1) * 16, lanes] = jnp.where(high == BF16(2 * m), parts, BF16(0))
        for m in range(16):
            b_s[m * 16 : (m + 1) * 16, lanes] = jnp.where(low == BF16(16 * m), BF16(1), BF16(0))
    sums = lax.dot_general(a_s[...], b_s[...], (((1,), (1,)), ((), ())), preferred_element_type=F32)
    return sums[:, :NZ], sums[:, NZ:]


def kept_kernel(rec, nodes, count, slots, counts, acc, a_s, b_s, gone, order):
    def clear(c, _):
        gone[c] = 0
        return 0

    lax.fori_loop(0, SLOTS, clear, 0, unroll=8)
    for way in range(4):
        number = counts[0, way]

        def mark(k, _, way=way):
            gone[slots[0, way, k]] = 1
            return 0

        lax.fori_loop(0, number, mark, 0)
    live = count[0]

    def gather(c, found):
        order[found] = c
        stays = jnp.logical_and(c < live, gone[c] == 0)
        return found + stays.astype(jnp.int32)

    found = lax.fori_loop(0, SLOTS, gather, 0, unroll=8)
    acc[...] = jnp.zeros_like(acc)

    def group(c, _):
        def rows_of(g):
            at = c * GROUP + g
            inside = at < found
            slot = jnp.where(inside, order[at], 0)
            return nodes[pl.ds(slot, 1), :], jnp.where(inside, rec[slot], 0.0)

        left, right = hot_group(rows_of, a_s, b_s)
        acc[0] += left
        acc[1] += right
        return 0

    lax.fori_loop(0, (found + GROUP - 1) // GROUP, group, 0)


def face_flux(s, upper, lower, step):
    return -DIFFUSION[s] * ((upper - lower) + (VALENCE[s] * 0.5) * (upper + lower) * step)


def arrive_kernel(acc_in, x0, x1, y0, y1, nodes, conc, pot, conc_next, dens, force, s0, s1, acc, a_s, b_s, rec, cells, wide):
    px, py = parity("gx"), parity("gy")
    for b, (buf, way) in enumerate(((x0, 1 - px), (x1, px), (y0, 3 - py), (y1, 2 + py))):
        for t in range(8):
            rec[b * 16 + 2 * t] = buf[T_REC + t, 0:4]
            rec[b * 16 + 2 * t + 1] = buf[T_REC + t, 4:8]
        cells[b * 16 : (b + 1) * 16] = nodes[0, way]

    def rows_at(c):
        def rows_of(g):
            at = c * GROUP + g
            return cells[pl.ds(at, 1), :], rec[at]

        return rows_of

    left, right = hot_group(rows_at(0), a_s, b_s)
    acc[0] = acc_in[0] + left
    acc[1] = acc_in[1] + right

    def group(c, _):
        left, right = hot_group(rows_at(c), a_s, b_s)
        acc[0] += left
        acc[1] += right
        return 0

    lax.fori_loop(1, 4 * MOVERS // GROUP, group, 0)

    x_low_first, y_low_first = px == 1, py == 1
    for f in range(4):
        first, last = (T_CONC + 2 * f, T_CONC + 2 * f + 2) if f < 3 else (T_POT, T_POT + 2)
        own = conc[f] if f < 3 else pot[...]
        wide[f, 1 : BX + 1, 8 : 8 + BY] = own
        if f < 3:
            xa, xb = x0[first:last], x1[first:last]
            wide[f, 0, 8 : 8 + BY] = jnp.where(x_low_first, xa, xb).reshape(BY, NZ)
            wide[f, BX + 1, 8 : 8 + BY] = jnp.where(x_low_first, xb, xa).reshape(BY, NZ)
            ya, yb = y0[first:last].reshape(BX, NZ), y1[first:last].reshape(BX, NZ)
            y_low, y_high = jnp.where(y_low_first, ya, yb), jnp.where(y_low_first, yb, ya)
        else:
            lows = jnp.where(x_low_first, x0[T_EPS - 2 : T_EPS], x1[T_EPS - 2 : T_EPS])
            highs = jnp.where(x_low_first, x1[T_POT : T_POT + 2], x0[T_POT : T_POT + 2])
            wide[f, 0, 8 : 8 + BY] = lows.reshape(BY, NZ)
            wide[f, BX + 1, 8 : 8 + BY] = highs.reshape(BY, NZ)
            y_low = jnp.where(y_low_first, y0[T_POT:T_EPS, 7], y1[T_POT:T_EPS, 7])
            y_high = jnp.where(y_low_first, y1[T_POT:T_EPS, 0], y0[T_POT:T_EPS, 0])
        wide[f, 1 : BX + 1, 7] = y_low
        wide[f, 1 : BX + 1, 8 + BY] = y_high

    dens[...] = jnp.zeros_like(dens)

    def spread(channel, ex, first, number):
        half, row = (0, ex) if ex < WIDE // 2 else (1, ex - WIDE // 2)
        base = (row * WIDE + first) * 8 + channel
        return acc[half, pl.ds(base, number, stride=8)] + acc[half, pl.ds(base + 4, number, stride=8)]

    for ex in range(WIDE):
        dens[ex, 7 : 7 + WIDE] = spread(0, ex, 0, WIDE)
        for a in range(3):
            force[a, ex] = spread(a + 1, ex, 1, BY)

    def plane(x, _):
        pc, pe, pw = wide[3, x + 1, 8:24], wide[3, x + 2, 8:24], wide[3, x, 8:24]
        pn, ps = wide[3, x + 1, 9:25], wide[3, x + 1, 7:23]
        pz = pltpu.roll(pc, NZ - 1, 1)
        dx, dw, dn, ds, dz = pe - pc, pc - pw, pn - pc, pc - ps, pz - pc
        total = dens[x + 1, 8:24]
        for s in range(3):
            c = wide[s, x + 1, 8:24]
            flux_x = face_flux(s, wide[s, x + 2, 8:24], c, dx)
            flux_w = face_flux(s, c, wide[s, x, 8:24], dw)
            flux_n = face_flux(s, wide[s, x + 1, 9:25], c, dn)
            flux_s = face_flux(s, c, wide[s, x + 1, 7:23], ds)
            flux_z = face_flux(s, pltpu.roll(c, NZ - 1, 1), c, dz)
            div = ((flux_x - flux_w) + (flux_n - flux_s)) + (flux_z - pltpu.roll(flux_z, 1, 1))
            later = c - TIME_STEP * div
            conc_next[s, x] = later
            total = total + VALENCE[s] * later
        dens[x + 1, 8:24] = total
        return 0

    lax.fori_loop(0, BX, plane, 0)

    for out, up in ((s0, 1 - py), (s1, py)):
        for ex in range(WIDE):
            out[T_DY + ex] = jnp.where(up == 1, dens[ex, 17:25], dens[ex, 7:15])
        for a in range(3):
            for ex in range(WIDE):
                r = a * WIDE + ex
                rim = jnp.where(up == 1, spread(a + 1, ex, WIDE - 1, 1), spread(a + 1, ex, 0, 1))
                out[T_FY + r // 8, r % 8 : r % 8 + 1] = rim
        out[T_FY + 6, 6:8] = jnp.zeros((2, NZ), F32)


def middle_kernel(dens, force, r0, r1, y0, y1, dext, fcore, s0, s1):
    px, py = parity("gx"), parity("gy")
    low_first = py == 1
    dext[...] = jnp.zeros_like(dext)
    for ex in range(WIDE):
        dext[ex + 7] = dens[ex]
        a, b = r0[T_DY + ex], r1[T_DY + ex]
        dext[ex + 7, 1:9] += jnp.where(low_first, a, b)
        dext[ex + 7, 23:31] += jnp.where(low_first, b, a)
    for c in range(3):
        for ex in range(WIDE):
            r = c * WIDE + ex
            a, b = r0[T_FY + r // 8, r % 8 : r % 8 + 1], r1[T_FY + r // 8, r % 8 : r % 8 + 1]
            fcore[c, ex] = force[c, ex]
            fcore[c, ex, 0:1] += jnp.where(low_first, a, b)
            fcore[c, ex, 15:16] += jnp.where(low_first, b, a)
    for out, up in ((s0, 1 - px), (s1, px)):
        out[T_DX:T_FX] = dext[pl.ds(7 + 10 * up, 8)].reshape(32, 8, NZ)
        out[T_FX:T_CX] = fcore[:, up * (WIDE - 1)].reshape(6, 8, NZ)
        for n, (buf, first) in enumerate(((y0, T_POT), (y1, T_POT), (y0, T_EPS), (y1, T_EPS))):
            out[T_CX + 8 * n : T_CX + 8 * n + 8] = buf[pl.ds(first + W * up, W)]


def sweep_kernel(dext, fcore, r0, r1, x0, x1, y0, y1, pot, eps, pot_next, force, phi_a, phi_b, ew, cx, cy, cz, cd, inv):
    px, py = parity("gx"), parity("gy")
    x_low_first, y_low_first = px == 1, py == 1

    force[...] = fcore[:, 1 : BX + 1]
    fa, fb = r0[T_FX:T_CX].reshape(3, BY, NZ), r1[T_FX:T_CX].reshape(3, BY, NZ)
    force[:, 0] += jnp.where(x_low_first, fa, fb)
    force[:, BX - 1] += jnp.where(x_low_first, fb, fa)

    cd[...] = dext[...]
    da, db = r0[T_DX:T_FX].reshape(8, EXT, NZ), r1[T_DX:T_FX].reshape(8, EXT, NZ)
    cd[1:9] += jnp.where(x_low_first, da, db)
    cd[23:31] += jnp.where(x_low_first, db, da)

    zero = jnp.zeros((EXT, 8, NZ), F32)
    for buf in (phi_a, phi_b, ew):
        buf[:, 0:8] = zero
        buf[:, 40:48] = zero
    for n, (buf, own, tile) in enumerate(((phi_a, pot, T_POT), (ew, eps, T_EPS))):
        buf[W : W + BX, 16:32] = own[...]
        a, b = x0[tile : tile + 16].reshape(W, BY, NZ), x1[tile : tile + 16].reshape(W, BY, NZ)
        buf[0:W, 16:32] = jnp.where(x_low_first, a, b)
        buf[W + BX : EXT, 16:32] = jnp.where(x_low_first, b, a)
        a, b = y0[tile : tile + 16], y1[tile : tile + 16]
        buf[W : W + BX, 8:16] = jnp.where(y_low_first, a, b)
        buf[W : W + BX, 32:40] = jnp.where(y_low_first, b, a)
        corner = T_CX + 16 * n
        for r, low in ((r0, x_low_first), (r1, jnp.logical_not(x_low_first))):
            a, b = r[corner : corner + 8], r[corner + 8 : corner + 16]
            first = jnp.where(low, 0, W + BX)
            buf[pl.ds(first, W), 8:16] = jnp.where(y_low_first, a, b)
            buf[pl.ds(first, W), 32:40] = jnp.where(y_low_first, b, a)

    def coefficients(x, _):
        e = ew[x, 8:40]
        up = e + ew[jnp.minimum(x + 1, EXT - 1), 8:40]
        cx[x] = up
        n = e + ew[x, 9:41]
        s = e + ew[x, 7:39]
        cy[x] = n
        z = e + pltpu.roll(e, NZ - 1, 1)
        cz[x] = z
        down = e + ew[jnp.maximum(x - 1, 0), 8:40]
        inv[x] = 1.0 / ((((up + down) + (n + s)) + (z + pltpu.roll(z, 1, 1))) + 2.0 * SCREENING)
        cd[x] = 2.0 * cd[x]
        return 0

    lax.fori_loop(0, EXT, coefficients, 0)

    for k in range(1, SWEEPS + 1):
        old, new = (phi_a, phi_b) if k % 2 == 1 else (phi_b, phi_a)
        lo, hi = (8, 40) if k < SWEEPS else (16, 32)

        def plane(x, _, old=old, new=new, lo=lo, hi=hi, k=k):
            f = slice(lo - 8, hi - 8)
            p = old[x, lo:hi]
            z = cz[x, f]
            c = cy[x, f]
            e_here = ew[x, lo:hi]
            total = cx[x, f] * old[x + 1, lo:hi] + cx[x - 1, f] * old[x - 1, lo:hi]
            total += c * old[x, lo + 1 : hi + 1] + (e_here + ew[x, lo - 1 : hi - 1]) * old[x, lo - 1 : hi - 1]
            total += z * pltpu.roll(p, NZ - 1, 1) + pltpu.roll(z * p, 1, 1)
            total = (total + cd[x, f]) * inv[x, f]
            if k < SWEEPS:
                new[x, lo:hi] = total
            else:
                pot_next[x - W] = total
            return 0

        lax.fori_loop(k, EXT - k, plane, 0, unroll=2)


def shape(*dims):
    return jax.ShapeDtypeStruct(dims, F32)


def call(kernel, name, ins, outs, scratch=(), flops=0):
    moved = 4 * sum(int(o.size) for o in outs)
    return pl.pallas_call(
        kernel,
        name=name,
        in_specs=ins,
        out_specs=[VMEM] * len(outs),
        out_shape=outs,
        scratch_shapes=scratch,
        compiler_params=pltpu.CompilerParams(vmem_limit_bytes=40 << 20),
        cost_estimate=pl.CostEstimate(flops=flops, bytes_accessed=moved, transcendentals=0),
    )


def body(conc, pot, eps, records, count, slots, counts, own_nodes, arrive_nodes):
    hot = [pltpu.VMEM((ROWS, GROUP * NODES), BF16), pltpu.VMEM((2 * NZ, GROUP * NODES), BF16)]
    sends = call(pack_kernel, "pack", [VMEM] * 4 + [SMEM] * 2, [shape(T_A, 8, NZ)] * 4)(
        conc, pot, eps, records, slots, counts
    )
    y0, y1 = swap(sends[2], "gy", 0), swap(sends[3], "gy", 1)
    x1, x0 = swap(sends[1], "gx", 1), swap(sends[0], "gx", 0)
    (acc,) = call(
        kept_kernel,
        "spread_kept",
        [VMEM] * 2 + [SMEM] * 3,
        [shape(2, ROWS, NZ)],
        hot + [pltpu.SMEM((SLOTS,), jnp.int32), pltpu.SMEM((SLOTS + GROUP,), jnp.int32)],
        flops=2 * ROWS * 2 * NZ * KEPT * NODES,
    )(records, own_nodes, count, slots, counts)
    conc_next, dens, force, b0, b1 = call(
        arrive_kernel,
        "spread_arrived",
        [VMEM] * 8,
        [shape(3, BX, BY, NZ), shape(WIDE, EXT, NZ), shape(3, WIDE, BY, NZ), shape(T_BY, 8, NZ), shape(T_BY, 8, NZ)],
        [pltpu.VMEM((2, ROWS, NZ), F32)]
        + hot
        + [
            pltpu.VMEM((4 * MOVERS, CHANNELS, NODES), F32),
            pltpu.VMEM((4 * MOVERS, NODES), jnp.int32),
            pltpu.VMEM((4, WIDE, 32, NZ), F32),
        ],
        flops=2 * ROWS * 2 * NZ * 4 * MOVERS * NODES,
    )(acc, x0, x1, y0, y1, arrive_nodes, conc, pot)
    c0, c1 = swap(b0, "gy", 0), swap(b1, "gy", 1)
    dext, fcore, e0, e1 = call(
        middle_kernel,
        "join_y",
        [VMEM] * 6,
        [shape(EXT, EXT, NZ), shape(3, WIDE, BY, NZ), shape(T_BX, 8, NZ), shape(T_BX, 8, NZ)],
    )(dens, force, c0, c1, y0, y1)
    g1, g0 = swap(e1, "gx", 1), swap(e0, "gx", 0)
    field = pltpu.VMEM((EXT, 48, NZ), F32)
    plain = pltpu.VMEM((EXT, EXT, NZ), F32)
    pot_next, body_force = call(
        sweep_kernel,
        "sweeps",
        [VMEM] * 10,
        [shape(BX, BY, NZ), shape(3, BX, BY, NZ)],
        [field, field, field, plain, plain, plain, plain, plain],
        flops=20 * SWEEPS * EXT * EXT * NZ,
    )(dext, fcore, g0, g1, x0, x1, y0, y1, pot, eps)
    return conc_next, pot_next, body_force


def solution(mesh):
    placed = (
        P(None, "gx", "gy", None),
        P("gx", "gy", None),
        P("gx", "gy", None),
        P(("gx", "gy"), None, None),
        P(("gx", "gy")),
        P(("gx", "gy"), None, None),
        P(("gx", "gy"), None),
        P(("gx", "gy"), None),
        P(("gx", "gy"), None, None, None),
    )
    return jax.shard_map(
        body,
        mesh=mesh,
        in_specs=placed,
        out_specs=(P(None, "gx", "gy", None), P("gx", "gy", None), P(None, "gx", "gy", None)),
        check_vma=False,
    )
```

```python
import jax
import jax.numpy as jnp
from jax import lax
from jax.experimental import pallas as pl
from jax.experimental.pallas import tpu as pltpu
from jax.sharding import PartitionSpec as P

SWEEPS = 8
DIFFUSION = (1.0, 0.7, 0.45)
VALENCE = (1.0, -1.0, 2.0)
TIME_STEP = 0.05
SCREENING = 0.05

F32 = jnp.float32
BF16 = jnp.bfloat16
BX, BY, NZ = 16, 16, 128
SLOTS, MOVERS, CHANNELS, NODES = 128, 16, 4, 128
W = 8
EXT = BX + 2 * W
WIDE = BX + 2
PAIRS = WIDE * WIDE // 2
ROWS = PAIRS * 2 * CHANNELS
GROUP = 8
LATER = 24

Y_CONC, Y_POT, Y_EPS, Y_END = 8, 14, 30, 46
X_CONC, X_POT, X_EPS, X_END = 8, 14, 46, 78
DY_FORCE, DY_END = WIDE * W, WIDE * W + 56
DX_FORCE, DX_END = 32, 38

VMEM = pl.BlockSpec(memory_space=pltpu.VMEM)
SMEM = pl.BlockSpec(memory_space=pltpu.SMEM)
HBM = pl.BlockSpec(memory_space=pltpu.HBM)


def parity(axis):
    return lax.rem(lax.axis_index(axis), 2)


def swap(block, axis, odd):
    count = lax.axis_size(axis)
    route = [(i, (((i - odd) % count ^ 1) + odd) % count) for i in range(count)]
    return lax.ppermute(block, axis, route)


def hot_group(rows_of, a_s, b_s):
    sub = lax.broadcasted_iota(jnp.int32, (16, NODES), 0)
    second = (sub >= 8).astype(F32)
    subf = sub.astype(F32)
    for g in range(GROUP):
        cell, value = rows_of(g)
        half = (cell >= PAIRS * NZ).astype(jnp.int32)
        high = ((cell - half * (PAIRS * NZ)) >> 7).astype(F32)
        low = ((cell & (NZ - 1)) + half * NZ).astype(F32)
        high = (jnp.broadcast_to(high, (16, NODES)) - second).astype(BF16)
        low = (jnp.broadcast_to(low, (16, NODES)) - subf).astype(BF16)
        lead = value.astype(BF16).astype(F32)
        rest = value - lead
        parts = jnp.concatenate([lead, rest, lead, rest], axis=0).astype(BF16)
        lanes = slice(g * NODES, (g + 1) * NODES)
        for m in range(ROWS // 16):
            a_s[m * 16 : (m + 1) * 16, lanes] = jnp.where(high == BF16(2 * m), parts, BF16(0))
        for m in range(16):
            b_s[m * 16 : (m + 1) * 16, lanes] = jnp.where(low == BF16(16 * m), BF16(1), BF16(0))
    sums = lax.dot_general(a_s[...], b_s[...], (((1,), (1,)), ((), ())), preferred_element_type=F32)
    return sums[:, :NZ], sums[:, NZ:]


def spread_groups(groups, rows_of, acc_in, acc, a_s, b_s):
    left, right = hot_group(lambda g: rows_of(g), a_s, b_s)
    acc[0] = acc_in[0] + left
    acc[1] = acc_in[1] + right

    def group(c, _):
        left, right = hot_group(lambda g: rows_of(c * GROUP + g), a_s, b_s)
        acc[0] += left
        acc[1] += right
        return 0

    lax.fori_loop(1, groups, group, 0)


def first_kernel(
    conc_h, pot_h, eps_h, rec_h, nodes_h, count_h, slots_h, counts_h,
    conc, pot, eps, y0, y1, xr, kept_rec, kept_nodes, acc,
    rec, nodes, count, slots, counts, gone, order, a_s, b_s, sems,
):
    pairs = ((slots_h, slots), (counts_h, counts), (count_h, count), (rec_h, rec), (pot_h, pot), (eps_h, eps), (conc_h, conc), (nodes_h, nodes))
    copies = [pltpu.make_async_copy(a, b, sems.at[n]) for n, (a, b) in enumerate(pairs)]
    for copy in copies:
        copy.start()
    acc[...] = jnp.zeros_like(acc)

    def clear(c, _):
        gone[c] = 0
        return 0

    lax.fori_loop(0, SLOTS, clear, 0, unroll=16)
    for copy in copies[:3]:
        copy.wait()
    for way in range(4):

        def mark(k, _, way=way):
            gone[slots[0, way, k]] = 1
            return 0

        lax.fori_loop(0, counts[0, way], mark, 0)
    live = count[0]

    def gather(c, found):
        order[found] = c
        stays = jnp.logical_and(c < live, gone[c] == 0)
        return found + stays.astype(jnp.int32)

    found = lax.fori_loop(0, SLOTS, gather, 0, unroll=16)
    for copy in copies[3:]:
        copy.wait()

    for n, (axis, odd) in enumerate((("gy", 0), ("gy", 1), ("gx", 0), ("gx", 1))):
        p = parity(axis)
        up = 1 - p if odd == 0 else p
        way = (1 if axis == "gx" else 3) - up
        number = counts[0, way]
        out = (y0, y1, xr.at[0], xr.at[1])[n]
        for k in range(MOVERS):
            row = rec[slots[0, way, k]]
            out[k // 2, (k % 2) * 4 : (k % 2) * 4 + 4] = jnp.where(k < number, row, 0.0)
        if axis == "gx":
            out[X_CONC:X_POT] = conc[:, up * (BX - 1)].reshape(6, 8, NZ)
        else:
            for s in range(3):
                face = jnp.where(up == 1, conc[s, :, BY - 1], conc[s, :, 0])
                out[Y_CONC + 2 * s : Y_CONC + 2 * s + 2] = face.reshape(2, 8, NZ)
            start = pl.multiple_of(up * W, W)
            out[Y_POT:Y_EPS] = pot[:, pl.ds(start, W)]
            out[Y_EPS:Y_END] = eps[:, pl.ds(start, W)]

    def kept_row(at):
        inside = at < found
        slot = jnp.where(inside, order[at], 0)
        return nodes[pl.ds(slot, 1), :], jnp.where(inside, rec[slot], 0.0)

    for r in range(LATER):
        cell, value = kept_row(r)
        kept_nodes[r : r + 1] = cell
        kept_rec[r] = value

    def group(c, _):
        left, right = hot_group(lambda g: kept_row(c * GROUP + g), a_s, b_s)
        acc[0] += left
        acc[1] += right
        return 0

    lax.fori_loop(LATER // GROUP, (found + GROUP - 1) // GROUP, group, 0)


def kept_kernel(acc_in, rec, nodes, acc, a_s, b_s):
    spread_groups(LATER // GROUP, lambda r: (nodes[pl.ds(r, 1), :], rec[r]), acc_in, acc, a_s, b_s)


def pack_x_kernel(xr, pot, eps, y0, y1, s0, s1):
    px, py = parity("gx"), parity("gy")
    for n, (out, up) in enumerate(((s0, 1 - px), (s1, px))):
        out[0:X_POT] = xr[n]
        for first, own, tile in ((X_POT, pot, Y_POT), (X_EPS, eps, Y_EPS)):
            own = own[pl.ds(up * W, W)]
            a, b = y0[pl.ds(tile + up * W, W)], y1[pl.ds(tile + up * W, W)]
            low, high = jnp.where(py == 1, a, b), jnp.where(py == 1, b, a)
            for x in range(W):
                out[first + 4 * x] = low[x]
                out[first + 4 * x + 1] = own[x, 0:8]
                out[first + 4 * x + 2] = own[x, 8:16]
                out[first + 4 * x + 3] = high[x]


def collect(buf0, buf1, way0, way1, nodes, rec, cells):
    for b, (buf, way) in enumerate(((buf0, way0), (buf1, way1))):
        for t in range(8):
            rec[b * 16 + 2 * t] = buf[t, 0:4]
            rec[b * 16 + 2 * t + 1] = buf[t, 4:8]
        cells[b * 16 : (b + 1) * 16] = nodes[0, way]


def arrive_y_kernel(acc_in, y0, y1, nodes, acc, a_s, b_s, rec, cells):
    py = parity("gy")
    collect(y0, y1, 3 - py, 2 + py, nodes, rec, cells)
    spread_groups(2 * MOVERS // GROUP, lambda r: (cells[pl.ds(r, 1), :], rec[r]), acc_in, acc, a_s, b_s)


def face_flux(s, upper, lower, step):
    return -DIFFUSION[s] * ((upper - lower) + (VALENCE[s] * 0.5) * (upper + lower) * step)


def spread_rows(acc, channel, ex, first, number):
    half, row = divmod(ex, WIDE // 2)
    base = (row * WIDE + first) * 8 + channel
    return acc[half, pl.ds(base, number, stride=8)] + acc[half, pl.ds(base + 4, number, stride=8)]


def arrive_x_kernel(acc_in, x0, x1, y0, y1, nodes, conc, pot, conc_next, acc, dens, s0, s1, a_s, b_s, rec, cells, wide):
    px, py = parity("gx"), parity("gy")
    x_low_first, y_low_first = px == 1, py == 1
    collect(x0, x1, 1 - px, px, nodes, rec, cells)
    spread_groups(2 * MOVERS // GROUP, lambda r: (cells[pl.ds(r, 1), :], rec[r]), acc_in, acc, a_s, b_s)

    for f in range(4):
        wide[f, 1 : BX + 1, 8 : 8 + BY] = conc[f] if f < 3 else pot[...]
        if f < 3:
            xa, xb = (x[X_CONC + 2 * f : X_CONC + 2 * f + 2].reshape(BY, NZ) for x in (x0, x1))
            x_low, x_high = jnp.where(x_low_first, xa, xb), jnp.where(x_low_first, xb, xa)
            ya, yb = (y[Y_CONC + 2 * f : Y_CONC + 2 * f + 2].reshape(BX, NZ) for y in (y0, y1))
            y_low, y_high = jnp.where(y_low_first, ya, yb), jnp.where(y_low_first, yb, ya)
        else:
            last, first = X_POT + 4 * (W - 1) + 1, X_POT + 1
            x_low = jnp.where(x_low_first, x0[last : last + 2], x1[last : last + 2]).reshape(BY, NZ)
            x_high = jnp.where(x_low_first, x1[first : first + 2], x0[first : first + 2]).reshape(BY, NZ)
            y_low = jnp.where(y_low_first, y0[Y_POT:Y_EPS, 7], y1[Y_POT:Y_EPS, 7])
            y_high = jnp.where(y_low_first, y1[Y_POT:Y_EPS, 0], y0[Y_POT:Y_EPS, 0])
        wide[f, 0, 8 : 8 + BY] = x_low
        wide[f, BX + 1, 8 : 8 + BY] = x_high
        wide[f, 1 : BX + 1, 7] = y_low
        wide[f, 1 : BX + 1, 8 + BY] = y_high

    dens[...] = jnp.zeros_like(dens)
    for ex in range(WIDE):
        dens[ex, 7 : 7 + WIDE] = spread_rows(acc, 0, ex, 0, WIDE)

    for x in range(BX):
        pc, pe, pw = wide[3, x + 1, 8:24], wide[3, x + 2, 8:24], wide[3, x, 8:24]
        pn, ps = wide[3, x + 1, 9:25], wide[3, x + 1, 7:23]
        pz = pltpu.roll(pc, NZ - 1, 1)
        dx, dw, dn, ds, dz = pe - pc, pc - pw, pn - pc, pc - ps, pz - pc
        total = dens[x + 1, 8:24]
        for s in range(3):
            c = wide[s, x + 1, 8:24]
            flux_x = face_flux(s, wide[s, x + 2, 8:24], c, dx)
            flux_w = face_flux(s, c, wide[s, x, 8:24], dw)
            flux_n = face_flux(s, wide[s, x + 1, 9:25], c, dn)
            flux_s = face_flux(s, c, wide[s, x + 1, 7:23], ds)
            flux_z = face_flux(s, pltpu.roll(c, NZ - 1, 1), c, dz)
            div = ((flux_x - flux_w) + (flux_n - flux_s)) + (flux_z - pltpu.roll(flux_z, 1, 1))
            later = c - TIME_STEP * div
            conc_next[s, x] = later
            total = total + VALENCE[s] * later
        dens[x + 1, 8:24] = total

    for out, up in ((s0, 1 - py), (s1, py)):
        for ex in range(WIDE):
            out[ex * 8 : ex * 8 + 8] = jnp.where(up == 1, dens[ex, 17:25], dens[ex, 7:15])
        for a in range(3):
            for half in range(2):
                rims = []
                for ey in (0, WIDE - 1):
                    base = ey * 8 + a + 1
                    lead = acc[half, pl.ds(base, WIDE // 2, stride=WIDE * 8)]
                    rims.append(lead + acc[half, pl.ds(base + 4, WIDE // 2, stride=WIDE * 8)])
                r = DY_FORCE + a * WIDE + half * (WIDE // 2)
                out[r : r + WIDE // 2] = jnp.where(up == 1, rims[1], rims[0])
        out[DY_FORCE + 54 : DY_END] = jnp.zeros((2, NZ), F32)


def coefficient_kernel(acc, x0, x1, y0, y1, pot, eps, force, phi, xp, xm, yp, ym, zp, zm, inv, ew):
    px, py = parity("gx"), parity("gy")
    x_low_first, y_low_first = px == 1, py == 1
    for c in range(3):
        for ex in range(WIDE):
            force[c, ex] = spread_rows(acc, c + 1, ex, 1, BY)
    for buf, own, x_tile, y_tile in ((phi, pot, X_POT, Y_POT), (ew, eps, X_EPS, Y_EPS)):
        buf[W : W + BX, W : W + BY] = own[...]
        a, b = y0[y_tile : y_tile + BX], y1[y_tile : y_tile + BX]
        buf[W : W + BX, 0:W] = jnp.where(y_low_first, a, b)
        buf[W : W + BX, W + BY : EXT] = jnp.where(y_low_first, b, a)
        a, b = (x[x_tile : x_tile + 4 * W].reshape(W, EXT, NZ) for x in (x0, x1))
        buf[0:W] = jnp.where(x_low_first, a, b)
        buf[W + BX : EXT] = jnp.where(x_low_first, b, a)
    for x in range(1, EXT - 1):
        e = ew[x]
        up, down = e + ew[x + 1], e + ew[x - 1]
        north, south = e + pltpu.roll(e, EXT - 1, 0), e + pltpu.roll(e, 1, 0)
        over = e + pltpu.roll(e, NZ - 1, 1)
        under = pltpu.roll(over, 1, 1)
        scale = 1.0 / ((((up + down) + (north + south)) + (over + under)) + 2.0 * SCREENING)
        xp[x], xm[x] = up * scale, down * scale
        yp[x], ym[x] = north * scale, south * scale
        zp[x], zm[x] = over * scale, under * scale
        inv[x] = 2.0 * scale
    for buf in (xp, xm, yp, ym, zp, zm, inv):
        buf[0] = jnp.zeros((EXT, NZ), F32)
        buf[EXT - 1] = jnp.zeros((EXT, NZ), F32)


def join_y_kernel(dens, force, r0, r1, dext, fcore, s0, s1):
    px, py = parity("gx"), parity("gy")
    low_first = py == 1
    dext[0:7] = jnp.zeros((7, EXT, NZ), F32)
    dext[25:32] = jnp.zeros((7, EXT, NZ), F32)
    for ex in range(WIDE):
        dext[ex + 7] = dens[ex]
        a, b = r0[ex * 8 : ex * 8 + 8], r1[ex * 8 : ex * 8 + 8]
        dext[ex + 7, 1:9] += jnp.where(low_first, a, b)
        dext[ex + 7, 23:31] += jnp.where(low_first, b, a)
    fcore[...] = force[...]
    for c in range(3):
        r = DY_FORCE + c * WIDE
        a, b = r0[r : r + WIDE], r1[r : r + WIDE]
        fcore[c, :, 0] += jnp.where(low_first, a, b)
        fcore[c, :, BY - 1] += jnp.where(low_first, b, a)
    for out, up in ((s0, 1 - px), (s1, px)):
        out[0:DX_FORCE] = dext[pl.ds(7 + 10 * up, 8)].reshape(32, 8, NZ)
        out[DX_FORCE:DX_END] = fcore[:, up * (WIDE - 1)].reshape(6, 8, NZ)


def sweep_kernel(dext, fcore, r0, r1, phi, xp, xm, yp, ym, zp, zm, inv, pot_next, force, phi_a, phi_b, rhs):
    low_first = parity("gx") == 1
    force[...] = fcore[:, 1 : BX + 1]
    a, b = (r[DX_FORCE:DX_END].reshape(3, BY, NZ) for r in (r0, r1))
    force[:, 0] += jnp.where(low_first, a, b)
    force[:, BX - 1] += jnp.where(low_first, b, a)

    for x in range(1, EXT - 1):
        total = dext[x]
        if x < 9 or x > 22:
            t = 4 * (x - 1 if x < 9 else x - 23)
            a, b = (r[t : t + 4].reshape(EXT, NZ) for r in (r0, r1))
            total = total + (jnp.where(low_first, a, b) if x < 9 else jnp.where(low_first, b, a))
        rhs[x] = total * inv[x]

    for k in range(1, SWEEPS + 1):
        old = phi if k == 1 else (phi_a, phi_b)[k % 2]
        new = (phi_a, phi_b)[(k + 1) % 2]
        for x in range(k, EXT - k):
            if k < SWEEPS:
                f = slice(0, EXT)
                here = old[x]
                north, south = pltpu.roll(here, EXT - 1, 0), pltpu.roll(here, 1, 0)
            else:
                f = slice(W, W + BY)
                here = old[x, f]
                north, south = old[x, W + 1 : W + BY + 1], old[x, W - 1 : W + BY - 1]
            total = (xp[x, f] * old[x + 1, f] + xm[x, f] * old[x - 1, f]) + (yp[x, f] * north + ym[x, f] * south)
            total += (zp[x, f] * pltpu.roll(here, NZ - 1, 1) + zm[x, f] * pltpu.roll(here, 1, 1)) + rhs[x, f]
            if k < SWEEPS:
                new[x] = total
            else:
                pot_next[x - W] = total


def shape(*dims):
    return jax.ShapeDtypeStruct(dims, F32)


def call(kernel, name, ins, outs, scratch=(), flops=0):
    moved = 4 * sum(int(o.size) for o in outs)
    return pl.pallas_call(
        kernel,
        name=name,
        in_specs=ins,
        out_specs=[VMEM] * len(outs),
        out_shape=outs,
        scratch_shapes=scratch,
        compiler_params=pltpu.CompilerParams(vmem_limit_bytes=32 << 20),
        cost_estimate=pl.CostEstimate(flops=flops, bytes_accessed=moved, transcendentals=0),
    )


def body(conc, pot, eps, records, count, slots, counts, own_nodes, arrive_nodes):
    hot = [pltpu.VMEM((ROWS, GROUP * NODES), BF16), pltpu.VMEM((2 * NZ, GROUP * NODES), BF16)]
    some = [pltpu.VMEM((2 * MOVERS, CHANNELS, NODES), F32), pltpu.VMEM((2 * MOVERS, NODES), jnp.int32)]
    sums = shape(2, ROWS, NZ)
    row_flops = 2 * ROWS * 2 * NZ * NODES
    field = shape(EXT, EXT, NZ)
    core = shape(BX, BY, NZ)

    conc_v, pot_v, eps_v, a0, a1, xr, kept_rec, kept_nodes, acc = call(
        first_kernel,
        "first",
        [HBM] * 8,
        [
            shape(3, BX, BY, NZ), core, core, shape(Y_END, 8, NZ), shape(Y_END, 8, NZ), shape(2, X_POT, 8, NZ),
            shape(LATER, CHANNELS, NODES), jax.ShapeDtypeStruct((LATER, NODES), jnp.int32), sums,
        ],
        [
            pltpu.VMEM((SLOTS, CHANNELS, NODES), F32), pltpu.VMEM((SLOTS, NODES), jnp.int32), pltpu.SMEM((1,), jnp.int32),
            pltpu.SMEM((1, 4, MOVERS), jnp.int32), pltpu.SMEM((1, 4), jnp.int32), pltpu.SMEM((SLOTS,), jnp.int32),
            pltpu.SMEM((SLOTS + GROUP,), jnp.int32), *hot, pltpu.SemaphoreType.DMA((8,)),
        ],
        flops=row_flops * 32,
    )(conc, pot, eps, records, own_nodes, count, slots, counts)
    y0, y1 = swap(a0, "gy", 0), swap(a1, "gy", 1)
    (acc,) = call(kept_kernel, "spread_kept", [VMEM] * 3, [sums], hot, flops=row_flops * LATER)(acc, kept_rec, kept_nodes)
    b0, b1 = call(pack_x_kernel, "pack_x", [VMEM] * 5, [shape(X_END, 8, NZ)] * 2)(xr, pot_v, eps_v, y0, y1)
    x1, x0 = swap(b1, "gx", 1), swap(b0, "gx", 0)
    (acc,) = call(arrive_y_kernel, "spread_y", [VMEM] * 4, [sums], hot + some, flops=row_flops * 2 * MOVERS)(
        acc, y0, y1, arrive_nodes
    )
    conc_next, acc, dens, c0, c1 = call(
        arrive_x_kernel,
        "spread_x",
        [VMEM] * 8,
        [shape(3, BX, BY, NZ), sums, shape(WIDE, EXT, NZ), shape(DY_END, NZ), shape(DY_END, NZ)],
        hot + some + [pltpu.VMEM((4, WIDE, 32, NZ), F32)],
        flops=row_flops * 2 * MOVERS,
    )(acc, x0, x1, y0, y1, arrive_nodes, conc_v, pot_v)
    r0, r1 = swap(c0, "gy", 0), swap(c1, "gy", 1)
    force, phi, *weights = call(
        coefficient_kernel,
        "coefficients",
        [VMEM] * 7,
        [shape(3, WIDE, BY, NZ)] + [field] * 8,
        [pltpu.VMEM((EXT, EXT, NZ), F32)],
        flops=row_flops * 8,
    )(acc, x0, x1, y0, y1, pot_v, eps_v)
    dext, fcore, e0, e1 = call(
        join_y_kernel, "join_y", [VMEM] * 4, [field, shape(3, WIDE, BY, NZ), shape(DX_END, 8, NZ), shape(DX_END, 8, NZ)]
    )(dens, force, r0, r1)
    g1, g0 = swap(e1, "gx", 1), swap(e0, "gx", 0)
    pot_next, body_force = call(
        sweep_kernel,
        "sweeps",
        [VMEM] * 12,
        [core, shape(3, BX, BY, NZ)],
        [pltpu.VMEM((EXT, EXT, NZ), F32)] * 3,
        flops=20 * SWEEPS * EXT * EXT * NZ,
    )(dext, fcore, g0, g1, phi, *weights)
    return conc_next, pot_next, body_force


def solution(mesh):
    placed = (
        P(None, "gx", "gy", None),
        P("gx", "gy", None),
        P("gx", "gy", None),
        P(("gx", "gy"), None, None),
        P(("gx", "gy")),
        P(("gx", "gy"), None, None),
        P(("gx", "gy"), None),
        P(("gx", "gy"), None),
        P(("gx", "gy"), None, None, None),
    )
    return jax.shard_map(
        body,
        mesh=mesh,
        in_specs=placed,
        out_specs=(P(None, "gx", "gy", None), P("gx", "gy", None), P(None, "gx", "gy", None)),
        check_vma=False,
    )
```

```python
import jax
import jax.numpy as jnp
from jax import lax
from jax.experimental import pallas as pl
from jax.experimental.pallas import tpu as pltpu
from jax.sharding import PartitionSpec as P

SWEEPS = 8
DIFFUSION = (1.0, 0.7, 0.45)
VALENCE = (1.0, -1.0, 2.0)
TIME_STEP = 0.05
SCREENING = 0.05

F32 = jnp.float32
BF16 = jnp.bfloat16
BX, BY, NZ = 16, 16, 128
SLOTS, MOVERS, CHANNELS, NODES = 128, 16, 4, 128
W = 8
EXT = BX + 2 * W
WIDE = BX + 2
PAIRS = WIDE * WIDE // 2
ROWS = PAIRS * 2 * CHANNELS
GROUP = 8

Y_CONC, Y_POT, Y_EPS, Y_END = 8, 14, 30, 46
X_CONC, X_POT, X_EPS, X_END = 8, 14, 46, 78
DY_FORCE, DY_END = WIDE * W, WIDE * W + 56
DX_FORCE, DX_END = 32, 38

VMEM = pl.BlockSpec(memory_space=pltpu.VMEM)
SMEM = pl.BlockSpec(memory_space=pltpu.SMEM)
HBM = pl.BlockSpec(memory_space=pltpu.HBM)


def parity(axis):
    return lax.rem(lax.axis_index(axis), 2)


def swap(block, axis, odd):
    count = lax.axis_size(axis)
    route = [(i, (((i - odd) % count ^ 1) + odd) % count) for i in range(count)]
    return lax.ppermute(block, axis, route)


def hot_group(rows_of, a_s, b_s):
    sub = lax.broadcasted_iota(jnp.int32, (16, NODES), 0)
    second = (sub >= 8).astype(F32)
    subf = sub.astype(F32)
    for g in range(GROUP):
        cell, value = rows_of(g)
        half = (cell >= PAIRS * NZ).astype(jnp.int32)
        high = ((cell - half * (PAIRS * NZ)) >> 7).astype(F32)
        low = ((cell & (NZ - 1)) + half * NZ).astype(F32)
        high = (jnp.broadcast_to(high, (16, NODES)) - second).astype(BF16)
        low = (jnp.broadcast_to(low, (16, NODES)) - subf).astype(BF16)
        lead = value.astype(BF16).astype(F32)
        rest = value - lead
        parts = jnp.concatenate([lead, rest, lead, rest], axis=0).astype(BF16)
        lanes = slice(g * NODES, (g + 1) * NODES)
        for m in range(ROWS // 16):
            a_s[m * 16 : (m + 1) * 16, lanes] = jnp.where(high == BF16(2 * m), parts, BF16(0))
        for m in range(16):
            b_s[m * 16 : (m + 1) * 16, lanes] = jnp.where(low == BF16(16 * m), BF16(1), BF16(0))
    sums = lax.dot_general(a_s[...], b_s[...], (((1,), (1,)), ((), ())), preferred_element_type=F32)
    return sums[:, :NZ], sums[:, NZ:]


def spread_groups(groups, rows_of, acc_in, acc, a_s, b_s):
    left, right = hot_group(lambda g: rows_of(g), a_s, b_s)
    acc[0] = acc_in[0] + left
    acc[1] = acc_in[1] + right

    def group(c, _):
        left, right = hot_group(lambda g: rows_of(c * GROUP + g), a_s, b_s)
        acc[0] += left
        acc[1] += right
        return 0

    lax.fori_loop(1, groups, group, 0)


def way_of(axis, odd):
    p = parity(axis)
    up = 1 - p if odd == 0 else p
    return up, (1 if axis == "gx" else 3) - up


def pack_records(out, rec, slots, number, way):
    for k in range(MOVERS):
        row = rec[slots[0, way, k]]
        out[k // 2, (k % 2) * 4 : (k % 2) * 4 + 4] = jnp.where(k < number, row, 0.0)


def first_kernel(conc_h, pot_h, eps_h, rec_h, slots_h, counts_h, s0, s1, conc, rec, slots, counts, sems):
    copies = [(slots_h, slots), (counts_h, counts), (rec_h, rec), (conc_h, conc)]
    for odd, out in enumerate((s0, s1)):
        start = pl.multiple_of(way_of("gy", odd)[0] * W, W)
        copies.append((pot_h.at[:, pl.ds(start, W)], out.at[pl.ds(Y_POT, BX)]))
        copies.append((eps_h.at[:, pl.ds(start, W)], out.at[pl.ds(Y_EPS, BX)]))
    copies = [pltpu.make_async_copy(a, b, sems.at[n]) for n, (a, b) in enumerate(copies)]
    for copy in copies:
        copy.start()
    for copy in copies:
        copy.wait()
    for odd, out in enumerate((s0, s1)):
        up, way = way_of("gy", odd)
        pack_records(out, rec, slots, counts[0, way], way)
        for s in range(3):
            face = jnp.where(up == 1, conc[s, :, BY - 1], conc[s, :, 0])
            out[Y_CONC + 2 * s : Y_CONC + 2 * s + 2] = face.reshape(2, 8, NZ)


def kept_kernel(
    conc_h, pot_h, eps_h, rec_h, nodes_h, arrive_h, slots_h, counts_h, count,
    conc, pot, eps, arrive, xr, acc,
    rec, nodes, slots, counts, gone, order, a_s, b_s, sems,
):
    pairs = (
        (slots_h, slots), (counts_h, counts), (rec_h, rec), (nodes_h, nodes),
        (conc_h, conc), (pot_h, pot), (eps_h, eps), (arrive_h, arrive),
    )
    copies = [pltpu.make_async_copy(a, b, sems.at[n]) for n, (a, b) in enumerate(pairs)]
    for copy in copies:
        copy.start()
    acc[...] = jnp.zeros_like(acc)

    def clear(c, _):
        gone[c] = 0
        return 0

    lax.fori_loop(0, SLOTS, clear, 0, unroll=16)
    for copy in copies[:2]:
        copy.wait()
    for way in range(4):

        def mark(k, _, way=way):
            gone[slots[0, way, k]] = 1
            return 0

        lax.fori_loop(0, counts[0, way], mark, 0)
    live = count[0]

    def gather(c, found):
        order[found] = c
        stays = jnp.logical_and(c < live, gone[c] == 0)
        return found + stays.astype(jnp.int32)

    found = lax.fori_loop(0, SLOTS, gather, 0, unroll=16)
    for copy in copies[2:]:
        copy.wait()
    for odd in range(2):
        up, way = way_of("gx", odd)
        pack_records(xr.at[odd], rec, slots, counts[0, way], way)
        xr[odd, X_CONC:X_POT] = conc[:, up * (BX - 1)].reshape(6, 8, NZ)

    def group(c, _):
        def kept_row(g):
            at = c * GROUP + g
            inside = at < found
            slot = jnp.where(inside, order[at], 0)
            return nodes[pl.ds(slot, 1), :], jnp.where(inside, rec[slot], 0.0)

        left, right = hot_group(kept_row, a_s, b_s)
        acc[0] += left
        acc[1] += right
        return 0

    lax.fori_loop(0, (found + GROUP - 1) // GROUP, group, 0)


def pack_x_kernel(xr, pot, eps, y0, y1, s0, s1):
    px, py = parity("gx"), parity("gy")
    for n, (out, up) in enumerate(((s0, 1 - px), (s1, px))):
        out[0:X_POT] = xr[n]
        for first, own, tile in ((X_POT, pot, Y_POT), (X_EPS, eps, Y_EPS)):
            own = own[pl.ds(up * W, W)]
            a, b = y0[pl.ds(tile + up * W, W)], y1[pl.ds(tile + up * W, W)]
            low, high = jnp.where(py == 1, a, b), jnp.where(py == 1, b, a)
            for x in range(W):
                out[first + 4 * x] = low[x]
                out[first + 4 * x + 1] = own[x, 0:8]
                out[first + 4 * x + 2] = own[x, 8:16]
                out[first + 4 * x + 3] = high[x]


def collect(buf0, buf1, way0, way1, nodes, rec, cells):
    for b, (buf, way) in enumerate(((buf0, way0), (buf1, way1))):
        for t in range(8):
            rec[b * 16 + 2 * t] = buf[t, 0:4]
            rec[b * 16 + 2 * t + 1] = buf[t, 4:8]
        cells[b * 16 : (b + 1) * 16] = nodes[0, way]


def arrive_y_kernel(acc_in, y0, y1, nodes, acc, a_s, b_s, rec, cells):
    py = parity("gy")
    collect(y0, y1, 3 - py, 2 + py, nodes, rec, cells)
    spread_groups(2 * MOVERS // GROUP, lambda r: (cells[pl.ds(r, 1), :], rec[r]), acc_in, acc, a_s, b_s)


def face_flux(s, upper, lower, step):
    return -DIFFUSION[s] * ((upper - lower) + (VALENCE[s] * 0.5) * (upper + lower) * step)


def spread_rows(acc, channel, ex, first, number):
    half, row = divmod(ex, WIDE // 2)
    base = (row * WIDE + first) * 8 + channel
    return acc[half, pl.ds(base, number, stride=8)] + acc[half, pl.ds(base + 4, number, stride=8)]


def arrive_x_kernel(acc_in, x0, x1, y0, y1, nodes, conc, pot, conc_next, acc, dens, s0, s1, a_s, b_s, rec, cells, wide):
    px, py = parity("gx"), parity("gy")
    x_low_first, y_low_first = px == 1, py == 1
    collect(x0, x1, 1 - px, px, nodes, rec, cells)
    spread_groups(2 * MOVERS // GROUP, lambda r: (cells[pl.ds(r, 1), :], rec[r]), acc_in, acc, a_s, b_s)

    for f in range(4):
        wide[f, 1 : BX + 1, 8 : 8 + BY] = conc[f] if f < 3 else pot[...]
        if f < 3:
            xa, xb = (x[X_CONC + 2 * f : X_CONC + 2 * f + 2].reshape(BY, NZ) for x in (x0, x1))
            x_low, x_high = jnp.where(x_low_first, xa, xb), jnp.where(x_low_first, xb, xa)
            ya, yb = (y[Y_CONC + 2 * f : Y_CONC + 2 * f + 2].reshape(BX, NZ) for y in (y0, y1))
            y_low, y_high = jnp.where(y_low_first, ya, yb), jnp.where(y_low_first, yb, ya)
        else:
            last, first = X_POT + 4 * (W - 1) + 1, X_POT + 1
            x_low = jnp.where(x_low_first, x0[last : last + 2], x1[last : last + 2]).reshape(BY, NZ)
            x_high = jnp.where(x_low_first, x1[first : first + 2], x0[first : first + 2]).reshape(BY, NZ)
            y_low = jnp.where(y_low_first, y0[Y_POT:Y_EPS, 7], y1[Y_POT:Y_EPS, 7])
            y_high = jnp.where(y_low_first, y1[Y_POT:Y_EPS, 0], y0[Y_POT:Y_EPS, 0])
        wide[f, 0, 8 : 8 + BY] = x_low
        wide[f, BX + 1, 8 : 8 + BY] = x_high
        wide[f, 1 : BX + 1, 7] = y_low
        wide[f, 1 : BX + 1, 8 + BY] = y_high

    dens[...] = jnp.zeros_like(dens)
    for ex in range(WIDE):
        dens[ex, 7 : 7 + WIDE] = spread_rows(acc, 0, ex, 0, WIDE)

    for x in range(BX):
        pc, pe, pw = wide[3, x + 1, 8:24], wide[3, x + 2, 8:24], wide[3, x, 8:24]
        pn, ps = wide[3, x + 1, 9:25], wide[3, x + 1, 7:23]
        pz = pltpu.roll(pc, NZ - 1, 1)
        dx, dw, dn, ds, dz = pe - pc, pc - pw, pn - pc, pc - ps, pz - pc
        total = dens[x + 1, 8:24]
        for s in range(3):
            c = wide[s, x + 1, 8:24]
            flux_x = face_flux(s, wide[s, x + 2, 8:24], c, dx)
            flux_w = face_flux(s, c, wide[s, x, 8:24], dw)
            flux_n = face_flux(s, wide[s, x + 1, 9:25], c, dn)
            flux_s = face_flux(s, c, wide[s, x + 1, 7:23], ds)
            flux_z = face_flux(s, pltpu.roll(c, NZ - 1, 1), c, dz)
            div = ((flux_x - flux_w) + (flux_n - flux_s)) + (flux_z - pltpu.roll(flux_z, 1, 1))
            later = c - TIME_STEP * div
            conc_next[s, x] = later
            total = total + VALENCE[s] * later
        dens[x + 1, 8:24] = total

    for out, up in ((s0, 1 - py), (s1, py)):
        for ex in range(WIDE):
            out[ex * 8 : ex * 8 + 8] = jnp.where(up == 1, dens[ex, 17:25], dens[ex, 7:15])
        for a in range(3):
            for half in range(2):
                rims = []
                for ey in (0, WIDE - 1):
                    base = ey * 8 + a + 1
                    lead = acc[half, pl.ds(base, WIDE // 2, stride=WIDE * 8)]
                    rims.append(lead + acc[half, pl.ds(base + 4, WIDE // 2, stride=WIDE * 8)])
                r = DY_FORCE + a * WIDE + half * (WIDE // 2)
                out[r : r + WIDE // 2] = jnp.where(up == 1, rims[1], rims[0])
        out[DY_FORCE + 54 : DY_END] = jnp.zeros((2, NZ), F32)


def coefficient_kernel(acc, x0, x1, y0, y1, pot, eps, force, phi, xp, xm, yp, ym, zp, zm, inv, ew):
    px, py = parity("gx"), parity("gy")
    x_low_first, y_low_first = px == 1, py == 1
    for c in range(3):
        for ex in range(WIDE):
            force[c, ex] = spread_rows(acc, c + 1, ex, 1, BY)
    for buf, own, x_tile, y_tile in ((phi, pot, X_POT, Y_POT), (ew, eps, X_EPS, Y_EPS)):
        buf[W : W + BX, W : W + BY] = own[...]
        a, b = y0[y_tile : y_tile + BX], y1[y_tile : y_tile + BX]
        buf[W : W + BX, 0:W] = jnp.where(y_low_first, a, b)
        buf[W : W + BX, W + BY : EXT] = jnp.where(y_low_first, b, a)
        a, b = (x[x_tile : x_tile + 4 * W].reshape(W, EXT, NZ) for x in (x0, x1))
        buf[0:W] = jnp.where(x_low_first, a, b)
        buf[W + BX : EXT] = jnp.where(x_low_first, b, a)
    for x in range(1, EXT - 1):
        e = ew[x]
        up, down = e + ew[x + 1], e + ew[x - 1]
        north, south = e + pltpu.roll(e, EXT - 1, 0), e + pltpu.roll(e, 1, 0)
        over = e + pltpu.roll(e, NZ - 1, 1)
        under = pltpu.roll(over, 1, 1)
        scale = 1.0 / ((((up + down) + (north + south)) + (over + under)) + 2.0 * SCREENING)
        xp[x], xm[x] = up * scale, down * scale
        yp[x], ym[x] = north * scale, south * scale
        zp[x], zm[x] = over * scale, under * scale
        inv[x] = 2.0 * scale
    for buf in (xp, xm, yp, ym, zp, zm, inv):
        buf[0] = jnp.zeros((EXT, NZ), F32)
        buf[EXT - 1] = jnp.zeros((EXT, NZ), F32)


def join_y_kernel(dens, force, r0, r1, dext, fcore, s0, s1):
    px, py = parity("gx"), parity("gy")
    low_first = py == 1
    dext[0:7] = jnp.zeros((7, EXT, NZ), F32)
    dext[25:32] = jnp.zeros((7, EXT, NZ), F32)
    for ex in range(WIDE):
        dext[ex + 7] = dens[ex]
        a, b = r0[ex * 8 : ex * 8 + 8], r1[ex * 8 : ex * 8 + 8]
        dext[ex + 7, 1:9] += jnp.where(low_first, a, b)
        dext[ex + 7, 23:31] += jnp.where(low_first, b, a)
    fcore[...] = force[...]
    for c in range(3):
        r = DY_FORCE + c * WIDE
        a, b = r0[r : r + WIDE], r1[r : r + WIDE]
        fcore[c, :, 0] += jnp.where(low_first, a, b)
        fcore[c, :, BY - 1] += jnp.where(low_first, b, a)
    for out, up in ((s0, 1 - px), (s1, px)):
        out[0:DX_FORCE] = dext[pl.ds(7 + 10 * up, 8)].reshape(32, 8, NZ)
        out[DX_FORCE:DX_END] = fcore[:, up * (WIDE - 1)].reshape(6, 8, NZ)


def sweep_kernel(dext, fcore, r0, r1, phi, xp, xm, yp, ym, zp, zm, inv, pot_next, force, phi_a, phi_b, rhs):
    low_first = parity("gx") == 1
    force[...] = fcore[:, 1 : BX + 1]
    a, b = (r[DX_FORCE:DX_END].reshape(3, BY, NZ) for r in (r0, r1))
    force[:, 0] += jnp.where(low_first, a, b)
    force[:, BX - 1] += jnp.where(low_first, b, a)

    for x in range(1, EXT - 1):
        total = dext[x]
        if x < 9 or x > 22:
            t = 4 * (x - 1 if x < 9 else x - 23)
            a, b = (r[t : t + 4].reshape(EXT, NZ) for r in (r0, r1))
            total = total + (jnp.where(low_first, a, b) if x < 9 else jnp.where(low_first, b, a))
        rhs[x] = total * inv[x]

    for k in range(1, SWEEPS + 1):
        old = phi if k == 1 else (phi_a, phi_b)[k % 2]
        new = (phi_a, phi_b)[(k + 1) % 2]
        for x in range(k, EXT - k):
            if k < SWEEPS:
                f = slice(0, EXT)
                here = old[x]
                north, south = pltpu.roll(here, EXT - 1, 0), pltpu.roll(here, 1, 0)
            else:
                f = slice(W, W + BY)
                here = old[x, f]
                north, south = old[x, W + 1 : W + BY + 1], old[x, W - 1 : W + BY - 1]
            total = (xp[x, f] * old[x + 1, f] + xm[x, f] * old[x - 1, f]) + (yp[x, f] * north + ym[x, f] * south)
            total += (zp[x, f] * pltpu.roll(here, NZ - 1, 1) + zm[x, f] * pltpu.roll(here, 1, 1)) + rhs[x, f]
            if k < SWEEPS:
                new[x] = total
            else:
                pot_next[x - W] = total


def shape(*dims):
    return jax.ShapeDtypeStruct(dims, F32)


def call(kernel, name, ins, outs, scratch=(), flops=0):
    moved = 4 * sum(int(o.size) for o in outs)
    return pl.pallas_call(
        kernel,
        name=name,
        in_specs=ins,
        out_specs=[VMEM] * len(outs),
        out_shape=outs,
        scratch_shapes=scratch,
        compiler_params=pltpu.CompilerParams(vmem_limit_bytes=32 << 20),
        cost_estimate=pl.CostEstimate(flops=flops, bytes_accessed=moved, transcendentals=0),
    )


def body(conc, pot, eps, records, count, slots, counts, own_nodes, arrive_nodes):
    hot = [pltpu.VMEM((ROWS, GROUP * NODES), BF16), pltpu.VMEM((2 * NZ, GROUP * NODES), BF16)]
    some = [pltpu.VMEM((2 * MOVERS, CHANNELS, NODES), F32), pltpu.VMEM((2 * MOVERS, NODES), jnp.int32)]
    sums = shape(2, ROWS, NZ)
    row_flops = 2 * ROWS * 2 * NZ * NODES
    field = shape(EXT, EXT, NZ)
    core = shape(BX, BY, NZ)

    ins = [pltpu.with_memory_space_constraint(x, pltpu.HBM) for x in (conc, pot, eps, records)]
    lists = [pltpu.with_memory_space_constraint(x, pltpu.HBM) for x in (slots, counts)]
    more = [pltpu.with_memory_space_constraint(x, pltpu.HBM) for x in (own_nodes, arrive_nodes)]
    small = [pltpu.SMEM((1, 4, MOVERS), jnp.int32), pltpu.SMEM((1, 4), jnp.int32)]
    rec = pltpu.VMEM((SLOTS, CHANNELS, NODES), F32)
    a0, a1 = call(
        first_kernel,
        "first",
        [HBM] * 6,
        [shape(Y_END, 8, NZ)] * 2,
        [pltpu.VMEM((3, BX, BY, NZ), F32), rec, *small, pltpu.SemaphoreType.DMA((8,))],
    )(*ins, *lists)
    y0, y1 = swap(a0, "gy", 0), swap(a1, "gy", 1)
    conc_v, pot_v, eps_v, arrive_v, xr, acc = call(
        kept_kernel,
        "spread_kept",
        [HBM] * 8 + [SMEM],
        [shape(3, BX, BY, NZ), core, core, jax.ShapeDtypeStruct((1, 4, MOVERS, NODES), jnp.int32), shape(2, X_POT, 8, NZ), sums],
        [
            rec, pltpu.VMEM((SLOTS, NODES), jnp.int32), *small, pltpu.SMEM((SLOTS,), jnp.int32),
            pltpu.SMEM((SLOTS + GROUP,), jnp.int32), *hot, pltpu.SemaphoreType.DMA((8,)),
        ],
        flops=row_flops * 64,
    )(*ins, *more, *lists, count)
    b0, b1 = call(pack_x_kernel, "pack_x", [VMEM] * 5, [shape(X_END, 8, NZ)] * 2)(xr, pot_v, eps_v, y0, y1)
    x1, x0 = swap(b1, "gx", 1), swap(b0, "gx", 0)
    (acc,) = call(arrive_y_kernel, "spread_y", [VMEM] * 4, [sums], hot + some, flops=row_flops * 2 * MOVERS)(
        acc, y0, y1, arrive_v
    )
    conc_next, acc, dens, c0, c1 = call(
        arrive_x_kernel,
        "spread_x",
        [VMEM] * 8,
        [shape(3, BX, BY, NZ), sums, shape(WIDE, EXT, NZ), shape(DY_END, NZ), shape(DY_END, NZ)],
        hot + some + [pltpu.VMEM((4, WIDE, 32, NZ), F32)],
        flops=row_flops * 2 * MOVERS,
    )(acc, x0, x1, y0, y1, arrive_v, conc_v, pot_v)
    r0, r1 = swap(c0, "gy", 0), swap(c1, "gy", 1)
    force, phi, *weights = call(
        coefficient_kernel,
        "coefficients",
        [VMEM] * 7,
        [shape(3, WIDE, BY, NZ)] + [field] * 8,
        [pltpu.VMEM((EXT, EXT, NZ), F32)],
        flops=row_flops * 8,
    )(acc, x0, x1, y0, y1, pot_v, eps_v)
    dext, fcore, e0, e1 = call(
        join_y_kernel, "join_y", [VMEM] * 4, [field, shape(3, WIDE, BY, NZ), shape(DX_END, 8, NZ), shape(DX_END, 8, NZ)]
    )(dens, force, r0, r1)
    g1, g0 = swap(e1, "gx", 1), swap(e0, "gx", 0)
    pot_next, body_force = call(
        sweep_kernel,
        "sweeps",
        [VMEM] * 12,
        [core, shape(3, BX, BY, NZ)],
        [pltpu.VMEM((EXT, EXT, NZ), F32)] * 3,
        flops=20 * SWEEPS * EXT * EXT * NZ,
    )(dext, fcore, g0, g1, phi, *weights)
    return conc_next, pot_next, body_force


def solution(mesh):
    placed = (
        P(None, "gx", "gy", None),
        P("gx", "gy", None),
        P("gx", "gy", None),
        P(("gx", "gy"), None, None),
        P(("gx", "gy")),
        P(("gx", "gy"), None, None),
        P(("gx", "gy"), None),
        P(("gx", "gy"), None),
        P(("gx", "gy"), None, None, None),
    )
    return jax.shard_map(
        body,
        mesh=mesh,
        in_specs=placed,
        out_specs=(P(None, "gx", "gy", None), P("gx", "gy", None), P(None, "gx", "gy", None)),
        check_vma=False,
    )
```

```python
import jax
import jax.numpy as jnp
from jax import lax
from jax.experimental import pallas as pl
from jax.experimental.pallas import tpu as pltpu
from jax.sharding import PartitionSpec as P

SWEEPS = 8
DIFFUSION = (1.0, 0.7, 0.45)
VALENCE = (1.0, -1.0, 2.0)
TIME_STEP = 0.05
SCREENING = 0.05

F32 = jnp.float32
BF16 = jnp.bfloat16
BX, BY, NZ = 16, 16, 128
SLOTS, MOVERS, CHANNELS, NODES = 128, 16, 4, 128
W = 8
EXT = BX + 2 * W
WIDE = BX + 2
PAIRS = WIDE * WIDE // 2
ROWS = PAIRS * 2 * CHANNELS
GROUP = 8
EARLY = 5
STORE = SLOTS + GROUP

Y_CONC, Y_POT, Y_EPS, Y_NUM, Y_END = 8, 14, 30, 46, 47
X_CONC, X_POT, X_EPS, X_NUM, X_END = 8, 14, 46, 78, 79
DY_FORCE, DY_END = WIDE * W, WIDE * W + 56
DX_FORCE, DX_END = 32, 38

VMEM = pl.BlockSpec(memory_space=pltpu.VMEM)
SMEM = pl.BlockSpec(memory_space=pltpu.SMEM)
HBM = pl.BlockSpec(memory_space=pltpu.HBM)


def parity(axis):
    return lax.rem(lax.axis_index(axis), 2)


def swap(block, axis, odd):
    count = lax.axis_size(axis)
    route = [(i, (((i - odd) % count ^ 1) + odd) % count) for i in range(count)]
    return lax.ppermute(block, axis, route)


def hot_group(first, rec, cells, a_s, b_s):
    sub = lax.broadcasted_iota(jnp.int32, (16, NODES), 0)
    second = (sub >= 8).astype(F32)
    subf = sub.astype(F32)
    for g in range(GROUP):
        cell, value = cells[first + g], rec[first + g]
        half = (cell >= PAIRS * NZ).astype(jnp.int32)
        high = ((cell - half * (PAIRS * NZ)) >> 7).astype(F32)
        low = ((cell & (NZ - 1)) + half * NZ).astype(F32)
        high = (jnp.broadcast_to(high, (16, NODES)) - second).astype(BF16)
        low = (jnp.broadcast_to(low, (16, NODES)) - subf).astype(BF16)
        lead = value.astype(BF16).astype(F32)
        rest = value - lead
        parts = jnp.concatenate([lead, rest, lead, rest], axis=0).astype(BF16)
        lanes = slice(g * NODES, (g + 1) * NODES)
        for m in range(ROWS // 16):
            a_s[m * 16 : (m + 1) * 16, lanes] = jnp.where(high == BF16(2 * m), parts, BF16(0))
        for m in range(16):
            b_s[m * 16 : (m + 1) * 16, lanes] = jnp.where(low == BF16(16 * m), BF16(1), BF16(0))
    sums = lax.dot_general(a_s[...], b_s[...], (((1,), (1,)), ((), ())), preferred_element_type=F32)
    return sums[:, :NZ], sums[:, NZ:]


def spread_groups(start, stop, rec, cells, acc, a_s, b_s):
    def group(c, _):
        left, right = hot_group(c * GROUP, rec, cells, a_s, b_s)
        acc[0] += left
        acc[1] += right
        return 0

    lax.fori_loop(start, stop, group, 0)


def number_in(tile):
    return jnp.max(tile).astype(jnp.int32)


def append(total, buf, number_tile, way, nodes, rec, cells):
    for k in range(MOVERS):
        rec[total + k] = buf[k // 2, (k % 2) * 4 : (k % 2) * 4 + 4]
        cells[total + k] = nodes[0, way, k : k + 1]
    return total + number_in(buf[number_tile])


def way_of(axis, odd):
    p = parity(axis)
    up = 1 - p if odd == 0 else p
    return up, (1 if axis == "gx" else 3) - up


def pack_records(out, rec, slots, number, way, number_tile):
    out[number_tile] = jnp.full((8, NZ), number.astype(F32))
    for k in range(MOVERS):
        row = rec[slots[0, way, k]]
        out[k // 2, (k % 2) * 4 : (k % 2) * 4 + 4] = jnp.where(k < number, row, 0.0)


def first_kernel(conc_h, pot_h, eps_h, rec_h, slots_h, counts_h, s1, s0, conc, rec, slots, counts, sems):
    copies = [(slots_h, slots), (counts_h, counts), (rec_h, rec), (conc_h, conc)]
    for odd, out in enumerate((s0, s1)):
        start = pl.multiple_of(way_of("gy", odd)[0] * W, W)
        copies.append((pot_h.at[:, pl.ds(start, W)], out.at[pl.ds(Y_POT, BX)]))
        copies.append((eps_h.at[:, pl.ds(start, W)], out.at[pl.ds(Y_EPS, BX)]))
    copies = [pltpu.make_async_copy(a, b, sems.at[n]) for n, (a, b) in enumerate(copies)]
    for copy in copies:
        copy.start()
    for copy in copies:
        copy.wait()
    for odd, out in enumerate((s0, s1)):
        up, way = way_of("gy", odd)
        pack_records(out, rec, slots, counts[0, way], way, Y_NUM)
        for s in range(3):
            face = jnp.where(up == 1, conc[s, :, BY - 1], conc[s, :, 0])
            out[Y_CONC + 2 * s : Y_CONC + 2 * s + 2] = face.reshape(2, 8, NZ)


def kept_kernel(
    conc_h, pot_h, eps_h, rec_h, nodes_h, arrive_h, slots_h, counts_h, count,
    conc, pot, eps, arrive, xr, rows, cells, state, acc,
    rec, nodes, slots, counts, gone, a_s, b_s, sems,
):
    pairs = (
        (slots_h, slots), (counts_h, counts), (rec_h, rec), (nodes_h, nodes),
        (conc_h, conc), (pot_h, pot), (eps_h, eps), (arrive_h, arrive),
    )
    copies = [pltpu.make_async_copy(a, b, sems.at[n]) for n, (a, b) in enumerate(pairs)]
    for copy in copies:
        copy.start()
    acc[...] = jnp.zeros_like(acc)

    def clear(c, _):
        gone[c] = 0
        return 0

    lax.fori_loop(0, SLOTS, clear, 0, unroll=16)
    for copy in copies[:2]:
        copy.wait()
    for way in range(4):

        def mark(k, _, way=way):
            gone[slots[0, way, k]] = 1
            return 0

        lax.fori_loop(0, counts[0, way], mark, 0)
    live = count[0]
    for copy in copies[2:]:
        copy.wait()

    def gather(c, found):
        rows[found] = rec[c]
        cells[found] = nodes[pl.ds(c, 1), :]
        stays = jnp.logical_and(c < live, gone[c] == 0)
        return found + stays.astype(jnp.int32)

    found = lax.fori_loop(0, SLOTS, gather, 0, unroll=16)
    state[...] = jnp.full((8, NZ), found.astype(F32))
    for odd in range(2):
        up, way = way_of("gx", odd)
        pack_records(xr.at[odd], rec, slots, counts[0, way], way, X_POT)
        xr[odd, X_CONC:X_POT] = conc[:, up * (BX - 1)].reshape(6, 8, NZ)
    spread_groups(0, jnp.minimum(EARLY, found // GROUP), rows, cells, acc, a_s, b_s)


def pack_x_kernel(xr, pot, eps, y0, y1, s1, s0):
    px, py = parity("gx"), parity("gy")
    for n, (out, up) in enumerate(((s0, 1 - px), (s1, px))):
        out[0:X_POT] = xr[n, 0:X_POT]
        out[X_NUM] = xr[n, X_POT]
        for first, own, tile in ((X_POT, pot, Y_POT), (X_EPS, eps, Y_EPS)):
            own = own[pl.ds(up * W, W)]
            a, b = y0[pl.ds(tile + up * W, W)], y1[pl.ds(tile + up * W, W)]
            low, high = jnp.where(py == 1, a, b), jnp.where(py == 1, b, a)
            for x in range(W):
                out[first + 4 * x] = low[x]
                out[first + 4 * x + 1] = own[x, 0:8]
                out[first + 4 * x + 2] = own[x, 8:16]
                out[first + 4 * x + 3] = high[x]


def arrive_y_kernel(acc_in, rows_in, cells_in, state, y0, y1, nodes, rows, cells, state_out, acc, a_s, b_s, rec, cell):
    py = parity("gy")
    acc[...] = acc_in[...]
    rec[0:STORE] = rows_in[...]
    cell[0:STORE] = cells_in[...]
    found = number_in(state[...])
    total = append(found, y0, Y_NUM, 3 - py, nodes, rec, cell)
    total = append(total, y1, Y_NUM, 2 + py, nodes, rec, cell)
    done = total // GROUP
    spread_groups(jnp.minimum(EARLY, found // GROUP), done, rec, cell, acc, a_s, b_s)
    for g in range(GROUP):
        rows[g] = rec[done * GROUP + g]
        cells[g] = cell[done * GROUP + g]
    state_out[...] = jnp.full((8, NZ), (total - done * GROUP).astype(F32))


def face_flux(s, upper, lower, step):
    return -DIFFUSION[s] * ((upper - lower) + (VALENCE[s] * 0.5) * (upper + lower) * step)


def spread_rows(acc, channel, ex, first, number):
    half, row = divmod(ex, WIDE // 2)
    base = (row * WIDE + first) * 8 + channel
    return acc[half, pl.ds(base, number, stride=8)] + acc[half, pl.ds(base + 4, number, stride=8)]


def arrive_x_kernel(
    acc_in, rows, cells, state, x0, x1, y0, y1, nodes, conc, pot,
    conc_next, acc, dens, s1, s0,
    a_s, b_s, rec, cell, wide,
):
    px, py = parity("gx"), parity("gy")
    x_low_first, y_low_first = px == 1, py == 1
    acc[...] = acc_in[...]
    rec[0:GROUP] = rows[...]
    cell[0:GROUP] = cells[...]
    total = append(number_in(state[...]), x0, X_NUM, 1 - px, nodes, rec, cell)
    total = append(total, x1, X_NUM, px, nodes, rec, cell)
    for g in range(GROUP):
        rec[total + g] = jnp.zeros((CHANNELS, NODES), F32)
        cell[total + g] = jnp.zeros((1, NODES), jnp.int32)
    spread_groups(0, (total + GROUP - 1) // GROUP, rec, cell, acc, a_s, b_s)

    for f in range(4):
        wide[f, 1 : BX + 1, 8 : 8 + BY] = conc[f] if f < 3 else pot[...]
        if f < 3:
            xa, xb = (x[X_CONC + 2 * f : X_CONC + 2 * f + 2].reshape(BY, NZ) for x in (x0, x1))
            x_low, x_high = jnp.where(x_low_first, xa, xb), jnp.where(x_low_first, xb, xa)
            ya, yb = (y[Y_CONC + 2 * f : Y_CONC + 2 * f + 2].reshape(BX, NZ) for y in (y0, y1))
            y_low, y_high = jnp.where(y_low_first, ya, yb), jnp.where(y_low_first, yb, ya)
        else:
            last, first = X_POT + 4 * (W - 1) + 1, X_POT + 1
            x_low = jnp.where(x_low_first, x0[last : last + 2], x1[last : last + 2]).reshape(BY, NZ)
            x_high = jnp.where(x_low_first, x1[first : first + 2], x0[first : first + 2]).reshape(BY, NZ)
            y_low = jnp.where(y_low_first, y0[Y_POT:Y_EPS, 7], y1[Y_POT:Y_EPS, 7])
            y_high = jnp.where(y_low_first, y1[Y_POT:Y_EPS, 0], y0[Y_POT:Y_EPS, 0])
        wide[f, 0, 8 : 8 + BY] = x_low
        wide[f, BX + 1, 8 : 8 + BY] = x_high
        wide[f, 1 : BX + 1, 7] = y_low
        wide[f, 1 : BX + 1, 8 + BY] = y_high

    dens[...] = jnp.zeros_like(dens)
    for ex in range(WIDE):
        dens[ex, 7 : 7 + WIDE] = spread_rows(acc, 0, ex, 0, WIDE)

    for x in range(BX):
        pc, pe, pw = wide[3, x + 1, 8:24], wide[3, x + 2, 8:24], wide[3, x, 8:24]
        pn, ps = wide[3, x + 1, 9:25], wide[3, x + 1, 7:23]
        pz = pltpu.roll(pc, NZ - 1, 1)
        dx, dw, dn, ds, dz = pe - pc, pc - pw, pn - pc, pc - ps, pz - pc
        total = dens[x + 1, 8:24]
        for s in range(3):
            c = wide[s, x + 1, 8:24]
            flux_x = face_flux(s, wide[s, x + 2, 8:24], c, dx)
            flux_w = face_flux(s, c, wide[s, x, 8:24], dw)
            flux_n = face_flux(s, wide[s, x + 1, 9:25], c, dn)
            flux_s = face_flux(s, c, wide[s, x + 1, 7:23], ds)
            flux_z = face_flux(s, pltpu.roll(c, NZ - 1, 1), c, dz)
            div = ((flux_x - flux_w) + (flux_n - flux_s)) + (flux_z - pltpu.roll(flux_z, 1, 1))
            later = c - TIME_STEP * div
            conc_next[s, x] = later
            total = total + VALENCE[s] * later
        dens[x + 1, 8:24] = total

    for out, up in ((s0, 1 - py), (s1, py)):
        for ex in range(WIDE):
            out[ex * 8 : ex * 8 + 8] = jnp.where(up == 1, dens[ex, 17:25], dens[ex, 7:15])
        for a in range(3):
            for half in range(2):
                rims = []
                for ey in (0, WIDE - 1):
                    base = ey * 8 + a + 1
                    lead = acc[half, pl.ds(base, WIDE // 2, stride=WIDE * 8)]
                    rims.append(lead + acc[half, pl.ds(base + 4, WIDE // 2, stride=WIDE * 8)])
                r = DY_FORCE + a * WIDE + half * (WIDE // 2)
                out[r : r + WIDE // 2] = jnp.where(up == 1, rims[1], rims[0])
        out[DY_FORCE + 54 : DY_END] = jnp.zeros((2, NZ), F32)


def coefficient_kernel(acc, x0, x1, y0, y1, pot, eps, force, phi, xp, xm, yp, ym, zp, zm, inv, ew):
    px, py = parity("gx"), parity("gy")
    x_low_first, y_low_first = px == 1, py == 1
    for c in range(3):
        for ex in range(WIDE):
            force[c, ex] = spread_rows(acc, c + 1, ex, 1, BY)
    for buf, own, x_tile, y_tile in ((phi, pot, X_POT, Y_POT), (ew, eps, X_EPS, Y_EPS)):
        buf[W : W + BX, W : W + BY] = own[...]
        a, b = y0[y_tile : y_tile + BX], y1[y_tile : y_tile + BX]
        buf[W : W + BX, 0:W] = jnp.where(y_low_first, a, b)
        buf[W : W + BX, W + BY : EXT] = jnp.where(y_low_first, b, a)
        a, b = (x[x_tile : x_tile + 4 * W].reshape(W, EXT, NZ) for x in (x0, x1))
        buf[0:W] = jnp.where(x_low_first, a, b)
        buf[W + BX : EXT] = jnp.where(x_low_first, b, a)
    for x in range(1, EXT - 1):
        e = ew[x]
        up, down = e + ew[x + 1], e + ew[x - 1]
        north, south = e + pltpu.roll(e, EXT - 1, 0), e + pltpu.roll(e, 1, 0)
        over = e + pltpu.roll(e, NZ - 1, 1)
        under = pltpu.roll(over, 1, 1)
        scale = 1.0 / ((((up + down) + (north + south)) + (over + under)) + 2.0 * SCREENING)
        xp[x], xm[x] = up * scale, down * scale
        yp[x], ym[x] = north * scale, south * scale
        zp[x], zm[x] = over * scale, under * scale
        inv[x] = 2.0 * scale
    for buf in (xp, xm, yp, ym, zp, zm, inv):
        buf[0] = jnp.zeros((EXT, NZ), F32)
        buf[EXT - 1] = jnp.zeros((EXT, NZ), F32)


def join_y_kernel(dens, force, r0, r1, dext, fcore, s1, s0):
    px, py = parity("gx"), parity("gy")
    low_first = py == 1
    dext[0:7] = jnp.zeros((7, EXT, NZ), F32)
    dext[25:32] = jnp.zeros((7, EXT, NZ), F32)
    for ex in range(WIDE):
        dext[ex + 7] = dens[ex]
        a, b = r0[ex * 8 : ex * 8 + 8], r1[ex * 8 : ex * 8 + 8]
        dext[ex + 7, 1:9] += jnp.where(low_first, a, b)
        dext[ex + 7, 23:31] += jnp.where(low_first, b, a)
    fcore[...] = force[...]
    for c in range(3):
        r = DY_FORCE + c * WIDE
        a, b = r0[r : r + WIDE], r1[r : r + WIDE]
        fcore[c, :, 0] += jnp.where(low_first, a, b)
        fcore[c, :, BY - 1] += jnp.where(low_first, b, a)
    for out, up in ((s0, 1 - px), (s1, px)):
        out[0:DX_FORCE] = dext[pl.ds(7 + 10 * up, 8)].reshape(32, 8, NZ)
        out[DX_FORCE:DX_END] = fcore[:, up * (WIDE - 1)].reshape(6, 8, NZ)


def sweep_kernel(dext, fcore, r0, r1, phi, xp, xm, yp, ym, zp, zm, inv, pot_next, force, phi_a, phi_b, rhs):
    low_first = parity("gx") == 1
    force[...] = fcore[:, 1 : BX + 1]
    a, b = (r[DX_FORCE:DX_END].reshape(3, BY, NZ) for r in (r0, r1))
    force[:, 0] += jnp.where(low_first, a, b)
    force[:, BX - 1] += jnp.where(low_first, b, a)

    for x in range(1, EXT - 1):
        total = dext[x]
        if x < 9 or x > 22:
            t = 4 * (x - 1 if x < 9 else x - 23)
            a, b = (r[t : t + 4].reshape(EXT, NZ) for r in (r0, r1))
            total = total + (jnp.where(low_first, a, b) if x < 9 else jnp.where(low_first, b, a))
        rhs[x] = total * inv[x]

    for k in range(1, SWEEPS + 1):
        old = phi if k == 1 else (phi_a, phi_b)[k % 2]
        new = (phi_a, phi_b)[(k + 1) % 2]
        for x in range(k, EXT - k):
            if k < SWEEPS:
                f = slice(0, EXT)
                here = old[x]
                north, south = pltpu.roll(here, EXT - 1, 0), pltpu.roll(here, 1, 0)
            else:
                f = slice(W, W + BY)
                here = old[x, f]
                north, south = old[x, W + 1 : W + BY + 1], old[x, W - 1 : W + BY - 1]
            total = (xp[x, f] * old[x + 1, f] + xm[x, f] * old[x - 1, f]) + (yp[x, f] * north + ym[x, f] * south)
            total += (zp[x, f] * pltpu.roll(here, NZ - 1, 1) + zm[x, f] * pltpu.roll(here, 1, 1)) + rhs[x, f]
            if k < SWEEPS:
                new[x] = total
            else:
                pot_next[x - W] = total


def shape(*dims):
    return jax.ShapeDtypeStruct(dims, F32)


def call(kernel, name, ins, outs, scratch=(), flops=0):
    moved = 4 * sum(int(o.size) for o in outs)
    return pl.pallas_call(
        kernel,
        name=name,
        in_specs=ins,
        out_specs=[VMEM] * len(outs),
        out_shape=outs,
        scratch_shapes=scratch,
        compiler_params=pltpu.CompilerParams(vmem_limit_bytes=32 << 20),
        cost_estimate=pl.CostEstimate(flops=flops, bytes_accessed=moved, transcendentals=0),
    )


def body(conc, pot, eps, records, count, slots, counts, own_nodes, arrive_nodes):
    hot = [pltpu.VMEM((ROWS, GROUP * NODES), BF16), pltpu.VMEM((2 * NZ, GROUP * NODES), BF16)]
    def store(number, kind=pltpu.VMEM):
        return [kind((number, CHANNELS, NODES), F32), kind((number, 1, NODES), jnp.int32)]

    sums = shape(2, ROWS, NZ)
    row_flops = 2 * ROWS * 2 * NZ * NODES
    field = shape(EXT, EXT, NZ)
    core = shape(BX, BY, NZ)

    ins = [pltpu.with_memory_space_constraint(x, pltpu.HBM) for x in (conc, pot, eps, records)]
    lists = [pltpu.with_memory_space_constraint(x, pltpu.HBM) for x in (slots, counts)]
    more = [pltpu.with_memory_space_constraint(x, pltpu.HBM) for x in (own_nodes, arrive_nodes)]
    small = [pltpu.SMEM((1, 4, MOVERS), jnp.int32), pltpu.SMEM((1, 4), jnp.int32)]
    rec = pltpu.VMEM((SLOTS, CHANNELS, NODES), F32)
    a1, a0 = call(
        first_kernel,
        "first",
        [HBM] * 6,
        [shape(Y_END, 8, NZ)] * 2,
        [pltpu.VMEM((3, BX, BY, NZ), F32), rec, *small, pltpu.SemaphoreType.DMA((8,))],
    )(*ins, *lists)
    y0, y1 = swap(a0, "gy", 0), swap(a1, "gy", 1)
    conc_v, pot_v, eps_v, arrive_v, xr, rows, cells, state, acc = call(
        kept_kernel,
        "spread_kept",
        [HBM] * 8 + [SMEM],
        [
            shape(3, BX, BY, NZ), core, core, jax.ShapeDtypeStruct((1, 4, MOVERS, NODES), jnp.int32),
            shape(2, X_POT + 1, 8, NZ), *store(STORE, jax.ShapeDtypeStruct), shape(8, NZ), sums,
        ],
        [rec, pltpu.VMEM((SLOTS, NODES), jnp.int32), *small, pltpu.SMEM((SLOTS,), jnp.int32), *hot, pltpu.SemaphoreType.DMA((8,))],
        flops=row_flops * EARLY * GROUP,
    )(*ins, *more, *lists, count)
    b1, b0 = call(pack_x_kernel, "pack_x", [VMEM] * 5, [shape(X_END, 8, NZ)] * 2)(xr, pot_v, eps_v, y0, y1)
    x1, x0 = swap(b1, "gx", 1), swap(b0, "gx", 0)
    rows, cells, state, acc = call(
        arrive_y_kernel,
        "spread_y",
        [VMEM] * 7,
        [*store(GROUP, jax.ShapeDtypeStruct), shape(8, NZ), sums],
        hot + store(STORE + 2 * MOVERS + GROUP),
        flops=row_flops * 48,
    )(acc, rows, cells, state, y0, y1, arrive_v)
    conc_next, acc, dens, c1, c0 = call(
        arrive_x_kernel,
        "spread_x",
        [VMEM] * 11,
        [shape(3, BX, BY, NZ), sums, shape(WIDE, EXT, NZ), shape(DY_END, NZ), shape(DY_END, NZ)],
        hot + store(2 * MOVERS + 2 * GROUP) + [pltpu.VMEM((4, WIDE, 32, NZ), F32)],
        flops=row_flops * 2 * MOVERS,
    )(acc, rows, cells, state, x0, x1, y0, y1, arrive_v, conc_v, pot_v)
    r0, r1 = swap(c0, "gy", 0), swap(c1, "gy", 1)
    force, phi, *weights = call(
        coefficient_kernel,
        "coefficients",
        [VMEM] * 7,
        [shape(3, WIDE, BY, NZ)] + [field] * 8,
        [pltpu.VMEM((EXT, EXT, NZ), F32)],
        flops=row_flops * 8,
    )(acc, x0, x1, y0, y1, pot_v, eps_v)
    dext, fcore, e1, e0 = call(
        join_y_kernel, "join_y", [VMEM] * 4, [field, shape(3, WIDE, BY, NZ), shape(DX_END, 8, NZ), shape(DX_END, 8, NZ)]
    )(dens, force, r0, r1)
    g1, g0 = swap(e1, "gx", 1), swap(e0, "gx", 0)
    pot_next, body_force = call(
        sweep_kernel,
        "sweeps",
        [VMEM] * 12,
        [core, shape(3, BX, BY, NZ)],
        [pltpu.VMEM((EXT, EXT, NZ), F32)] * 3,
        flops=20 * SWEEPS * EXT * EXT * NZ,
    )(dext, fcore, g0, g1, phi, *weights)
    return conc_next, pot_next, body_force


def solution(mesh):
    placed = (
        P(None, "gx", "gy", None),
        P("gx", "gy", None),
        P("gx", "gy", None),
        P(("gx", "gy"), None, None),
        P(("gx", "gy")),
        P(("gx", "gy"), None, None),
        P(("gx", "gy"), None),
        P(("gx", "gy"), None),
        P(("gx", "gy"), None, None, None),
    )
    return jax.shard_map(
        body,
        mesh=mesh,
        in_specs=placed,
        out_specs=(P(None, "gx", "gy", None), P("gx", "gy", None), P(None, "gx", "gy", None)),
        check_vma=False,
    )
```

```python
import jax
import jax.numpy as jnp
from jax import lax
from jax.experimental import pallas as pl
from jax.experimental.pallas import tpu as pltpu
from jax.sharding import PartitionSpec as P

SWEEPS = 8
DIFFUSION = (1.0, 0.7, 0.45)
VALENCE = (1.0, -1.0, 2.0)
TIME_STEP = 0.05
SCREENING = 0.05

F32 = jnp.float32
BF16 = jnp.bfloat16
BX, BY, NZ = 16, 16, 128
SLOTS, MOVERS, CHANNELS, NODES = 128, 16, 4, 128
W = 8
EXT = BX + 2 * W
WIDE = BX + 2
PAIRS = WIDE * WIDE // 2
ROWS = PAIRS * 2 * CHANNELS
GROUP = 8
EARLY = 7
STORE = SLOTS + GROUP

Y_CONC, Y_POT, Y_EPS, Y_NUM, Y_END = 8, 14, 30, 46, 47
X_CONC, X_POT, X_EPS, X_NUM, X_END = 8, 14, 46, 78, 79
DY_FORCE, DY_END = WIDE * W, WIDE * W + 56
DX_AT = [sum(EXT - 2 - 2 * d for d in range(n)) for n in range(W + 1)]
DX_FORCE, DX_END = DX_AT[W], DX_AT[W] + 3 * BY

VMEM = pl.BlockSpec(memory_space=pltpu.VMEM)
SMEM = pl.BlockSpec(memory_space=pltpu.SMEM)
HBM = pl.BlockSpec(memory_space=pltpu.HBM)


def parity(axis):
    return lax.rem(lax.axis_index(axis), 2)


def swap(block, axis, odd):
    count = lax.axis_size(axis)
    route = [(i, (((i - odd) % count ^ 1) + odd) % count) for i in range(count)]
    return lax.ppermute(block, axis, route)


def hot_group(first, rec, cells):
    sub = lax.broadcasted_iota(jnp.int32, (16, NODES), 0)
    second = (sub >= 8).astype(F32)
    subf = sub.astype(F32)
    left, right = [], []
    for g in range(GROUP):
        cell, value = cells[first + g], rec[first + g]
        half = (cell >= PAIRS * NZ).astype(jnp.int32)
        high = ((cell - half * (PAIRS * NZ)) >> 7).astype(F32)
        low = ((cell & (NZ - 1)) + half * NZ).astype(F32)
        high = (jnp.broadcast_to(high, (16, NODES)) - second).astype(BF16)
        low = (jnp.broadcast_to(low, (16, NODES)) - subf).astype(BF16)
        lead = value.astype(BF16).astype(F32)
        rest = value - lead
        parts = jnp.concatenate([lead, rest, lead, rest], axis=0).astype(BF16)
        left.append(jnp.concatenate([jnp.where(high == BF16(2 * m), parts, BF16(0)) for m in range(ROWS // 16)], axis=0))
        right.append(jnp.concatenate([jnp.where(low == BF16(16 * m), BF16(1), BF16(0)) for m in range(16)], axis=0))
    left, right = jnp.concatenate(left, axis=1), jnp.concatenate(right, axis=1)
    sums = lax.dot_general(left, right, (((1,), (1,)), ((), ())), preferred_element_type=F32)
    return sums[:, :NZ], sums[:, NZ:]


def spread_groups(start, stop, rec, cells, acc):
    def group(c, _):
        left, right = hot_group(c * GROUP, rec, cells)
        acc[0] += left
        acc[1] += right
        return 0

    lax.fori_loop(start, stop, group, 0)


def number_in(tile):
    return jnp.max(tile).astype(jnp.int32)


def append(total, buf, number_tile, way, nodes, rec, cells):
    for k in range(MOVERS):
        rec[total + k] = buf[k // 2, (k % 2) * 4 : (k % 2) * 4 + 4]
        cells[total + k] = nodes[0, way, k : k + 1]
    return total + number_in(buf[number_tile])


def way_of(axis, odd):
    p = parity(axis)
    up = 1 - p if odd == 0 else p
    return up, (1 if axis == "gx" else 3) - up


def pack_records(out, rec, slots, number, way, number_tile):
    out[number_tile] = jnp.full((8, NZ), number.astype(F32))
    for k in range(MOVERS):
        row = rec[slots[0, way, k]]
        out[k // 2, (k % 2) * 4 : (k % 2) * 4 + 4] = jnp.where(k < number, row, 0.0)


def first_kernel(
    conc_h, pot_h, eps_h, rec_h, nodes_h, arrive_h, slots_h, counts_h, count,
    s1, s0, conc, pot, eps, arrive, xr, rows, cells, state,
    rec, nodes, slots, counts, gone, sems,
):
    copies = [(slots_h, slots), (counts_h, counts), (rec_h, rec), (nodes_h, nodes), (conc_h, conc)]
    for odd, out in enumerate((s0, s1)):
        start = pl.multiple_of(way_of("gy", odd)[0] * W, W)
        copies.append((pot_h.at[:, pl.ds(start, W)], out.at[pl.ds(Y_POT, BX)]))
        copies.append((eps_h.at[:, pl.ds(start, W)], out.at[pl.ds(Y_EPS, BX)]))
    copies += [(pot_h, pot), (eps_h, eps), (arrive_h, arrive)]
    copies = [pltpu.make_async_copy(a, b, sems.at[n]) for n, (a, b) in enumerate(copies)]
    for copy in copies:
        copy.start()

    def clear(c, _):
        gone[c] = 0
        return 0

    lax.fori_loop(0, SLOTS, clear, 0, unroll=16)
    for copy in copies[:2]:
        copy.wait()
    for way in range(4):

        def mark(k, _, way=way):
            gone[slots[0, way, k]] = 1
            return 0

        lax.fori_loop(0, counts[0, way], mark, 0)
    live = count[0]
    for copy in copies[2:]:
        copy.wait()

    def gather(c, found):
        rows[found] = rec[c]
        cells[found] = nodes[pl.ds(c, 1), :]
        stays = jnp.logical_and(c < live, gone[c] == 0)
        return found + stays.astype(jnp.int32)

    found = lax.fori_loop(0, SLOTS, gather, 0, unroll=16)
    state[...] = jnp.full((8, NZ), found.astype(F32))
    for odd in range(2):
        up, way = way_of("gx", odd)
        pack_records(xr.at[odd], rec, slots, counts[0, way], way, X_POT)
        xr[odd, X_CONC:X_POT] = conc[:, up * (BX - 1)].reshape(6, 8, NZ)
    for odd, out in enumerate((s0, s1)):
        up, way = way_of("gy", odd)
        pack_records(out, rec, slots, counts[0, way], way, Y_NUM)
        for s in range(3):
            face = jnp.where(up == 1, conc[s, :, BY - 1], conc[s, :, 0])
            out[Y_CONC + 2 * s : Y_CONC + 2 * s + 2] = face.reshape(2, 8, NZ)


def kept_kernel(rows, cells, state, state_out, acc):
    state_out[...] = state[...]
    acc[...] = jnp.zeros_like(acc)
    spread_groups(0, jnp.minimum(EARLY, number_in(state[...]) // GROUP), rows, cells, acc)


def pack_x_kernel(xr, pot, eps, y0, y1, state, s1, s0):
    del state
    px, py = parity("gx"), parity("gy")
    for n, (out, up) in enumerate(((s0, 1 - px), (s1, px))):
        out[0:X_POT] = xr[n, 0:X_POT]
        out[X_NUM] = xr[n, X_POT]
        for first, own, tile in ((X_POT, pot, Y_POT), (X_EPS, eps, Y_EPS)):
            own = own[pl.ds(up * W, W)]
            a, b = y0[pl.ds(tile + up * W, W)], y1[pl.ds(tile + up * W, W)]
            low, high = jnp.where(py == 1, a, b), jnp.where(py == 1, b, a)
            for x in range(W):
                out[first + 4 * x] = low[x]
                out[first + 4 * x + 1] = own[x, 0:8]
                out[first + 4 * x + 2] = own[x, 8:16]
                out[first + 4 * x + 3] = high[x]


def arrive_y_kernel(acc_in, rows_in, cells_in, state, y0, y1, nodes, rows, cells, state_out, acc, rec, cell):
    py = parity("gy")
    acc[...] = acc_in[...]
    rec[0:STORE] = rows_in[...]
    cell[0:STORE] = cells_in[...]
    found = number_in(state[...])
    total = append(found, y0, Y_NUM, 3 - py, nodes, rec, cell)
    total = append(total, y1, Y_NUM, 2 + py, nodes, rec, cell)
    done = total // GROUP
    spread_groups(jnp.minimum(EARLY, found // GROUP), done, rec, cell, acc)
    for g in range(GROUP):
        rows[g] = rec[done * GROUP + g]
        cells[g] = cell[done * GROUP + g]
    state_out[...] = jnp.full((8, NZ), (total - done * GROUP).astype(F32))


def face_flux(s, upper, lower, step):
    return -DIFFUSION[s] * ((upper - lower) + (VALENCE[s] * 0.5) * (upper + lower) * step)


def spread_rows(acc, channel, ex, first, number):
    half, row = divmod(ex, WIDE // 2)
    base = (row * WIDE + first) * 8 + channel
    return acc[half, pl.ds(base, number, stride=8)] + acc[half, pl.ds(base + 4, number, stride=8)]


def arrive_x_kernel(
    acc_in, rows, cells, state, x1, x0, y0, y1, nodes, conc, pot,
    conc_next, acc, dens, s1, s0,
    rec, cell, wide,
):
    px, py = parity("gx"), parity("gy")
    x_low_first, y_low_first = px == 1, py == 1
    acc[...] = acc_in[...]
    rec[0:GROUP] = rows[...]
    cell[0:GROUP] = cells[...]
    total = append(number_in(state[...]), x0, X_NUM, 1 - px, nodes, rec, cell)
    total = append(total, x1, X_NUM, px, nodes, rec, cell)
    for g in range(GROUP):
        rec[total + g] = jnp.zeros((CHANNELS, NODES), F32)
        cell[total + g] = jnp.zeros((1, NODES), jnp.int32)
    spread_groups(0, (total + GROUP - 1) // GROUP, rec, cell, acc)

    for f in range(4):
        wide[f, 1 : BX + 1, 8 : 8 + BY] = conc[f] if f < 3 else pot[...]
        if f < 3:
            xa, xb = (x[X_CONC + 2 * f : X_CONC + 2 * f + 2].reshape(BY, NZ) for x in (x0, x1))
            x_low, x_high = jnp.where(x_low_first, xa, xb), jnp.where(x_low_first, xb, xa)
            ya, yb = (y[Y_CONC + 2 * f : Y_CONC + 2 * f + 2].reshape(BX, NZ) for y in (y0, y1))
            y_low, y_high = jnp.where(y_low_first, ya, yb), jnp.where(y_low_first, yb, ya)
        else:
            last, first = X_POT + 4 * (W - 1) + 1, X_POT + 1
            x_low = jnp.where(x_low_first, x0[last : last + 2], x1[last : last + 2]).reshape(BY, NZ)
            x_high = jnp.where(x_low_first, x1[first : first + 2], x0[first : first + 2]).reshape(BY, NZ)
            y_low = jnp.where(y_low_first, y0[Y_POT:Y_EPS, 7], y1[Y_POT:Y_EPS, 7])
            y_high = jnp.where(y_low_first, y1[Y_POT:Y_EPS, 0], y0[Y_POT:Y_EPS, 0])
        wide[f, 0, 8 : 8 + BY] = x_low
        wide[f, BX + 1, 8 : 8 + BY] = x_high
        wide[f, 1 : BX + 1, 7] = y_low
        wide[f, 1 : BX + 1, 8 + BY] = y_high

    dens[...] = jnp.zeros_like(dens)
    for ex in range(WIDE):
        dens[ex, 7 : 7 + WIDE] = spread_rows(acc, 0, ex, 0, WIDE)

    before = [face_flux(s, wide[s, 1, 8:24], wide[s, 0, 8:24], wide[3, 1, 8:24] - wide[3, 0, 8:24]) for s in range(3)]
    for x in range(BX):
        pc, pe = wide[3, x + 1, 8:24], wide[3, x + 2, 8:24]
        pn, ps = wide[3, x + 1, 9:25], wide[3, x + 1, 7:23]
        pz = pltpu.roll(pc, NZ - 1, 1)
        dx, dn, ds, dz = pe - pc, pn - pc, pc - ps, pz - pc
        total = dens[x + 1, 8:24]
        for s in range(3):
            c = wide[s, x + 1, 8:24]
            flux_x = face_flux(s, wide[s, x + 2, 8:24], c, dx)
            flux_n = face_flux(s, wide[s, x + 1, 9:25], c, dn)
            flux_s = face_flux(s, c, wide[s, x + 1, 7:23], ds)
            flux_z = face_flux(s, pltpu.roll(c, NZ - 1, 1), c, dz)
            div = ((flux_x - before[s]) + (flux_n - flux_s)) + (flux_z - pltpu.roll(flux_z, 1, 1))
            before[s] = flux_x
            later = c - TIME_STEP * div
            conc_next[s, x] = later
            total = total + VALENCE[s] * later
        dens[x + 1, 8:24] = total

    for out, up in ((s0, 1 - py), (s1, py)):
        for ex in range(WIDE):
            out[ex * 8 : ex * 8 + 8] = jnp.where(up == 1, dens[ex, 17:25], dens[ex, 7:15])
        for a in range(3):
            for half in range(2):
                rims = []
                for ey in (0, WIDE - 1):
                    base = ey * 8 + a + 1
                    lead = acc[half, pl.ds(base, WIDE // 2, stride=WIDE * 8)]
                    rims.append(lead + acc[half, pl.ds(base + 4, WIDE // 2, stride=WIDE * 8)])
                r = DY_FORCE + a * WIDE + half * (WIDE // 2)
                out[r : r + WIDE // 2] = jnp.where(up == 1, rims[1], rims[0])
        out[DY_FORCE + 54 : DY_END] = jnp.zeros((2, NZ), F32)


def coefficient_kernel(acc, x0, x1, y0, y1, pot, eps, force, phi, xp, xm, yp, ym, zp, zm, inv, ew):
    px, py = parity("gx"), parity("gy")
    x_low_first, y_low_first = px == 1, py == 1
    for c in range(3):
        for ex in range(WIDE):
            force[c, ex] = spread_rows(acc, c + 1, ex, 1, BY)
    for buf, own, x_tile, y_tile in ((phi, pot, X_POT, Y_POT), (ew, eps, X_EPS, Y_EPS)):
        buf[W : W + BX, W : W + BY] = own[...]
        a, b = y0[y_tile : y_tile + BX], y1[y_tile : y_tile + BX]
        buf[W : W + BX, 0:W] = jnp.where(y_low_first, a, b)
        buf[W : W + BX, W + BY : EXT] = jnp.where(y_low_first, b, a)
        a, b = (x[x_tile : x_tile + 4 * W].reshape(W, EXT, NZ) for x in (x0, x1))
        buf[0:W] = jnp.where(x_low_first, a, b)
        buf[W + BX : EXT] = jnp.where(x_low_first, b, a)
    for x in range(1, EXT - 1):
        e = ew[x]
        up, down = e + ew[x + 1], e + ew[x - 1]
        north, south = e + pltpu.roll(e, EXT - 1, 0), e + pltpu.roll(e, 1, 0)
        over = e + pltpu.roll(e, NZ - 1, 1)
        under = pltpu.roll(over, 1, 1)
        scale = 1.0 / ((((up + down) + (north + south)) + (over + under)) + 2.0 * SCREENING)
        xp[x], xm[x] = up * scale, down * scale
        yp[x], ym[x] = north * scale, south * scale
        zp[x], zm[x] = over * scale, under * scale
        inv[x] = 2.0 * scale
    for buf in (xp, xm, yp, ym, zp, zm, inv):
        buf[0] = jnp.zeros((EXT, NZ), F32)
        buf[EXT - 1] = jnp.zeros((EXT, NZ), F32)


def join_y_kernel(dens, force, r0, r1, dext, fcore, s1, s0):
    px, py = parity("gx"), parity("gy")
    low_first = py == 1
    dext[0:7] = jnp.zeros((7, EXT, NZ), F32)
    dext[25:32] = jnp.zeros((7, EXT, NZ), F32)
    for ex in range(WIDE):
        dext[ex + 7] = dens[ex]
        a, b = r0[ex * 8 : ex * 8 + 8], r1[ex * 8 : ex * 8 + 8]
        dext[ex + 7, 1:9] += jnp.where(low_first, a, b)
        dext[ex + 7, 23:31] += jnp.where(low_first, b, a)
    fcore[...] = force[...]
    for c in range(3):
        r = DY_FORCE + c * WIDE
        a, b = r0[r : r + WIDE], r1[r : r + WIDE]
        fcore[c, :, 0] += jnp.where(low_first, a, b)
        fcore[c, :, BY - 1] += jnp.where(low_first, b, a)
    for out, up in ((s0, 1 - px), (s1, px)):
        for d in range(W):
            plane = jnp.where(up == 1, dext[24 - d, d + 1 : 31 - d], dext[7 + d, d + 1 : 31 - d])
            out[DX_AT[d] : DX_AT[d + 1]] = plane
        for c in range(3):
            out[DX_FORCE + c * BY : DX_FORCE + (c + 1) * BY] = fcore[c, up * (WIDE - 1)]


def sweep_kernel(dext, fcore, r1, r0, phi, xp, xm, yp, ym, zp, zm, inv, pot_next, force, phi_a, phi_b, rhs):
    low_first = parity("gx") == 1
    force[...] = fcore[:, 1 : BX + 1]
    a, b = (r[DX_FORCE:DX_END].reshape(3, BY, NZ) for r in (r0, r1))
    force[:, 0] += jnp.where(low_first, a, b)
    force[:, BX - 1] += jnp.where(low_first, b, a)

    rhs[1 : EXT - 1] = dext[1 : EXT - 1]
    for d in range(W):
        a, b = (r[DX_AT[d] : DX_AT[d + 1]] for r in (r0, r1))
        rhs[8 - d, d + 1 : 31 - d] += jnp.where(low_first, a, b)
        rhs[23 + d, d + 1 : 31 - d] += jnp.where(low_first, b, a)
    rhs[1 : EXT - 1] = rhs[1 : EXT - 1] * inv[1 : EXT - 1]

    for k in range(1, SWEEPS + 1):
        old = phi if k == 1 else (phi_a, phi_b)[k % 2]
        new = (phi_a, phi_b)[(k + 1) % 2]
        for x in range(k, EXT - k):
            if k < SWEEPS:
                f = slice(0, EXT)
                here = old[x]
                north, south = pltpu.roll(here, EXT - 1, 0), pltpu.roll(here, 1, 0)
            else:
                f = slice(W, W + BY)
                here = old[x, f]
                north, south = old[x, W + 1 : W + BY + 1], old[x, W - 1 : W + BY - 1]
            total = (xp[x, f] * old[x + 1, f] + xm[x, f] * old[x - 1, f]) + (yp[x, f] * north + ym[x, f] * south)
            total += (zp[x, f] * pltpu.roll(here, NZ - 1, 1) + zm[x, f] * pltpu.roll(here, 1, 1)) + rhs[x, f]
            if k < SWEEPS:
                new[x] = total
            else:
                pot_next[x - W] = total


def shape(*dims):
    return jax.ShapeDtypeStruct(dims, F32)


def call(kernel, name, ins, outs, scratch=(), flops=0):
    moved = 4 * sum(int(o.size) for o in outs)
    return pl.pallas_call(
        kernel,
        name=name,
        in_specs=ins,
        out_specs=[VMEM] * len(outs),
        out_shape=outs,
        scratch_shapes=scratch,
        compiler_params=pltpu.CompilerParams(vmem_limit_bytes=32 << 20),
        cost_estimate=pl.CostEstimate(flops=flops, bytes_accessed=moved, transcendentals=0),
    )


def body(conc, pot, eps, records, count, slots, counts, own_nodes, arrive_nodes):
    def store(number, kind=pltpu.VMEM):
        return [kind((number, CHANNELS, NODES), F32), kind((number, 1, NODES), jnp.int32)]

    sums = shape(2, ROWS, NZ)
    row_flops = 2 * ROWS * 2 * NZ * NODES
    field = shape(EXT, EXT, NZ)
    core = shape(BX, BY, NZ)

    ins = [pltpu.with_memory_space_constraint(x, pltpu.HBM) for x in (conc, pot, eps, records)]
    lists = [pltpu.with_memory_space_constraint(x, pltpu.HBM) for x in (slots, counts)]
    more = [pltpu.with_memory_space_constraint(x, pltpu.HBM) for x in (own_nodes, arrive_nodes)]
    small = [pltpu.SMEM((1, 4, MOVERS), jnp.int32), pltpu.SMEM((1, 4), jnp.int32)]
    rec = pltpu.VMEM((SLOTS, CHANNELS, NODES), F32)
    a1, a0, conc_v, pot_v, eps_v, arrive_v, xr, rows, cells, state = call(
        first_kernel,
        "first",
        [HBM] * 8 + [SMEM],
        [
            shape(Y_END, 8, NZ), shape(Y_END, 8, NZ), shape(3, BX, BY, NZ), core, core,
            jax.ShapeDtypeStruct((1, 4, MOVERS, NODES), jnp.int32),
            shape(2, X_POT + 1, 8, NZ), *store(STORE, jax.ShapeDtypeStruct), shape(8, NZ),
        ],
        [rec, pltpu.VMEM((SLOTS, NODES), jnp.int32), *small, pltpu.SMEM((SLOTS,), jnp.int32), pltpu.SemaphoreType.DMA((12,))],
    )(*ins, *more, *lists, count)
    y0, y1 = swap(a0, "gy", 0), swap(a1, "gy", 1)
    late, acc = call(kept_kernel, "spread_kept", [VMEM] * 3, [shape(8, NZ), sums], flops=row_flops * EARLY * GROUP)(
        rows, cells, state
    )
    b1, b0 = call(pack_x_kernel, "pack_x", [VMEM] * 6, [shape(X_END, 8, NZ)] * 2)(xr, pot_v, eps_v, y0, y1, late)
    x1, x0 = swap(b1, "gx", 1), swap(b0, "gx", 0)
    rows, cells, state, acc = call(
        arrive_y_kernel,
        "spread_y",
        [VMEM] * 7,
        [*store(GROUP, jax.ShapeDtypeStruct), shape(8, NZ), sums],
        store(STORE + 2 * MOVERS + GROUP),
        flops=row_flops * 48,
    )(acc, rows, cells, state, y0, y1, arrive_v)
    conc_next, acc, dens, c1, c0 = call(
        arrive_x_kernel,
        "spread_x",
        [VMEM] * 11,
        [shape(3, BX, BY, NZ), sums, shape(WIDE, EXT, NZ), shape(DY_END, NZ), shape(DY_END, NZ)],
        store(2 * MOVERS + 2 * GROUP) + [pltpu.VMEM((4, WIDE, 32, NZ), F32)],
        flops=row_flops * 2 * MOVERS,
    )(acc, rows, cells, state, x1, x0, y0, y1, arrive_v, conc_v, pot_v)
    r0, r1 = swap(c0, "gy", 0), swap(c1, "gy", 1)
    force, phi, *weights = call(
        coefficient_kernel,
        "coefficients",
        [VMEM] * 7,
        [shape(3, WIDE, BY, NZ)] + [field] * 8,
        [pltpu.VMEM((EXT, EXT, NZ), F32)],
        flops=row_flops * 8,
    )(acc, x0, x1, y0, y1, pot_v, eps_v)
    dext, fcore, e1, e0 = call(
        join_y_kernel, "join_y", [VMEM] * 4, [field, shape(3, WIDE, BY, NZ), shape(DX_END, NZ), shape(DX_END, NZ)]
    )(dens, force, r0, r1)
    g1, g0 = swap(e1, "gx", 1), swap(e0, "gx", 0)
    pot_next, body_force = call(
        sweep_kernel,
        "sweeps",
        [VMEM] * 12,
        [core, shape(3, BX, BY, NZ)],
        [pltpu.VMEM((EXT, EXT, NZ), F32)] * 3,
        flops=20 * SWEEPS * EXT * EXT * NZ,
    )(dext, fcore, g1, g0, phi, *weights)
    return conc_next, pot_next, body_force


def solution(mesh):
    placed = (
        P(None, "gx", "gy", None),
        P("gx", "gy", None),
        P("gx", "gy", None),
        P(("gx", "gy"), None, None),
        P(("gx", "gy")),
        P(("gx", "gy"), None, None),
        P(("gx", "gy"), None),
        P(("gx", "gy"), None),
        P(("gx", "gy"), None, None, None),
    )
    return jax.shard_map(
        body,
        mesh=mesh,
        in_specs=placed,
        out_specs=(P(None, "gx", "gy", None), P("gx", "gy", None), P(None, "gx", "gy", None)),
        check_vma=False,
    )
```

```python
import jax
import jax.numpy as jnp
from jax import lax
from jax.experimental import pallas as pl
from jax.experimental.pallas import tpu as pltpu
from jax.sharding import PartitionSpec as P

SWEEPS = 8
DIFFUSION = (1.0, 0.7, 0.45)
VALENCE = (1.0, -1.0, 2.0)
TIME_STEP = 0.05
SCREENING = 0.05

F32 = jnp.float32
BF16 = jnp.bfloat16
BX, BY, NZ = 16, 16, 128
SLOTS, MOVERS, CHANNELS, NODES = 128, 16, 4, 128
W = 8
EXT = BX + 2 * W
WIDE = BX + 2
PAIRS = WIDE * WIDE // 2
ROWS = PAIRS * 2 * CHANNELS
GROUP = 8
EARLY = 7
STORE = SLOTS + GROUP

Y_CONC, Y_POT, Y_EPS, Y_NUM, Y_END = 8, 14, 30, 46, 47
X_CONC, X_POT, X_EPS, X_NUM, X_END = 8, 14, 46, 78, 79
DY_FORCE, DY_END = WIDE * W, WIDE * W + 56
DX_AT = [sum(EXT - 2 - 2 * d for d in range(n)) for n in range(W + 1)]
DX_FORCE, DX_END = DX_AT[W], DX_AT[W] + 3 * BY

VMEM = pl.BlockSpec(memory_space=pltpu.VMEM)
SMEM = pl.BlockSpec(memory_space=pltpu.SMEM)
HBM = pl.BlockSpec(memory_space=pltpu.HBM)


def parity(axis):
    return lax.rem(lax.axis_index(axis), 2)


def swap(block, axis, odd):
    count = lax.axis_size(axis)
    route = [(i, (((i - odd) % count ^ 1) + odd) % count) for i in range(count)]
    return lax.ppermute(block, axis, route)


def chip_pair(block):
    pairs = [[i, i + 1] for i in range(0, lax.axis_size("gx"), 2)]
    return lax.all_gather(block, "gx", axis_index_groups=pairs)


def hot_group(first, number, rec, cells):
    sub = lax.broadcasted_iota(jnp.int32, (16, NODES), 0)
    second = (sub >= 8).astype(F32)
    subf = sub.astype(F32)
    left, right = [], []
    for g in range(number):
        cell, value = cells[first + g], rec[first + g]
        half = (cell >= PAIRS * NZ).astype(jnp.int32)
        high = ((cell - half * (PAIRS * NZ)) >> 7).astype(F32)
        low = ((cell & (NZ - 1)) + half * NZ).astype(F32)
        high = (jnp.broadcast_to(high, (16, NODES)) - second).astype(BF16)
        low = (jnp.broadcast_to(low, (16, NODES)) - subf).astype(BF16)
        lead = value.astype(BF16).astype(F32)
        rest = value - lead
        parts = jnp.concatenate([lead, rest, lead, rest], axis=0).astype(BF16)
        left.append(jnp.concatenate([jnp.where(high == BF16(2 * m), parts, BF16(0)) for m in range(ROWS // 16)], axis=0))
        right.append(jnp.concatenate([jnp.where(low == BF16(16 * m), BF16(1), BF16(0)) for m in range(16)], axis=0))
    left, right = jnp.concatenate(left, axis=1), jnp.concatenate(right, axis=1)
    sums = lax.dot_general(left, right, (((1,), (1,)), ((), ())), preferred_element_type=F32)
    return sums[:, :NZ], sums[:, NZ:]


def spread_groups(start, stop, rec, cells, acc):
    def groups(number):
        def group(c, first):
            left, right = hot_group(first, number, rec, cells)
            acc[0] += left
            acc[1] += right
            return first + number

        return group

    count = stop - start
    first = lax.fori_loop(0, count // 2, groups(2 * GROUP), start * GROUP)
    lax.fori_loop(0, lax.rem(count, 2), groups(GROUP), first)


def mirrored(px, low, high):
    return jnp.where(px == 1, high, low)


def number_in(tile):
    return jnp.max(tile).astype(jnp.int32)


def append(total, buf, number_tile, way, nodes, rec, cells):
    for k in range(MOVERS):
        rec[total + k] = buf[k // 2, (k % 2) * 4 : (k % 2) * 4 + 4]
        cells[total + k] = nodes[0, way, k : k + 1]
    return total + number_in(buf[number_tile])


def way_of(axis, odd):
    p = parity(axis)
    up = 1 - p if odd == 0 else p
    return up, (1 if axis == "gx" else 3) - up


def pack_records(out, rec, slots, number, way, number_tile):
    out[number_tile] = jnp.full((8, NZ), number.astype(F32))
    for k in range(MOVERS):
        row = rec[slots[0, way, k]]
        out[k // 2, (k % 2) * 4 : (k % 2) * 4 + 4] = jnp.where(k < number, row, 0.0)


def first_kernel(
    conc_h, pot_h, eps_h, rec_h, nodes_h, arrive_h, slots_h, counts_h, count,
    s1, s0, conc, pot, eps, arrive, xr, rows, cells, state,
    rec, nodes, slots, counts, gone, sems,
):
    copies = [(slots_h, slots), (counts_h, counts), (rec_h, rec), (nodes_h, nodes), (conc_h, conc)]
    for odd, out in enumerate((s0, s1)):
        start = pl.multiple_of(way_of("gy", odd)[0] * W, W)
        copies.append((pot_h.at[:, pl.ds(start, W)], out.at[pl.ds(Y_POT, BX)]))
        copies.append((eps_h.at[:, pl.ds(start, W)], out.at[pl.ds(Y_EPS, BX)]))
    copies += [(pot_h, pot), (eps_h, eps), (arrive_h, arrive)]
    copies = [pltpu.make_async_copy(a, b, sems.at[n]) for n, (a, b) in enumerate(copies)]
    for copy in copies:
        copy.start()

    def clear(c, _):
        gone[c] = 0
        return 0

    lax.fori_loop(0, SLOTS, clear, 0, unroll=16)
    for copy in copies[:2]:
        copy.wait()
    for way in range(4):

        def mark(k, _, way=way):
            gone[slots[0, way, k]] = 1
            return 0

        lax.fori_loop(0, counts[0, way], mark, 0)
    live = count[0]
    for copy in copies[2:]:
        copy.wait()

    def gather(c, found):
        rows[found] = rec[c]
        cells[found] = nodes[pl.ds(c, 1), :]
        stays = jnp.logical_and(c < live, gone[c] == 0)
        return found + stays.astype(jnp.int32)

    found = lax.fori_loop(0, SLOTS, gather, 0, unroll=16)
    state[...] = jnp.full((8, NZ), found.astype(F32))
    for odd in range(2):
        up, way = way_of("gx", odd)
        pack_records(xr.at[odd], rec, slots, counts[0, way], way, X_POT)
        xr[odd, X_CONC:X_POT] = conc[:, up * (BX - 1)].reshape(6, 8, NZ)
    for odd, out in enumerate((s0, s1)):
        up, way = way_of("gy", odd)
        pack_records(out, rec, slots, counts[0, way], way, Y_NUM)
        for s in range(3):
            face = jnp.where(up == 1, conc[s, :, BY - 1], conc[s, :, 0])
            out[Y_CONC + 2 * s : Y_CONC + 2 * s + 2] = face.reshape(2, 8, NZ)


def kept_kernel(rows, cells, state, state_out, acc):
    state_out[...] = state[...]
    acc[...] = jnp.zeros_like(acc)
    spread_groups(0, jnp.minimum(EARLY, number_in(state[...]) // GROUP), rows, cells, acc)


def pack_x_kernel(xr, pot, eps, y1, y0, state, s1, s0):
    del state
    px, py = parity("gx"), parity("gy")
    for n, (out, up) in enumerate(((s0, 1 - px), (s1, px))):
        out[0:X_POT] = xr[n, 0:X_POT]
        out[X_NUM] = xr[n, X_POT]
        for first, own, tile in ((X_POT, pot, Y_POT), (X_EPS, eps, Y_EPS)):
            own = own[pl.ds(up * W, W)]
            a, b = y0[pl.ds(tile + up * W, W)], y1[pl.ds(tile + up * W, W)]
            low, high = jnp.where(py == 1, a, b), jnp.where(py == 1, b, a)
            for x in range(W):
                out[first + 4 * x] = low[x]
                out[first + 4 * x + 1] = own[x, 0:8]
                out[first + 4 * x + 2] = own[x, 8:16]
                out[first + 4 * x + 3] = high[x]


def arrive_y_kernel(acc_in, rows_in, cells_in, state, y0, y1, nodes, rows, cells, state_out, acc, rec, cell):
    py = parity("gy")
    del acc_in
    rec[0:STORE] = rows_in[...]
    cell[0:STORE] = cells_in[...]
    found = number_in(state[...])
    total = append(found, y0, Y_NUM, 3 - py, nodes, rec, cell)
    total = append(total, y1, Y_NUM, 2 + py, nodes, rec, cell)
    done = total // GROUP
    spread_groups(jnp.minimum(EARLY, found // GROUP), done, rec, cell, acc)
    for g in range(GROUP):
        rows[g] = rec[done * GROUP + g]
        cells[g] = cell[done * GROUP + g]
    state_out[...] = jnp.full((8, NZ), (total - done * GROUP).astype(F32))


def face_flux(s, upper, lower, step):
    return -DIFFUSION[s] * ((upper - lower) + (VALENCE[s] * 0.5) * (upper + lower) * step)


def spread_rows(acc, channel, ex, first, number):
    half, row = divmod(ex, WIDE // 2)
    base = (row * WIDE + first) * 8 + channel
    return acc[half, pl.ds(base, number, stride=8)] + acc[half, pl.ds(base + 4, number, stride=8)]


def arrive_x_kernel(
    acc_in, rows, cells, state, x1, x0, y0, y1, nodes, conc, pot,
    conc_next, acc, dens, s1, s0,
    rec, cell, wide,
):
    px, py = parity("gx"), parity("gy")
    x_low_first, y_low_first = px == 1, py == 1
    del acc_in
    rec[0:GROUP] = rows[...]
    cell[0:GROUP] = cells[...]
    total = append(number_in(state[...]), x0, X_NUM, 1 - px, nodes, rec, cell)
    total = append(total, x1, X_NUM, px, nodes, rec, cell)
    for g in range(GROUP):
        rec[total + g] = jnp.zeros((CHANNELS, NODES), F32)
        cell[total + g] = jnp.zeros((1, NODES), jnp.int32)
    spread_groups(0, (total + GROUP - 1) // GROUP, rec, cell, acc)

    for f in range(4):
        wide[f, 1 : BX + 1, 8 : 8 + BY] = conc[f] if f < 3 else pot[...]
        if f < 3:
            xa, xb = (x[X_CONC + 2 * f : X_CONC + 2 * f + 2].reshape(BY, NZ) for x in (x0, x1))
            x_low, x_high = jnp.where(x_low_first, xa, xb), jnp.where(x_low_first, xb, xa)
            ya, yb = (y[Y_CONC + 2 * f : Y_CONC + 2 * f + 2].reshape(BX, NZ) for y in (y0, y1))
            y_low, y_high = jnp.where(y_low_first, ya, yb), jnp.where(y_low_first, yb, ya)
        else:
            last, first = X_POT + 4 * (W - 1) + 1, X_POT + 1
            x_low = jnp.where(x_low_first, x0[last : last + 2], x1[last : last + 2]).reshape(BY, NZ)
            x_high = jnp.where(x_low_first, x1[first : first + 2], x0[first : first + 2]).reshape(BY, NZ)
            y_low = jnp.where(y_low_first, y0[Y_POT:Y_EPS, 7], y1[Y_POT:Y_EPS, 7])
            y_high = jnp.where(y_low_first, y1[Y_POT:Y_EPS, 0], y0[Y_POT:Y_EPS, 0])
        wide[f, 0, 8 : 8 + BY] = x_low
        wide[f, BX + 1, 8 : 8 + BY] = x_high
        wide[f, 1 : BX + 1, 7] = y_low
        wide[f, 1 : BX + 1, 8 + BY] = y_high

    dens[...] = jnp.zeros_like(dens)
    for ex in range(WIDE):
        dens[ex, 7 : 7 + WIDE] = spread_rows(acc, 0, ex, 0, WIDE)

    before = [face_flux(s, wide[s, 1, 8:24], wide[s, 0, 8:24], wide[3, 1, 8:24] - wide[3, 0, 8:24]) for s in range(3)]
    for x in range(BX):
        pc, pe = wide[3, x + 1, 8:24], wide[3, x + 2, 8:24]
        pn, ps = wide[3, x + 1, 9:25], wide[3, x + 1, 7:23]
        pz = pltpu.roll(pc, NZ - 1, 1)
        dx, dn, ds, dz = pe - pc, pn - pc, pc - ps, pz - pc
        total = dens[x + 1, 8:24]
        for s in range(3):
            c = wide[s, x + 1, 8:24]
            flux_x = face_flux(s, wide[s, x + 2, 8:24], c, dx)
            flux_n = face_flux(s, wide[s, x + 1, 9:25], c, dn)
            flux_s = face_flux(s, c, wide[s, x + 1, 7:23], ds)
            flux_z = face_flux(s, pltpu.roll(c, NZ - 1, 1), c, dz)
            div = ((flux_x - before[s]) + (flux_n - flux_s)) + (flux_z - pltpu.roll(flux_z, 1, 1))
            before[s] = flux_x
            later = c - TIME_STEP * div
            conc_next[s, x] = later
            total = total + VALENCE[s] * later
        dens[x + 1, 8:24] = total

    for out, up in ((s0, 1 - py), (s1, py)):
        for ex in range(WIDE):
            out[ex * 8 : ex * 8 + 8] = jnp.where(up == 1, dens[ex, 17:25], dens[ex, 7:15])
        for a in range(3):
            for half in range(2):
                rims = []
                for ey in (0, WIDE - 1):
                    base = ey * 8 + a + 1
                    lead = acc[half, pl.ds(base, WIDE // 2, stride=WIDE * 8)]
                    rims.append(lead + acc[half, pl.ds(base + 4, WIDE // 2, stride=WIDE * 8)])
                r = DY_FORCE + a * WIDE + half * (WIDE // 2)
                out[r : r + WIDE // 2] = jnp.where(up == 1, rims[1], rims[0])
        out[DY_FORCE + 54 : DY_END] = jnp.zeros((2, NZ), F32)


def coefficient_kernel(acc, x0, x1, y0, y1, pot, eps, force, phi, xp, xm, yp, ym, zp, zm, inv, ew):
    px, y_low_first = parity("gx"), parity("gy") == 1
    for c in range(3):
        for ex in range(WIDE):
            force[c, ex] = spread_rows(acc, c + 1, ex, 1, BY)
    for buf, own, x_tile, y_tile in ((phi, pot, X_POT, Y_POT), (ew, eps, X_EPS, Y_EPS)):
        for n in range(BX):
            x = mirrored(px, n, BX - 1 - n)
            a, b = y0[y_tile + x], y1[y_tile + x]
            buf[W + n, 0:W] = jnp.where(y_low_first, a, b)
            buf[W + n, W : W + BY] = own[x]
            buf[W + n, W + BY : EXT] = jnp.where(y_low_first, b, a)
        for n in range(W):
            at = pl.ds(x_tile + 4 * mirrored(px, n, W - 1 - n), 4)
            buf[n] = x1[at].reshape(EXT, NZ)
            buf[W + BX + n] = x0[at].reshape(EXT, NZ)
    for x in range(1, EXT - 1):
        e = ew[x]
        up, down = e + ew[x + 1], e + ew[x - 1]
        north, south = e + pltpu.roll(e, EXT - 1, 0), e + pltpu.roll(e, 1, 0)
        over = e + pltpu.roll(e, NZ - 1, 1)
        under = pltpu.roll(over, 1, 1)
        scale = 1.0 / ((((up + down) + (north + south)) + (over + under)) + 2.0 * SCREENING)
        xp[x], xm[x] = up * scale, down * scale
        yp[x], ym[x] = north * scale, south * scale
        zp[x], zm[x] = over * scale, under * scale
        inv[x] = 2.0 * scale
    for buf in (xp, xm, yp, ym, zp, zm, inv):
        buf[0] = jnp.zeros((EXT, NZ), F32)
        buf[EXT - 1] = jnp.zeros((EXT, NZ), F32)


def join_y_kernel(dens, force, r1, r0, dext, fcore, s1, s0):
    px, py = parity("gx"), parity("gy")
    low_first = py == 1
    dext[0:7] = jnp.zeros((7, EXT, NZ), F32)
    dext[25:32] = jnp.zeros((7, EXT, NZ), F32)
    for n in range(WIDE):
        ex = mirrored(px, n, WIDE - 1 - n)
        dext[n + 7] = dens[ex]
        at = pl.ds(pl.multiple_of(ex * 8, 8), 8)
        a, b = r0[at], r1[at]
        dext[n + 7, 1:9] += jnp.where(low_first, a, b)
        dext[n + 7, 23:31] += jnp.where(low_first, b, a)
    fcore[...] = force[...]
    for c in range(3):
        r = DY_FORCE + c * WIDE
        a, b = r0[r : r + WIDE], r1[r : r + WIDE]
        fcore[c, :, 0] += jnp.where(low_first, a, b)
        fcore[c, :, BY - 1] += jnp.where(low_first, b, a)
    pack_rims(dext, fcore, s1, px, 7, 1)
    pack_rims(dext, fcore, s0, 1 - px, 24, -1)


def pack_rims(dext, fcore, out, up, first, way):
    for d in range(W):
        out[DX_AT[d] : DX_AT[d + 1]] = dext[first + way * d, d + 1 : 31 - d]
    for c in range(3):
        out[DX_FORCE + c * BY : DX_FORCE + (c + 1) * BY] = fcore[c, up * (WIDE - 1)]


def sweep_plane(k, x, west, here, east, weights, rhs):
    xp, xm, yp, ym, zp, zm = weights
    if k < SWEEPS:
        f = slice(0, EXT)
        north, south = pltpu.roll(here[...], EXT - 1, 0), pltpu.roll(here[...], 1, 0)
    else:
        f = slice(W, W + BY)
        north, south = here[W + 1 : W + BY + 1], here[W - 1 : W + BY - 1]
    centre = here[f]
    total = (xp[x, f] * east[f] + xm[x, f] * west[f]) + (yp[x, f] * north + ym[x, f] * south)
    return total + ((zp[x, f] * pltpu.roll(centre, NZ - 1, 1) + zm[x, f] * pltpu.roll(centre, 1, 1)) + rhs[x, f])


def near_kernel(dext, r0, phi, xp, xm, yp, ym, zp, zm, inv, near, edges, phi_a, phi_b, rhs):
    weights, other = (xp, xm, yp, ym, zp, zm), 1 - parity("gx")
    rhs[9 : EXT - 1] = dext[9 : EXT - 1]
    for d in range(W):
        rhs[23 + d, d + 1 : 31 - d] += r0[other, DX_AT[d] : DX_AT[d + 1]]
    rhs[9 : EXT - 1] = rhs[9 : EXT - 1] * inv[9 : EXT - 1]
    for k in range(1, SWEEPS + 1):
        old = phi if k == 1 else (phi_a, phi_b)[k % 2]
        new = (phi_a, phi_b)[(k + 1) % 2]
        for x in range(W + k, EXT - k):
            total = sweep_plane(k, x, old.at[x - 1], old.at[x], old.at[x + 1], weights, rhs)
            if k == SWEEPS:
                near[x - 16] = total
                continue
            new[x] = total
            if x < W + k + 2:
                edges[2 * k - 2 + x - W - k] = total


def far_kernel(dext, r1, r0, fcore, phi, xp, xm, yp, ym, zp, zm, inv, near, edges, pot_next, force, phi_a, phi_b, rhs):
    px = parity("gx")
    weights = (xp, xm, yp, ym, zp, zm)
    rhs[1:16] = dext[1:16]
    for d in range(W):
        rhs[8 - d, d + 1 : 31 - d] += r1[DX_AT[d] : DX_AT[d + 1]]
    rhs[1:16] = rhs[1:16] * inv[1:16]

    def plane(k, x):
        if k == 0:
            return phi.at[x]
        return edges.at[2 * k - 2 + x - W - k] if x >= W + k else (phi_a, phi_b)[(k + 1) % 2].at[x]

    for k in range(1, SWEEPS + 1):
        for x in range(k, W + k):
            total = sweep_plane(k, x, plane(k - 1, x - 1), plane(k - 1, x), plane(k - 1, x + 1), weights, rhs)
            if k < SWEEPS:
                plane(k, x)[...] = total
            else:
                pot_next[mirrored(px, x - W, 23 - x)] = total
    for x in range(16, 24):
        pot_next[mirrored(px, x - W, 23 - x)] = near[x - 16]

    low_first = px == 1
    force[...] = fcore[:, 1 : BX + 1]
    a, b = (r[DX_FORCE:DX_END].reshape(3, BY, NZ) for r in (r0.at[1 - px], r1))
    force[:, 0] += jnp.where(low_first, a, b)
    force[:, BX - 1] += jnp.where(low_first, b, a)


def shape(*dims):
    return jax.ShapeDtypeStruct(dims, F32)


def call(kernel, name, ins, outs, scratch=(), flops=0, aliases=None):
    moved = 4 * sum(int(o.size) for o in outs)
    return pl.pallas_call(
        kernel,
        name=name,
        in_specs=ins,
        out_specs=[VMEM] * len(outs),
        out_shape=outs,
        scratch_shapes=scratch,
        input_output_aliases=aliases or {},
        compiler_params=pltpu.CompilerParams(vmem_limit_bytes=32 << 20),
        cost_estimate=pl.CostEstimate(flops=flops, bytes_accessed=moved, transcendentals=0),
    )


def body(conc, pot, eps, records, count, slots, counts, own_nodes, arrive_nodes):
    def store(number, kind=pltpu.VMEM):
        return [kind((number, CHANNELS, NODES), F32), kind((number, 1, NODES), jnp.int32)]

    sums = shape(2, ROWS, NZ)
    row_flops = 2 * ROWS * 2 * NZ * NODES
    field = shape(EXT, EXT, NZ)
    core = shape(BX, BY, NZ)

    ins = [pltpu.with_memory_space_constraint(x, pltpu.HBM) for x in (conc, pot, eps, records)]
    lists = [pltpu.with_memory_space_constraint(x, pltpu.HBM) for x in (slots, counts)]
    more = [pltpu.with_memory_space_constraint(x, pltpu.HBM) for x in (own_nodes, arrive_nodes)]
    small = [pltpu.SMEM((1, 4, MOVERS), jnp.int32), pltpu.SMEM((1, 4), jnp.int32)]
    rec = pltpu.VMEM((SLOTS, CHANNELS, NODES), F32)
    a1, a0, conc_v, pot_v, eps_v, arrive_v, xr, rows, cells, state = call(
        first_kernel,
        "first",
        [HBM] * 8 + [SMEM],
        [
            shape(Y_END, 8, NZ), shape(Y_END, 8, NZ), shape(3, BX, BY, NZ), core, core,
            jax.ShapeDtypeStruct((1, 4, MOVERS, NODES), jnp.int32),
            shape(2, X_POT + 1, 8, NZ), *store(STORE, jax.ShapeDtypeStruct), shape(8, NZ),
        ],
        [rec, pltpu.VMEM((SLOTS, NODES), jnp.int32), *small, pltpu.SMEM((SLOTS,), jnp.int32), pltpu.SemaphoreType.DMA((12,))],
    )(*ins, *more, *lists, count)
    y0, y1 = swap(a0, "gy", 0), swap(a1, "gy", 1)
    late, acc = call(kept_kernel, "spread_kept", [VMEM] * 3, [shape(8, NZ), sums], flops=row_flops * EARLY * GROUP)(
        rows, cells, state
    )
    b1, b0 = call(pack_x_kernel, "pack_x", [VMEM] * 6, [shape(X_END, 8, NZ)] * 2)(xr, pot_v, eps_v, y1, y0, late)
    x1, x0 = swap(b1, "gx", 1), swap(b0, "gx", 0)
    rows, cells, state, acc = call(
        arrive_y_kernel,
        "spread_y",
        [VMEM] * 7,
        [*store(GROUP, jax.ShapeDtypeStruct), shape(8, NZ), sums],
        store(STORE + 2 * MOVERS + GROUP),
        flops=row_flops * 48,
        aliases={0: 3},
    )(acc, rows, cells, state, y0, y1, arrive_v)
    conc_next, acc, dens, c1, c0 = call(
        arrive_x_kernel,
        "spread_x",
        [VMEM] * 11,
        [shape(3, BX, BY, NZ), sums, shape(WIDE, EXT, NZ), shape(DY_END, NZ), shape(DY_END, NZ)],
        store(2 * MOVERS + 2 * GROUP) + [pltpu.VMEM((4, WIDE, 32, NZ), F32)],
        flops=row_flops * 2 * MOVERS,
        aliases={0: 1},
    )(acc, rows, cells, state, x1, x0, y0, y1, arrive_v, conc_v, pot_v)
    r0, r1 = swap(c0, "gy", 0), swap(c1, "gy", 1)
    force, phi, *weights = call(
        coefficient_kernel,
        "coefficients",
        [VMEM] * 7,
        [shape(3, WIDE, BY, NZ)] + [field] * 8,
        [pltpu.VMEM((EXT, EXT, NZ), F32)],
        flops=row_flops * 8,
    )(acc, x0, x1, y0, y1, pot_v, eps_v)
    dext, fcore, e1, e0 = call(
        join_y_kernel, "join_y", [VMEM] * 4, [field, shape(3, WIDE, BY, NZ), shape(DX_END, NZ), shape(DX_END, NZ)]
    )(dens, force, r1, r0)
    g1, g0 = swap(e1, "gx", 1), chip_pair(e0)
    scratch = [pltpu.VMEM((EXT, EXT, NZ), F32)] * 3
    near, edges = call(
        near_kernel,
        "sweeps_near",
        [VMEM] * 10,
        [shape(BX // 2, BY, NZ), shape(2 * SWEEPS - 2, EXT, NZ)],
        scratch,
        flops=12 * SWEEPS * EXT * EXT * NZ,
    )(dext, g0, phi, *weights)
    pot_next, body_force = call(
        far_kernel,
        "sweeps_far",
        [VMEM] * 14,
        [core, shape(3, BX, BY, NZ)],
        scratch,
        flops=8 * SWEEPS * EXT * EXT * NZ,
    )(dext, g1, g0, fcore, phi, *weights, near, edges)
    return conc_next, pot_next, body_force


def solution(mesh):
    placed = (
        P(None, "gx", "gy", None),
        P("gx", "gy", None),
        P("gx", "gy", None),
        P(("gx", "gy"), None, None),
        P(("gx", "gy")),
        P(("gx", "gy"), None, None),
        P(("gx", "gy"), None),
        P(("gx", "gy"), None),
        P(("gx", "gy"), None, None, None),
    )
    return jax.shard_map(
        body,
        mesh=mesh,
        in_specs=placed,
        out_specs=(P(None, "gx", "gy", None), P("gx", "gy", None), P(None, "gx", "gy", None)),
        check_vma=False,
    )
```

```python
import jax
import jax.numpy as jnp
from jax import lax
from jax.experimental import pallas as pl
from jax.experimental.pallas import tpu as pltpu
from jax.sharding import PartitionSpec as P

SWEEPS = 8
DIFFUSION = (1.0, 0.7, 0.45)
VALENCE = (1.0, -1.0, 2.0)
TIME_STEP = 0.05
SCREENING = 0.05

F32 = jnp.float32
BF16 = jnp.bfloat16
BX, BY, NZ = 16, 16, 128
SLOTS, MOVERS, CHANNELS, NODES = 128, 16, 4, 128
W = 8
EXT = BX + 2 * W
WIDE = BX + 2
PAIRS = WIDE * WIDE // 2
ROWS = PAIRS * 2 * CHANNELS
GROUP = 8
EARLY = 9
STORE = SLOTS + GROUP

Y_CONC, Y_POT, Y_EPS, Y_NUM, Y_END = 8, 14, 30, 46, 47
X_CONC, X_POT, X_EPS, X_NUM, X_END = 8, 14, 46, 78, 79
DY_FORCE, DY_END = WIDE * W, WIDE * W + 56
DX_AT = [sum(EXT - 2 - 2 * d for d in range(n)) for n in range(W + 1)]
DX_FORCE, DX_END = DX_AT[W], DX_AT[W] + 3 * BY

VMEM = pl.BlockSpec(memory_space=pltpu.VMEM)
SMEM = pl.BlockSpec(memory_space=pltpu.SMEM)
HBM = pl.BlockSpec(memory_space=pltpu.HBM)


def parity(axis):
    return lax.rem(lax.axis_index(axis), 2)


def swap(block, axis, odd):
    count = lax.axis_size(axis)
    route = [(i, (((i - odd) % count ^ 1) + odd) % count) for i in range(count)]
    return lax.ppermute(block, axis, route)


def chip_pair(block):
    pairs = [[i, i + 1] for i in range(0, lax.axis_size("gx"), 2)]
    return lax.all_gather(block, "gx", axis_index_groups=pairs)


def hot_group(first, number, rec, cells):
    sub = lax.broadcasted_iota(jnp.int32, (16, NODES), 0)
    second = (sub >= 8).astype(F32)
    subf = sub.astype(F32)
    left, right = [], []
    for g in range(number):
        cell, value = cells[first + g], rec[first + g]
        half = (cell >= PAIRS * NZ).astype(jnp.int32)
        high = ((cell - half * (PAIRS * NZ)) >> 7).astype(F32)
        low = ((cell & (NZ - 1)) + half * NZ).astype(F32)
        high = (jnp.broadcast_to(high, (16, NODES)) - second).astype(BF16)
        low = (jnp.broadcast_to(low, (16, NODES)) - subf).astype(BF16)
        lead = value.astype(BF16).astype(F32)
        rest = value - lead
        parts = jnp.concatenate([lead, rest, lead, rest], axis=0).astype(BF16)
        left.append(jnp.concatenate([jnp.where(high == BF16(2 * m), parts, BF16(0)) for m in range(ROWS // 16)], axis=0))
        right.append(jnp.concatenate([jnp.where(low == BF16(16 * m), BF16(1), BF16(0)) for m in range(16)], axis=0))
    left, right = jnp.concatenate(left, axis=1), jnp.concatenate(right, axis=1)
    sums = lax.dot_general(left, right, (((1,), (1,)), ((), ())), preferred_element_type=F32)
    return sums[:, :NZ], sums[:, NZ:]


def spread_groups(start, stop, rec, cells, acc):
    def groups(number):
        def group(c, first):
            left, right = hot_group(first, number, rec, cells)
            acc[0] += left
            acc[1] += right
            return first + number

        return group

    count = stop - start
    first = lax.fori_loop(0, count // 2, groups(2 * GROUP), start * GROUP)
    lax.fori_loop(0, lax.rem(count, 2), groups(GROUP), first)


def mirrored(px, low, high):
    return jnp.where(px == 1, high, low)


def number_in(tile):
    return jnp.max(tile).astype(jnp.int32)


def append(total, buf, number_tile, way, nodes, rec, cells):
    for k in range(MOVERS):
        rec[total + k] = buf[k // 2, (k % 2) * 4 : (k % 2) * 4 + 4]
        cells[total + k] = nodes[0, way, k : k + 1]
    return total + number_in(buf[number_tile])


def way_of(axis, odd):
    p = parity(axis)
    up = 1 - p if odd == 0 else p
    return up, (1 if axis == "gx" else 3) - up


def pack_records(out, rec, slots, number, way, number_tile):
    out[number_tile] = jnp.full((8, NZ), number.astype(F32))
    for k in range(MOVERS):
        row = rec[slots[0, way, k]]
        out[k // 2, (k % 2) * 4 : (k % 2) * 4 + 4] = jnp.where(k < number, row, 0.0)


def first_kernel(
    conc_h, pot_h, eps_h, rec_h, nodes_h, arrive_h, slots_h, counts_h, count,
    s1, s0, conc, pot, eps, arrive, xr, rows, cells, state,
    rec, nodes, slots, counts, gone, sems,
):
    copies = [(slots_h, slots), (counts_h, counts), (rec_h, rec), (nodes_h, nodes), (conc_h, conc)]
    for odd, out in enumerate((s0, s1)):
        start = pl.multiple_of(way_of("gy", odd)[0] * W, W)
        copies.append((pot_h.at[:, pl.ds(start, W)], out.at[pl.ds(Y_POT, BX)]))
        copies.append((eps_h.at[:, pl.ds(start, W)], out.at[pl.ds(Y_EPS, BX)]))
    copies += [(pot_h, pot), (eps_h, eps), (arrive_h, arrive)]
    copies = [pltpu.make_async_copy(a, b, sems.at[n]) for n, (a, b) in enumerate(copies)]
    for copy in copies:
        copy.start()

    def clear(c, _):
        gone[c] = 0
        return 0

    lax.fori_loop(0, SLOTS, clear, 0, unroll=16)
    for copy in copies[:2]:
        copy.wait()
    for way in range(4):

        def mark(k, _, way=way):
            gone[slots[0, way, k]] = 1
            return 0

        lax.fori_loop(0, counts[0, way], mark, 0)
    live = count[0]
    for copy in copies[2:]:
        copy.wait()

    def gather(c, found):
        rows[found] = rec[c]
        cells[found] = nodes[pl.ds(c, 1), :]
        stays = jnp.logical_and(c < live, gone[c] == 0)
        return found + stays.astype(jnp.int32)

    found = lax.fori_loop(0, SLOTS, gather, 0, unroll=16)
    state[...] = jnp.full((8, NZ), found.astype(F32))
    for odd in range(2):
        up, way = way_of("gx", odd)
        pack_records(xr.at[odd], rec, slots, counts[0, way], way, X_POT)
        xr[odd, X_CONC:X_POT] = conc[:, up * (BX - 1)].reshape(6, 8, NZ)
    for odd, out in enumerate((s0, s1)):
        up, way = way_of("gy", odd)
        pack_records(out, rec, slots, counts[0, way], way, Y_NUM)
        for s in range(3):
            face = jnp.where(up == 1, conc[s, :, BY - 1], conc[s, :, 0])
            out[Y_CONC + 2 * s : Y_CONC + 2 * s + 2] = face.reshape(2, 8, NZ)


def kept_kernel(rows, cells, state, state_out, acc):
    state_out[...] = state[...]
    acc[...] = jnp.zeros_like(acc)
    spread_groups(0, jnp.minimum(EARLY, number_in(state[...]) // GROUP), rows, cells, acc)


def pack_x_kernel(xr, pot, eps, y1, y0, state, s1, s0):
    del state
    px, py = parity("gx"), parity("gy")
    for n, (out, up) in enumerate(((s0, 1 - px), (s1, px))):
        out[0:X_POT] = xr[n, 0:X_POT]
        out[X_NUM] = xr[n, X_POT]
        for first, own, tile in ((X_POT, pot, Y_POT), (X_EPS, eps, Y_EPS)):
            own = own[pl.ds(up * W, W)]
            a, b = y0[pl.ds(tile + up * W, W)], y1[pl.ds(tile + up * W, W)]
            low, high = jnp.where(py == 1, a, b), jnp.where(py == 1, b, a)
            for x in range(W):
                out[first + 4 * x] = low[x]
                out[first + 4 * x + 1] = own[x, 0:8]
                out[first + 4 * x + 2] = own[x, 8:16]
                out[first + 4 * x + 3] = high[x]


def arrive_y_kernel(acc_in, rows_in, cells_in, state, y0, y1, nodes, rows, cells, state_out, acc, rec, cell):
    py = parity("gy")
    del acc_in
    rec[0:STORE] = rows_in[...]
    cell[0:STORE] = cells_in[...]
    found = number_in(state[...])
    total = append(found, y0, Y_NUM, 3 - py, nodes, rec, cell)
    total = append(total, y1, Y_NUM, 2 + py, nodes, rec, cell)
    done = total // GROUP
    spread_groups(jnp.minimum(EARLY, found // GROUP), done, rec, cell, acc)
    for g in range(GROUP):
        rows[g] = rec[done * GROUP + g]
        cells[g] = cell[done * GROUP + g]
    state_out[...] = jnp.full((8, NZ), (total - done * GROUP).astype(F32))


def spread_rows(acc, channel, ex, first, number):
    half, row = divmod(ex, WIDE // 2)
    base = (row * WIDE + first) * 8 + channel
    return acc[half, pl.ds(base, number, stride=8)] + acc[half, pl.ds(base + 4, number, stride=8)]


def arrive_x_kernel(
    acc_in, rows, cells, state, x1, x0, y0, y1, nodes, conc, pot,
    conc_next, acc, dens, s1, s0,
    rec, cell, wide,
):
    px, py = parity("gx"), parity("gy")
    x_low_first, y_low_first = px == 1, py == 1
    del acc_in
    rec[0:GROUP] = rows[...]
    cell[0:GROUP] = cells[...]
    total = append(number_in(state[...]), x0, X_NUM, 1 - px, nodes, rec, cell)
    total = append(total, x1, X_NUM, px, nodes, rec, cell)
    for g in range(GROUP):
        rec[total + g] = jnp.zeros((CHANNELS, NODES), F32)
        cell[total + g] = jnp.zeros((1, NODES), jnp.int32)
    spread_groups(0, (total + GROUP - 1) // GROUP, rec, cell, acc)

    for f in range(4):
        wide[f, 1 : BX + 1, 8 : 8 + BY] = conc[f] if f < 3 else pot[...]
        if f < 3:
            xa, xb = (x[X_CONC + 2 * f : X_CONC + 2 * f + 2].reshape(BY, NZ) for x in (x0, x1))
            x_low, x_high = jnp.where(x_low_first, xa, xb), jnp.where(x_low_first, xb, xa)
            ya, yb = (y[Y_CONC + 2 * f : Y_CONC + 2 * f + 2].reshape(BX, NZ) for y in (y0, y1))
            y_low, y_high = jnp.where(y_low_first, ya, yb), jnp.where(y_low_first, yb, ya)
        else:
            last, first = X_POT + 4 * (W - 1) + 1, X_POT + 1
            x_low = jnp.where(x_low_first, x0[last : last + 2], x1[last : last + 2]).reshape(BY, NZ)
            x_high = jnp.where(x_low_first, x1[first : first + 2], x0[first : first + 2]).reshape(BY, NZ)
            y_low = jnp.where(y_low_first, y0[Y_POT:Y_EPS, 7], y1[Y_POT:Y_EPS, 7])
            y_high = jnp.where(y_low_first, y1[Y_POT:Y_EPS, 0], y0[Y_POT:Y_EPS, 0])
        wide[f, 0, 8 : 8 + BY] = x_low
        wide[f, BX + 1, 8 : 8 + BY] = x_high
        wide[f, 1 : BX + 1, 7] = y_low
        wide[f, 1 : BX + 1, 8 + BY] = y_high

    dens[...] = jnp.zeros_like(dens)
    for ex in range(WIDE):
        dens[ex, 7 : 7 + WIDE] = spread_rows(acc, 0, ex, 0, WIDE)

    def around(f, x):
        c = wide[f, x + 1, 8:24]
        beside = (wide[f, x + 2, 8:24], wide[f, x, 8:24], wide[f, x + 1, 9:25], wide[f, x + 1, 7:23])
        return c, (*beside, pltpu.roll(c, NZ - 1, 1), pltpu.roll(c, 1, 1))

    def total_of(terms):
        return ((terms[0] + terms[1]) + (terms[2] + terms[3])) + (terms[4] + terms[5])

    for x in range(BX):
        p, steps = around(3, x)
        steps = [q - p for q in steps]
        total = dens[x + 1, 8:24]
        for s in range(3):
            c, beside = around(s, x)
            plain = total_of([n - c for n in beside])
            drift = total_of([(n + c) * q for n, q in zip(beside, steps)])
            later = c + (TIME_STEP * DIFFUSION[s]) * (plain + (VALENCE[s] * 0.5) * drift)
            conc_next[s, x] = later
            total = total + VALENCE[s] * later
        dens[x + 1, 8:24] = total

    for out, up in ((s0, 1 - py), (s1, py)):
        for ex in range(WIDE):
            out[ex * 8 : ex * 8 + 8] = jnp.where(up == 1, dens[ex, 17:25], dens[ex, 7:15])
        for a in range(3):
            for half in range(2):
                rims = []
                for ey in (0, WIDE - 1):
                    base = ey * 8 + a + 1
                    lead = acc[half, pl.ds(base, WIDE // 2, stride=WIDE * 8)]
                    rims.append(lead + acc[half, pl.ds(base + 4, WIDE // 2, stride=WIDE * 8)])
                r = DY_FORCE + a * WIDE + half * (WIDE // 2)
                out[r : r + WIDE // 2] = jnp.where(up == 1, rims[1], rims[0])
        out[DY_FORCE + 54 : DY_END] = jnp.zeros((2, NZ), F32)


def coefficient_kernel(acc, x0, x1, y0, y1, pot, eps, conc_next, conc_out, force, base, xp, xm, yp, ym, zp, zm, inv, phi, ew, sem):
    copy = pltpu.make_async_copy(conc_next, conc_out, sem)
    copy.start()
    px, y_low_first = parity("gx"), parity("gy") == 1
    for c in range(3):
        for ex in range(WIDE):
            force[c, ex] = spread_rows(acc, c + 1, ex, 1, BY)
    for buf, own, x_tile, y_tile in ((phi, pot, X_POT, Y_POT), (ew, eps, X_EPS, Y_EPS)):
        for n in range(BX):
            x = mirrored(px, n, BX - 1 - n)
            a, b = y0[y_tile + x], y1[y_tile + x]
            buf[W + n, 0:W] = jnp.where(y_low_first, a, b)
            buf[W + n, W : W + BY] = own[x]
            buf[W + n, W + BY : EXT] = jnp.where(y_low_first, b, a)
        for n in range(W):
            at = pl.ds(x_tile + 4 * mirrored(px, n, W - 1 - n), 4)
            buf[n] = x1[at].reshape(EXT, NZ)
            buf[W + BX + n] = x0[at].reshape(EXT, NZ)
    for x in range(1, EXT - 1):
        e = ew[x]
        up, down = e + ew[x + 1], e + ew[x - 1]
        north, south = e + pltpu.roll(e, EXT - 1, 0), e + pltpu.roll(e, 1, 0)
        over = e + pltpu.roll(e, NZ - 1, 1)
        under = pltpu.roll(over, 1, 1)
        scale = 1.0 / ((((up + down) + (north + south)) + (over + under)) + 2.0 * SCREENING)
        xp[x], xm[x] = up * scale, down * scale
        yp[x], ym[x] = north * scale, south * scale
        zp[x], zm[x] = over * scale, under * scale
        inv[x] = 2.0 * scale
    for buf in (xp, xm, yp, ym, zp, zm, inv, base):
        buf[0] = jnp.zeros((EXT, NZ), F32)
        buf[EXT - 1] = jnp.zeros((EXT, NZ), F32)
    for x in range(1, EXT - 1):
        base[x] = sweep_plane(1, x, phi.at[x - 1], phi.at[x], phi.at[x + 1], (xp, xm, yp, ym, zp, zm), None)
    copy.wait()


def join_y_kernel(dens, force, r1, r0, dext, fcore, s1, s0):
    px, py = parity("gx"), parity("gy")
    low_first = py == 1
    dext[0:7] = jnp.zeros((7, EXT, NZ), F32)
    dext[25:32] = jnp.zeros((7, EXT, NZ), F32)
    for n in range(WIDE):
        ex = mirrored(px, n, WIDE - 1 - n)
        dext[n + 7] = dens[ex]
        at = pl.ds(pl.multiple_of(ex * 8, 8), 8)
        a, b = r0[at], r1[at]
        dext[n + 7, 1:9] += jnp.where(low_first, a, b)
        dext[n + 7, 23:31] += jnp.where(low_first, b, a)
    fcore[...] = force[...]
    for c in range(3):
        r = DY_FORCE + c * WIDE
        a, b = r0[r : r + WIDE], r1[r : r + WIDE]
        fcore[c, :, 0] += jnp.where(low_first, a, b)
        fcore[c, :, BY - 1] += jnp.where(low_first, b, a)
    pack_rims(dext, fcore, s1, px, 7, 1)
    pack_rims(dext, fcore, s0, 1 - px, 24, -1)


def pack_rims(dext, fcore, out, up, first, way):
    for d in range(W):
        out[DX_AT[d] : DX_AT[d + 1]] = dext[first + way * d, d + 1 : 31 - d]
    for c in range(3):
        out[DX_FORCE + c * BY : DX_FORCE + (c + 1) * BY] = fcore[c, up * (WIDE - 1)]


def sweep_plane(k, x, west, here, east, weights, rhs):
    xp, xm, yp, ym, zp, zm = weights
    if k < SWEEPS:
        f = slice(0, EXT)
        north, south = pltpu.roll(here[...], EXT - 1, 0), pltpu.roll(here[...], 1, 0)
    else:
        f = slice(W, W + BY)
        north, south = here[W + 1 : W + BY + 1], here[W - 1 : W + BY - 1]
    centre = here[f]
    total = (xp[x, f] * east[f] + xm[x, f] * west[f]) + (yp[x, f] * north + ym[x, f] * south)
    along = zp[x, f] * pltpu.roll(centre, NZ - 1, 1) + zm[x, f] * pltpu.roll(centre, 1, 1)
    return total + (along if rhs is None else along + rhs[x, f])


def near_kernel(dext, r0, base, xp, xm, yp, ym, zp, zm, inv, near, edges, phi_a, phi_b, rhs):
    weights, other = (xp, xm, yp, ym, zp, zm), 1 - parity("gx")
    rhs[9 : EXT - 1] = dext[9 : EXT - 1]
    for d in range(W):
        rhs[23 + d, d + 1 : 31 - d] += r0[other, DX_AT[d] : DX_AT[d + 1]]
    rhs[9 : EXT - 1] = rhs[9 : EXT - 1] * inv[9 : EXT - 1]
    for k in range(1, SWEEPS + 1):
        old, new = (phi_a, phi_b)[k % 2], (phi_a, phi_b)[(k + 1) % 2]
        for x in range(W + k, EXT - k):
            if k == 1:
                total = base[x] + rhs[x]
            else:
                total = sweep_plane(k, x, old.at[x - 1], old.at[x], old.at[x + 1], weights, rhs)
            if k == SWEEPS:
                near[x - 16] = total
                continue
            new[x] = total
            if x < W + k + 2:
                edges[2 * k - 2 + x - W - k] = total


def far_kernel(
    dext, r1, r0, fcore, base, xp, xm, yp, ym, zp, zm, inv, near, edges,
    pot_next, force_out,
    phi_a, phi_b, rhs, force, lower, upper, sems,
):
    px = parity("gx")
    weights = (xp, xm, yp, ym, zp, zm)
    low_first = px == 1
    force[...] = fcore[:, 1 : BX + 1]
    a, b = (r[DX_FORCE:DX_END].reshape(3, BY, NZ) for r in (r0.at[1 - px], r1))
    force[:, 0] += jnp.where(low_first, a, b)
    force[:, BX - 1] += jnp.where(low_first, b, a)
    for n in range(W):
        upper[n] = near[mirrored(px, n, W - 1 - n)]
    copies = [
        pltpu.make_async_copy(force, force_out, sems.at[0]),
        pltpu.make_async_copy(upper, pot_next.at[pl.ds(mirrored(px, W, 0), W)], sems.at[1]),
        pltpu.make_async_copy(lower, pot_next.at[pl.ds(mirrored(px, 0, W), W)], sems.at[2]),
    ]
    copies[0].start()
    copies[1].start()

    rhs[1:16] = dext[1:16]
    for d in range(W):
        rhs[8 - d, d + 1 : 31 - d] += r1[DX_AT[d] : DX_AT[d + 1]]
    rhs[1:16] = rhs[1:16] * inv[1:16]

    def plane(k, x):
        return edges.at[2 * k - 2 + x - W - k] if x >= W + k else (phi_a, phi_b)[(k + 1) % 2].at[x]

    for k in range(1, SWEEPS + 1):
        for x in range(k, W + k):
            if k == 1:
                total = base[x] + rhs[x]
            else:
                total = sweep_plane(k, x, plane(k - 1, x - 1), plane(k - 1, x), plane(k - 1, x + 1), weights, rhs)
            if k < SWEEPS:
                plane(k, x)[...] = total
            else:
                lower[mirrored(px, x - W, 15 - x)] = total
    copies[2].start()
    for copy in copies:
        copy.wait()


def shape(*dims):
    return jax.ShapeDtypeStruct(dims, F32)


def call(kernel, name, ins, outs, scratch=(), flops=0, aliases=None, far_outs=()):
    moved = 4 * sum(int(o.size) for o in outs)
    return pl.pallas_call(
        kernel,
        name=name,
        in_specs=ins,
        out_specs=[HBM if n in far_outs else VMEM for n in range(len(outs))],
        out_shape=outs,
        scratch_shapes=scratch,
        input_output_aliases=aliases or {},
        compiler_params=pltpu.CompilerParams(vmem_limit_bytes=32 << 20),
        cost_estimate=pl.CostEstimate(flops=flops, bytes_accessed=moved, transcendentals=0),
    )


def body(conc, pot, eps, records, count, slots, counts, own_nodes, arrive_nodes):
    def store(number, kind=pltpu.VMEM):
        return [kind((number, CHANNELS, NODES), F32), kind((number, 1, NODES), jnp.int32)]

    sums = shape(2, ROWS, NZ)
    row_flops = 2 * ROWS * 2 * NZ * NODES
    field = shape(EXT, EXT, NZ)
    core = shape(BX, BY, NZ)

    ins = [pltpu.with_memory_space_constraint(x, pltpu.HBM) for x in (conc, pot, eps, records)]
    lists = [pltpu.with_memory_space_constraint(x, pltpu.HBM) for x in (slots, counts)]
    more = [pltpu.with_memory_space_constraint(x, pltpu.HBM) for x in (own_nodes, arrive_nodes)]
    small = [pltpu.SMEM((1, 4, MOVERS), jnp.int32), pltpu.SMEM((1, 4), jnp.int32)]
    rec = pltpu.VMEM((SLOTS, CHANNELS, NODES), F32)
    a1, a0, conc_v, pot_v, eps_v, arrive_v, xr, rows, cells, state = call(
        first_kernel,
        "first",
        [HBM] * 8 + [SMEM],
        [
            shape(Y_END, 8, NZ), shape(Y_END, 8, NZ), shape(3, BX, BY, NZ), core, core,
            jax.ShapeDtypeStruct((1, 4, MOVERS, NODES), jnp.int32),
            shape(2, X_POT + 1, 8, NZ), *store(STORE, jax.ShapeDtypeStruct), shape(8, NZ),
        ],
        [rec, pltpu.VMEM((SLOTS, NODES), jnp.int32), *small, pltpu.SMEM((SLOTS,), jnp.int32), pltpu.SemaphoreType.DMA((12,))],
    )(*ins, *more, *lists, count)
    y0, y1 = swap(a0, "gy", 0), swap(a1, "gy", 1)
    late, acc = call(kept_kernel, "spread_kept", [VMEM] * 3, [shape(8, NZ), sums], flops=row_flops * EARLY * GROUP)(
        rows, cells, state
    )
    b1, b0 = call(pack_x_kernel, "pack_x", [VMEM] * 6, [shape(X_END, 8, NZ)] * 2)(xr, pot_v, eps_v, y1, y0, late)
    x1, x0 = swap(b1, "gx", 1), swap(b0, "gx", 0)
    rows, cells, state, acc = call(
        arrive_y_kernel,
        "spread_y",
        [VMEM] * 7,
        [*store(GROUP, jax.ShapeDtypeStruct), shape(8, NZ), sums],
        store(STORE + 2 * MOVERS + GROUP),
        flops=row_flops * 48,
        aliases={0: 3},
    )(acc, rows, cells, state, y0, y1, arrive_v)
    conc_near, acc, dens, c1, c0 = call(
        arrive_x_kernel,
        "spread_x",
        [VMEM] * 11,
        [shape(3, BX, BY, NZ), sums, shape(WIDE, EXT, NZ), shape(DY_END, NZ), shape(DY_END, NZ)],
        store(2 * MOVERS + 2 * GROUP) + [pltpu.VMEM((4, WIDE, 32, NZ), F32)],
        flops=row_flops * 2 * MOVERS,
        aliases={0: 1},
    )(acc, rows, cells, state, x1, x0, y0, y1, arrive_v, conc_v, pot_v)
    r0, r1 = swap(c0, "gy", 0), swap(c1, "gy", 1)
    conc_next, force, base, *weights = call(
        coefficient_kernel,
        "coefficients",
        [VMEM] * 8,
        [shape(3, BX, BY, NZ), shape(3, WIDE, BY, NZ)] + [field] * 8,
        [pltpu.VMEM((EXT, EXT, NZ), F32)] * 2 + [pltpu.SemaphoreType.DMA],
        flops=row_flops * 8,
        far_outs=(0,),
    )(acc, x0, x1, y0, y1, pot_v, eps_v, conc_near)
    dext, fcore, e1, e0 = call(
        join_y_kernel, "join_y", [VMEM] * 4, [field, shape(3, WIDE, BY, NZ), shape(DX_END, NZ), shape(DX_END, NZ)]
    )(dens, force, r1, r0)
    g1, g0 = swap(e1, "gx", 1), chip_pair(e0)
    scratch = [pltpu.VMEM((EXT, EXT, NZ), F32)] * 3
    near, edges = call(
        near_kernel,
        "sweeps_near",
        [VMEM] * 10,
        [shape(BX // 2, BY, NZ), shape(2 * SWEEPS - 2, EXT, NZ)],
        scratch,
        flops=12 * SWEEPS * EXT * EXT * NZ,
    )(dext, g0, base, *weights)
    pot_next, body_force = call(
        far_kernel,
        "sweeps_far",
        [VMEM] * 14,
        [core, shape(3, BX, BY, NZ)],
        scratch + [pltpu.VMEM((3, BX, BY, NZ), F32)] + [pltpu.VMEM((W, BY, NZ), F32)] * 2 + [pltpu.SemaphoreType.DMA((3,))],
        flops=8 * SWEEPS * EXT * EXT * NZ,
        far_outs=(0, 1),
    )(dext, g1, g0, fcore, base, *weights, near, edges)
    return conc_next, pot_next, body_force


def solution(mesh):
    placed = (
        P(None, "gx", "gy", None),
        P("gx", "gy", None),
        P("gx", "gy", None),
        P(("gx", "gy"), None, None),
        P(("gx", "gy")),
        P(("gx", "gy"), None, None),
        P(("gx", "gy"), None),
        P(("gx", "gy"), None),
        P(("gx", "gy"), None, None, None),
    )
    return jax.shard_map(
        body,
        mesh=mesh,
        in_specs=placed,
        out_specs=(P(None, "gx", "gy", None), P("gx", "gy", None), P(None, "gx", "gy", None)),
        check_vma=False,
    )
```

```python
import jax
import jax.numpy as jnp
from jax import lax
from jax.experimental import pallas as pl
from jax.experimental.pallas import tpu as pltpu
from jax.sharding import PartitionSpec as P

SWEEPS = 8
DIFFUSION = (1.0, 0.7, 0.45)
VALENCE = (1.0, -1.0, 2.0)
TIME_STEP = 0.05
SCREENING = 0.05

F32 = jnp.float32
BF16 = jnp.bfloat16
BX, BY, NZ = 16, 16, 128
SLOTS, MOVERS, CHANNELS, NODES = 128, 16, 4, 128
W = 8
EXT = BX + 2 * W
WIDE = BX + 2
PAIRS = WIDE * WIDE // 2
ROWS = PAIRS * 2 * CHANNELS
GROUP = 8
EARLY = 8
STORE = SLOTS + GROUP

Y_CONC, Y_POT, Y_EPS, Y_NUM, Y_END = 8, 14, 30, 46, 47
X_AT = [0] + [sum(EXT - 2 * d for d in range(1, n + 1)) for n in range(W + 1)]
X_CONC, X_NUM, X_POT = 64, 112, 120
X_EPS = X_POT + X_AT[W + 1]
X_END = X_EPS + X_AT[W + 1]
DY_FORCE, DY_END = WIDE * W, WIDE * W + 56
DX_AT = [sum(EXT - 2 - 2 * d for d in range(n)) for n in range(W + 1)]
DX_FORCE, DX_END = DX_AT[W], DX_AT[W] + 3 * BY

VMEM = pl.BlockSpec(memory_space=pltpu.VMEM)
SMEM = pl.BlockSpec(memory_space=pltpu.SMEM)
HBM = pl.BlockSpec(memory_space=pltpu.HBM)


def parity(axis):
    return lax.rem(lax.axis_index(axis), 2)


def swap(block, axis, odd):
    count = lax.axis_size(axis)
    route = [(i, (((i - odd) % count ^ 1) + odd) % count) for i in range(count)]
    return lax.ppermute(block, axis, route)


def chip_pair(block):
    pairs = [[i, i + 1] for i in range(0, lax.axis_size("gx"), 2)]
    return lax.all_gather(block, "gx", axis_index_groups=pairs)


def hot_group(first, number, rec, cells):
    sub = lax.broadcasted_iota(jnp.int32, (16, NODES), 0)
    second = (sub >= 8).astype(F32)
    subf = sub.astype(F32)
    left, right = [], []
    for g in range(number):
        cell, value = cells[first + g], rec[first + g]
        half = (cell >= PAIRS * NZ).astype(jnp.int32)
        high = ((cell - half * (PAIRS * NZ)) >> 7).astype(F32)
        low = ((cell & (NZ - 1)) + half * NZ).astype(F32)
        high = (jnp.broadcast_to(high, (16, NODES)) - second).astype(BF16)
        low = (jnp.broadcast_to(low, (16, NODES)) - subf).astype(BF16)
        lead = value.astype(BF16).astype(F32)
        rest = value - lead
        parts = jnp.concatenate([lead, rest, lead, rest], axis=0).astype(BF16)
        left.append(jnp.concatenate([jnp.where(high == BF16(2 * m), parts, BF16(0)) for m in range(ROWS // 16)], axis=0))
        right.append(jnp.concatenate([jnp.where(low == BF16(16 * m), BF16(1), BF16(0)) for m in range(16)], axis=0))
    left, right = jnp.concatenate(left, axis=1), jnp.concatenate(right, axis=1)
    sums = lax.dot_general(left, right, (((1,), (1,)), ((), ())), preferred_element_type=F32)
    return sums[:, :NZ], sums[:, NZ:]


def spread_groups(start, stop, rec, cells, acc):
    def groups(number):
        def group(c, first):
            left, right = hot_group(first, number, rec, cells)
            acc[0] += left
            acc[1] += right
            return first + number

        return group

    count = stop - start
    first = lax.fori_loop(0, count // 2, groups(2 * GROUP), start * GROUP)
    lax.fori_loop(0, lax.rem(count, 2), groups(GROUP), first)


def mirrored(px, low, high):
    return jnp.where(px == 1, high, low)


def number_in(tile):
    return jnp.max(tile).astype(jnp.int32)


def append(total, buf, number, way, nodes, rec, cells):
    for k in range(MOVERS):
        rec[total + k] = buf[record(buf, k)]
        cells[total + k] = nodes[0, way, k : k + 1]
    return total + number_in(number)


def way_of(axis, odd):
    p = parity(axis)
    up = 1 - p if odd == 0 else p
    return up, (1 if axis == "gx" else 3) - up


def pack_records(out, rec, slots, number, way):
    for k in range(MOVERS):
        row = rec[slots[0, way, k]]
        out[record(out, k)] = jnp.where(k < number, row, 0.0)


def record(buf, k):
    return (k // 2, pl.ds((k % 2) * 4, 4)) if len(buf.shape) == 3 else (pl.ds(4 * k, 4),)


def first_kernel(
    conc_h, pot_h, eps_h, rec_h, nodes_h, arrive_h, slots_h, counts_h, count,
    s1, s0, conc, pot, eps, arrive, xr, rows, cells, state, acc,
    rec, nodes, slots, counts, gone, sems,
):
    copies = [(slots_h, slots), (counts_h, counts), (rec_h, rec), (nodes_h, nodes), (conc_h, conc)]
    for odd, out in enumerate((s0, s1)):
        start = pl.multiple_of(way_of("gy", odd)[0] * W, W)
        copies.append((pot_h.at[:, pl.ds(start, W)], out.at[pl.ds(Y_POT, BX)]))
        copies.append((eps_h.at[:, pl.ds(start, W)], out.at[pl.ds(Y_EPS, BX)]))
    copies += [(pot_h, pot), (eps_h, eps), (arrive_h, arrive)]
    copies = [pltpu.make_async_copy(a, b, sems.at[n]) for n, (a, b) in enumerate(copies)]
    for copy in copies:
        copy.start()
    acc[...] = jnp.zeros_like(acc)

    def clear(c, _):
        gone[c] = 0
        return 0

    lax.fori_loop(0, SLOTS, clear, 0, unroll=16)
    for copy in copies[:2]:
        copy.wait()
    for way in range(4):

        def mark(k, _, way=way):
            gone[slots[0, way, k]] = 1
            return 0

        lax.fori_loop(0, counts[0, way], mark, 0)
    live = count[0]
    for copy in copies[2:4]:
        copy.wait()

    def gather(c, found):
        rows[found] = rec[c]
        cells[found] = nodes[pl.ds(c, 1), :]
        stays = jnp.logical_and(c < live, gone[c] == 0)
        return found + stays.astype(jnp.int32)

    found = lax.fori_loop(0, SLOTS, gather, 0, unroll=16)
    state[...] = jnp.full((8, NZ), found.astype(F32))
    copies[4].wait()
    for odd in range(2):
        up, way = way_of("gx", odd)
        number = counts[0, way]
        pack_records(xr.at[odd], rec, slots, number, way)
        xr[odd, X_CONC:X_NUM] = conc[:, up * (BX - 1)].reshape(X_NUM - X_CONC, NZ)
        xr[odd, X_NUM:X_POT] = jnp.full((8, NZ), number.astype(F32))
    for odd, out in enumerate((s0, s1)):
        up, way = way_of("gy", odd)
        number = counts[0, way]
        pack_records(out, rec, slots, number, way)
        out[Y_NUM] = jnp.full((8, NZ), number.astype(F32))
        for s in range(3):
            face = jnp.where(up == 1, conc[s, :, BY - 1], conc[s, :, 0])
            out[Y_CONC + 2 * s : Y_CONC + 2 * s + 2] = face.reshape(2, 8, NZ)
    for copy in copies[5:]:
        copy.wait()


def kept_kernel(acc_in, rows, cells, state, state_out, acc):
    del acc_in
    state_out[...] = state[...]
    spread_groups(0, jnp.minimum(EARLY, number_in(state[...]) // GROUP), rows, cells, acc)


def pack_x_kernel(xr, pot, eps, y1, y0, state, s1, s0):
    del state
    px, py = parity("gx"), parity("gy")
    for n, (out, up) in enumerate(((s0, 1 - px), (s1, px))):
        out[0:X_POT] = xr[n]
        for first, own, tile in ((X_POT, pot, Y_POT), (X_EPS, eps, Y_EPS)):
            for d in range(1, W + 1):
                x = jnp.where(up == 1, BX - d, d - 1)
                a, b = y0[tile + x], y1[tile + x]
                low, high = jnp.where(py == 1, a, b), jnp.where(py == 1, b, a)
                at = first + X_AT[d]
                if d < W:
                    out[at : at + W - d] = low[d:]
                    out[at + W - d + BY : at + 2 * (W - d) + BY] = high[: W - d]
                out[at + W - d : at + W - d + BY] = own[x]


def arrive_y_kernel(acc_in, rows_in, cells_in, state, y0, y1, nodes, rows, cells, state_out, acc, rec, cell):
    py = parity("gy")
    del acc_in
    rec[0:STORE] = rows_in[...]
    cell[0:STORE] = cells_in[...]
    found = number_in(state[...])
    total = append(found, y0, y0[Y_NUM], 3 - py, nodes, rec, cell)
    total = append(total, y1, y1[Y_NUM], 2 + py, nodes, rec, cell)
    done = total // GROUP
    spread_groups(jnp.minimum(EARLY, found // GROUP), done, rec, cell, acc)
    for g in range(GROUP):
        rows[g] = rec[done * GROUP + g]
        cells[g] = cell[done * GROUP + g]
    state_out[...] = jnp.full((8, NZ), (total - done * GROUP).astype(F32))


def spread_rows(acc, channel, ex, first, number):
    half, row = divmod(ex, WIDE // 2)
    base = (row * WIDE + first) * 8 + channel
    return acc[half, pl.ds(base, number, stride=8)] + acc[half, pl.ds(base + 4, number, stride=8)]


def arrive_x_kernel(
    acc_in, rows, cells, state, x1, x0, y0, y1, nodes, conc, pot,
    conc_next, acc, dens, s1, s0,
    rec, cell, wide,
):
    px, py = parity("gx"), parity("gy")
    x_low_first, y_low_first = px == 1, py == 1
    del acc_in
    rec[0:GROUP] = rows[...]
    cell[0:GROUP] = cells[...]
    total = append(number_in(state[...]), x0, x0[X_NUM:X_POT], 1 - px, nodes, rec, cell)
    total = append(total, x1, x1[X_NUM:X_POT], px, nodes, rec, cell)
    for g in range(GROUP):
        rec[total + g] = jnp.zeros((CHANNELS, NODES), F32)
        cell[total + g] = jnp.zeros((1, NODES), jnp.int32)
    spread_groups(0, (total + GROUP - 1) // GROUP, rec, cell, acc)

    for f in range(4):
        wide[f, 1 : BX + 1, 8 : 8 + BY] = conc[f] if f < 3 else pot[...]
        if f < 3:
            xa, xb = (x[X_CONC + BY * f : X_CONC + BY * f + BY] for x in (x0, x1))
            x_low, x_high = jnp.where(x_low_first, xa, xb), jnp.where(x_low_first, xb, xa)
            ya, yb = (y[Y_CONC + 2 * f : Y_CONC + 2 * f + 2].reshape(BX, NZ) for y in (y0, y1))
            y_low, y_high = jnp.where(y_low_first, ya, yb), jnp.where(y_low_first, yb, ya)
        else:
            xa, xb = (x[X_POT + W - 1 : X_POT + W - 1 + BY] for x in (x0, x1))
            x_low, x_high = jnp.where(x_low_first, xa, xb), jnp.where(x_low_first, xb, xa)
            y_low = jnp.where(y_low_first, y0[Y_POT:Y_EPS, 7], y1[Y_POT:Y_EPS, 7])
            y_high = jnp.where(y_low_first, y1[Y_POT:Y_EPS, 0], y0[Y_POT:Y_EPS, 0])
        wide[f, 0, 8 : 8 + BY] = x_low
        wide[f, BX + 1, 8 : 8 + BY] = x_high
        wide[f, 1 : BX + 1, 7] = y_low
        wide[f, 1 : BX + 1, 8 + BY] = y_high

    dens[...] = jnp.zeros_like(dens)
    for ex in range(WIDE):
        dens[ex, 7 : 7 + WIDE] = spread_rows(acc, 0, ex, 0, WIDE)

    def around(f, x):
        c = wide[f, x + 1, 8:24]
        beside = (wide[f, x + 2, 8:24], wide[f, x, 8:24], wide[f, x + 1, 9:25], wide[f, x + 1, 7:23])
        return c, (*beside, pltpu.roll(c, NZ - 1, 1), pltpu.roll(c, 1, 1))

    def total_of(terms):
        return ((terms[0] + terms[1]) + (terms[2] + terms[3])) + (terms[4] + terms[5])

    for x in range(BX):
        p, steps = around(3, x)
        steps = [q - p for q in steps]
        total = dens[x + 1, 8:24]
        for s in range(3):
            c, beside = around(s, x)
            plain = total_of([n - c for n in beside])
            drift = total_of([(n + c) * q for n, q in zip(beside, steps)])
            later = c + (TIME_STEP * DIFFUSION[s]) * (plain + (VALENCE[s] * 0.5) * drift)
            conc_next[s, x] = later
            total = total + VALENCE[s] * later
        dens[x + 1, 8:24] = total

    for out, up in ((s0, 1 - py), (s1, py)):
        for ex in range(WIDE):
            out[ex * 8 : ex * 8 + 8] = jnp.where(up == 1, dens[ex, 17:25], dens[ex, 7:15])
        for a in range(3):
            for half in range(2):
                rims = []
                for ey in (0, WIDE - 1):
                    base = ey * 8 + a + 1
                    lead = acc[half, pl.ds(base, WIDE // 2, stride=WIDE * 8)]
                    rims.append(lead + acc[half, pl.ds(base + 4, WIDE // 2, stride=WIDE * 8)])
                r = DY_FORCE + a * WIDE + half * (WIDE // 2)
                out[r : r + WIDE // 2] = jnp.where(up == 1, rims[1], rims[0])
        out[DY_FORCE + 54 : DY_END] = jnp.zeros((2, NZ), F32)


def coefficient_kernel(acc, x0, x1, y0, y1, pot, eps, conc_next, conc_out, force, base, xp, xm, yp, ym, zp, zm, inv, phi, ew, sem):
    copy = pltpu.make_async_copy(conc_next, conc_out, sem)
    copy.start()
    px, y_low_first = parity("gx"), parity("gy") == 1
    for c in range(3):
        for ex in range(WIDE):
            force[c, ex] = spread_rows(acc, c + 1, ex, 1, BY)
    for buf, own, x_tile, y_tile in ((phi, pot, X_POT, Y_POT), (ew, eps, X_EPS, Y_EPS)):
        for n in range(BX):
            x = mirrored(px, n, BX - 1 - n)
            a, b = y0[y_tile + x], y1[y_tile + x]
            buf[W + n, 0:W] = jnp.where(y_low_first, a, b)
            buf[W + n, W : W + BY] = own[x]
            buf[W + n, W + BY : EXT] = jnp.where(y_low_first, b, a)
        for n in (*range(W), *range(W + BX, EXT)):
            buf[n] = jnp.ones((EXT, NZ), F32)
        for d in range(1, W + 1):
            at = slice(x_tile + X_AT[d], x_tile + X_AT[d + 1])
            buf[W - d, d : EXT - d] = x1[at]
            buf[W + BX - 1 + d, d : EXT - d] = x0[at]
    for x in range(1, EXT - 1):
        e = ew[x]
        up, down = e + ew[x + 1], e + ew[x - 1]
        north, south = e + pltpu.roll(e, EXT - 1, 0), e + pltpu.roll(e, 1, 0)
        over = e + pltpu.roll(e, NZ - 1, 1)
        under = pltpu.roll(over, 1, 1)
        scale = 1.0 / ((((up + down) + (north + south)) + (over + under)) + 2.0 * SCREENING)
        xp[x], xm[x] = up * scale, down * scale
        yp[x], ym[x] = north * scale, south * scale
        zp[x], zm[x] = over * scale, under * scale
        inv[x] = 2.0 * scale
    for buf in (xp, xm, yp, ym, zp, zm, inv, base):
        buf[0] = jnp.zeros((EXT, NZ), F32)
        buf[EXT - 1] = jnp.zeros((EXT, NZ), F32)
    for x in range(1, EXT - 1):
        base[x] = sweep_plane(1, x, phi.at[x - 1], phi.at[x], phi.at[x + 1], (xp, xm, yp, ym, zp, zm), None)
    copy.wait()


def join_y_kernel(dens, force, r1, r0, dext, fcore, s1, s0):
    px, py = parity("gx"), parity("gy")
    low_first = py == 1
    dext[0:7] = jnp.zeros((7, EXT, NZ), F32)
    dext[25:32] = jnp.zeros((7, EXT, NZ), F32)
    for n in range(WIDE):
        ex = mirrored(px, n, WIDE - 1 - n)
        dext[n + 7] = dens[ex]
        at = pl.ds(pl.multiple_of(ex * 8, 8), 8)
        a, b = r0[at], r1[at]
        dext[n + 7, 1:9] += jnp.where(low_first, a, b)
        dext[n + 7, 23:31] += jnp.where(low_first, b, a)
    fcore[...] = force[...]
    for c in range(3):
        r = DY_FORCE + c * WIDE
        a, b = r0[r : r + WIDE], r1[r : r + WIDE]
        fcore[c, :, 0] += jnp.where(low_first, a, b)
        fcore[c, :, BY - 1] += jnp.where(low_first, b, a)
    pack_rims(dext, fcore, s1, px, 7, 1)
    pack_rims(dext, fcore, s0, 1 - px, 24, -1)


def pack_rims(dext, fcore, out, up, first, way):
    for d in range(W):
        out[DX_AT[d] : DX_AT[d + 1]] = dext[first + way * d, d + 1 : 31 - d]
    for c in range(3):
        out[DX_FORCE + c * BY : DX_FORCE + (c + 1) * BY] = fcore[c, up * (WIDE - 1)]


def sweep_plane(k, x, west, here, east, weights, rhs):
    xp, xm, yp, ym, zp, zm = weights
    if k < SWEEPS:
        f = slice(0, EXT)
        north, south = pltpu.roll(here[...], EXT - 1, 0), pltpu.roll(here[...], 1, 0)
    else:
        f = slice(W, W + BY)
        north, south = here[W + 1 : W + BY + 1], here[W - 1 : W + BY - 1]
    centre = here[f]
    total = (xp[x, f] * east[f] + xm[x, f] * west[f]) + (yp[x, f] * north + ym[x, f] * south)
    along = zp[x, f] * pltpu.roll(centre, NZ - 1, 1) + zm[x, f] * pltpu.roll(centre, 1, 1)
    return total + (along if rhs is None else along + rhs[x, f])


def near_kernel(dext, r0, base, xp, xm, yp, ym, zp, zm, inv, near, edges, phi_a, phi_b, rhs):
    weights, other = (xp, xm, yp, ym, zp, zm), 1 - parity("gx")
    rhs[9 : EXT - 1] = dext[9 : EXT - 1]
    for d in range(W):
        rhs[23 + d, d + 1 : 31 - d] += r0[other, DX_AT[d] : DX_AT[d + 1]]
    rhs[9 : EXT - 1] = rhs[9 : EXT - 1] * inv[9 : EXT - 1]
    for k in range(1, SWEEPS + 1):
        old, new = (phi_a, phi_b)[k % 2], (phi_a, phi_b)[(k + 1) % 2]
        for x in range(W + k, EXT - k):
            if k == 1:
                total = base[x] + rhs[x]
            else:
                total = sweep_plane(k, x, old.at[x - 1], old.at[x], old.at[x + 1], weights, rhs)
            if k == SWEEPS:
                near[x - 16] = total
                continue
            new[x] = total
            if x < W + k + 2:
                edges[2 * k - 2 + x - W - k] = total


def far_kernel(
    dext, r1, r0, fcore, base, xp, xm, yp, ym, zp, zm, inv, near, edges,
    pot_next, force_out,
    phi_a, phi_b, rhs, force, lower, upper, sems,
):
    px = parity("gx")
    weights = (xp, xm, yp, ym, zp, zm)
    low_first = px == 1
    force[...] = fcore[:, 1 : BX + 1]
    a, b = (r[DX_FORCE:DX_END].reshape(3, BY, NZ) for r in (r0.at[1 - px], r1))
    force[:, 0] += jnp.where(low_first, a, b)
    force[:, BX - 1] += jnp.where(low_first, b, a)
    for n in range(W):
        upper[n] = near[mirrored(px, n, W - 1 - n)]
    copies = [
        pltpu.make_async_copy(force, force_out, sems.at[0]),
        pltpu.make_async_copy(upper, pot_next.at[pl.ds(mirrored(px, W, 0), W)], sems.at[1]),
        pltpu.make_async_copy(lower, pot_next.at[pl.ds(mirrored(px, 0, W), W)], sems.at[2]),
    ]
    copies[0].start()
    copies[1].start()

    rhs[1:16] = dext[1:16]
    for d in range(W):
        rhs[8 - d, d + 1 : 31 - d] += r1[DX_AT[d] : DX_AT[d + 1]]
    rhs[1:16] = rhs[1:16] * inv[1:16]

    def plane(k, x):
        return edges.at[2 * k - 2 + x - W - k] if x >= W + k else (phi_a, phi_b)[(k + 1) % 2].at[x]

    for k in range(1, SWEEPS + 1):
        for x in range(k, W + k):
            if k == 1:
                total = base[x] + rhs[x]
            else:
                total = sweep_plane(k, x, plane(k - 1, x - 1), plane(k - 1, x), plane(k - 1, x + 1), weights, rhs)
            if k < SWEEPS:
                plane(k, x)[...] = total
            else:
                lower[mirrored(px, x - W, 15 - x)] = total
    copies[2].start()
    for copy in copies:
        copy.wait()


def shape(*dims):
    return jax.ShapeDtypeStruct(dims, F32)


def call(kernel, name, ins, outs, scratch=(), flops=0, aliases=None, far_outs=()):
    moved = 4 * sum(int(o.size) for o in outs)
    return pl.pallas_call(
        kernel,
        name=name,
        in_specs=ins,
        out_specs=[HBM if n in far_outs else VMEM for n in range(len(outs))],
        out_shape=outs,
        scratch_shapes=scratch,
        input_output_aliases=aliases or {},
        compiler_params=pltpu.CompilerParams(vmem_limit_bytes=32 << 20),
        cost_estimate=pl.CostEstimate(flops=flops, bytes_accessed=moved, transcendentals=0),
    )


def body(conc, pot, eps, records, count, slots, counts, own_nodes, arrive_nodes):
    def store(number, kind=pltpu.VMEM):
        return [kind((number, CHANNELS, NODES), F32), kind((number, 1, NODES), jnp.int32)]

    sums = shape(2, ROWS, NZ)
    row_flops = 2 * ROWS * 2 * NZ * NODES
    field = shape(EXT, EXT, NZ)
    core = shape(BX, BY, NZ)

    ins = [pltpu.with_memory_space_constraint(x, pltpu.HBM) for x in (conc, pot, eps, records)]
    lists = [pltpu.with_memory_space_constraint(x, pltpu.HBM) for x in (slots, counts)]
    more = [pltpu.with_memory_space_constraint(x, pltpu.HBM) for x in (own_nodes, arrive_nodes)]
    small = [pltpu.SMEM((1, 4, MOVERS), jnp.int32), pltpu.SMEM((1, 4), jnp.int32)]
    rec = pltpu.VMEM((SLOTS, CHANNELS, NODES), F32)
    a1, a0, conc_v, pot_v, eps_v, arrive_v, xr, rows, cells, state, acc = call(
        first_kernel,
        "first",
        [HBM] * 8 + [SMEM],
        [
            shape(Y_END, 8, NZ), shape(Y_END, 8, NZ), shape(3, BX, BY, NZ), core, core,
            jax.ShapeDtypeStruct((1, 4, MOVERS, NODES), jnp.int32),
            shape(2, X_POT, NZ), *store(STORE, jax.ShapeDtypeStruct), shape(8, NZ), sums,
        ],
        [rec, pltpu.VMEM((SLOTS, NODES), jnp.int32), *small, pltpu.SMEM((SLOTS,), jnp.int32), pltpu.SemaphoreType.DMA((12,))],
    )(*ins, *more, *lists, count)
    y0, y1 = swap(a0, "gy", 0), swap(a1, "gy", 1)
    late, acc = call(
        kept_kernel, "spread_kept", [VMEM] * 4, [shape(8, NZ), sums], flops=row_flops * EARLY * GROUP, aliases={0: 1}
    )(acc, rows, cells, state)
    b1, b0 = call(pack_x_kernel, "pack_x", [VMEM] * 6, [shape(X_END, NZ)] * 2)(xr, pot_v, eps_v, y1, y0, late)
    x1, x0 = swap(b1, "gx", 1), swap(b0, "gx", 0)
    rows, cells, state, acc = call(
        arrive_y_kernel,
        "spread_y",
        [VMEM] * 7,
        [*store(GROUP, jax.ShapeDtypeStruct), shape(8, NZ), sums],
        store(STORE + 2 * MOVERS + GROUP),
        flops=row_flops * 48,
        aliases={0: 3},
    )(acc, rows, cells, state, y0, y1, arrive_v)
    conc_near, acc, dens, c1, c0 = call(
        arrive_x_kernel,
        "spread_x",
        [VMEM] * 11,
        [shape(3, BX, BY, NZ), sums, shape(WIDE, EXT, NZ), shape(DY_END, NZ), shape(DY_END, NZ)],
        store(2 * MOVERS + 2 * GROUP) + [pltpu.VMEM((4, WIDE, 32, NZ), F32)],
        flops=row_flops * 2 * MOVERS,
        aliases={0: 1},
    )(acc, rows, cells, state, x1, x0, y0, y1, arrive_v, conc_v, pot_v)
    r0, r1 = swap(c0, "gy", 0), swap(c1, "gy", 1)
    conc_next, force, base, *weights = call(
        coefficient_kernel,
        "coefficients",
        [VMEM] * 8,
        [shape(3, BX, BY, NZ), shape(3, WIDE, BY, NZ)] + [field] * 8,
        [pltpu.VMEM((EXT, EXT, NZ), F32)] * 2 + [pltpu.SemaphoreType.DMA],
        flops=row_flops * 8,
        far_outs=(0,),
    )(acc, x0, x1, y0, y1, pot_v, eps_v, conc_near)
    dext, fcore, e1, e0 = call(
        join_y_kernel, "join_y", [VMEM] * 4, [field, shape(3, WIDE, BY, NZ), shape(DX_END, NZ), shape(DX_END, NZ)]
    )(dens, force, r1, r0)
    g1, g0 = swap(e1, "gx", 1), chip_pair(e0)
    scratch = [pltpu.VMEM((EXT, EXT, NZ), F32)] * 3
    near, edges = call(
        near_kernel,
        "sweeps_near",
        [VMEM] * 10,
        [shape(BX // 2, BY, NZ), shape(2 * SWEEPS - 2, EXT, NZ)],
        scratch,
        flops=12 * SWEEPS * EXT * EXT * NZ,
    )(dext, g0, base, *weights)
    pot_next, body_force = call(
        far_kernel,
        "sweeps_far",
        [VMEM] * 14,
        [core, shape(3, BX, BY, NZ)],
        scratch + [pltpu.VMEM((3, BX, BY, NZ), F32)] + [pltpu.VMEM((W, BY, NZ), F32)] * 2 + [pltpu.SemaphoreType.DMA((3,))],
        flops=8 * SWEEPS * EXT * EXT * NZ,
        far_outs=(0, 1),
    )(dext, g1, g0, fcore, base, *weights, near, edges)
    return conc_next, pot_next, body_force


def solution(mesh):
    placed = (
        P(None, "gx", "gy", None),
        P("gx", "gy", None),
        P("gx", "gy", None),
        P(("gx", "gy"), None, None),
        P(("gx", "gy")),
        P(("gx", "gy"), None, None),
        P(("gx", "gy"), None),
        P(("gx", "gy"), None),
        P(("gx", "gy"), None, None, None),
    )
    return jax.shard_map(
        body,
        mesh=mesh,
        in_specs=placed,
        out_specs=(P(None, "gx", "gy", None), P("gx", "gy", None), P(None, "gx", "gy", None)),
        check_vma=False,
    )
```

```python
import jax
import jax.numpy as jnp
from jax import lax
from jax.experimental import pallas as pl
from jax.experimental.pallas import tpu as pltpu
from jax.sharding import PartitionSpec as P

SWEEPS = 8
DIFFUSION = (1.0, 0.7, 0.45)
VALENCE = (1.0, -1.0, 2.0)
TIME_STEP = 0.05
SCREENING = 0.05

F32 = jnp.float32
BF16 = jnp.bfloat16
BX, BY, NZ = 16, 16, 128
SLOTS, MOVERS, CHANNELS, NODES = 128, 16, 4, 128
W = 8
EXT = BX + 2 * W
WIDE = BX + 2
PAIRS = WIDE * WIDE // 2
ROWS = PAIRS * 2 * CHANNELS
GROUP = 8
EARLY = 8
STORE = SLOTS + 4 * MOVERS + 2 * GROUP

Y_CONC, Y_POT, Y_EPS, Y_NUM, Y_END = 8, 14, 30, 46, 47
X_AT = [0] + [sum(EXT - 2 * d for d in range(1, n + 1)) for n in range(W + 1)]
X_CONC, X_NUM, X_POT = 64, 112, 120
X_EPS = X_POT + X_AT[W + 1]
X_END = X_EPS + X_AT[W + 1]
DY_FORCE, DY_END = WIDE * W, WIDE * W + 56
DX_AT = [sum(EXT - 2 - 2 * d for d in range(n)) for n in range(W + 1)]
DX_FORCE, DX_END = DX_AT[W], DX_AT[W] + 3 * BY

VMEM = pl.BlockSpec(memory_space=pltpu.VMEM)
SMEM = pl.BlockSpec(memory_space=pltpu.SMEM)
HBM = pl.BlockSpec(memory_space=pltpu.HBM)


def parity(axis):
    return lax.rem(lax.axis_index(axis), 2)


def swap(block, axis, odd):
    count = lax.axis_size(axis)
    route = [(i, (((i - odd) % count ^ 1) + odd) % count) for i in range(count)]
    return lax.ppermute(block, axis, route)


def chip_pair(block):
    pairs = [[i, i + 1] for i in range(0, lax.axis_size("gx"), 2)]
    return lax.all_gather(block, "gx", axis_index_groups=pairs)


def hot_group(first, number, rec, cells):
    sub = lax.broadcasted_iota(jnp.int32, (16, NODES), 0)
    second = (sub >= 8).astype(F32)
    subf = sub.astype(F32)
    left, right = [], []
    for g in range(number):
        cell, value = cells[first + g], rec[first + g]
        half = (cell >= PAIRS * NZ).astype(jnp.int32)
        high = ((cell - half * (PAIRS * NZ)) >> 7).astype(F32)
        low = ((cell & (NZ - 1)) + half * NZ).astype(F32)
        high = (jnp.broadcast_to(high, (16, NODES)) - second).astype(BF16)
        low = (jnp.broadcast_to(low, (16, NODES)) - subf).astype(BF16)
        lead = value.astype(BF16).astype(F32)
        rest = value - lead
        parts = jnp.concatenate([lead, rest, lead, rest], axis=0).astype(BF16)
        left.append(jnp.concatenate([jnp.where(high == BF16(2 * m), parts, BF16(0)) for m in range(ROWS // 16)], axis=0))
        right.append(jnp.concatenate([jnp.where(low == BF16(16 * m), BF16(1), BF16(0)) for m in range(16)], axis=0))
    left, right = jnp.concatenate(left, axis=1), jnp.concatenate(right, axis=1)
    sums = lax.dot_general(left, right, (((1,), (1,)), ((), ())), preferred_element_type=F32)
    return sums[:, :NZ], sums[:, NZ:]


def spread_groups(start, stop, rec, cells, acc):
    def groups(number):
        def group(c, first):
            left, right = hot_group(first, number, rec, cells)
            acc[0] += left
            acc[1] += right
            return first + number

        return group

    count = stop - start
    first = lax.fori_loop(0, count // 4, groups(4 * GROUP), start * GROUP)
    first = lax.fori_loop(0, lax.rem(count, 4) // 2, groups(2 * GROUP), first)
    lax.fori_loop(0, lax.rem(count, 2), groups(GROUP), first)


def mirrored(px, low, high):
    return jnp.where(px == 1, high, low)


def number_in(tile):
    return jnp.max(tile).astype(jnp.int32)


def append(total, buf, number, way, nodes, rec, cells):
    for k in range(MOVERS):
        rec[total + k] = buf[record(buf, k)]
        cells[total + k] = nodes[0, way, k : k + 1]
    return total + number_in(number)


def way_of(axis, odd):
    p = parity(axis)
    up = 1 - p if odd == 0 else p
    return up, (1 if axis == "gx" else 3) - up


def pack_records(out, rec, slots, number, way):
    for k in range(MOVERS):
        row = rec[slots[0, way, k]]
        out[record(out, k)] = jnp.where(k < number, row, 0.0)


def record(buf, k):
    return (k // 2, pl.ds((k % 2) * 4, 4)) if len(buf.shape) == 3 else (pl.ds(4 * k, 4),)


def first_kernel(
    conc_h, pot_h, eps_h, rec_h, nodes_h, arrive_h, slots_h, counts_h, count,
    s1, s0, conc, pot, eps, arrive, xr, rows, cells, state, acc,
    rec, nodes, slots, counts, gone, sems,
):
    copies = [(slots_h, slots), (counts_h, counts), (rec_h, rec), (nodes_h, nodes), (conc_h, conc)]
    for odd, out in enumerate((s0, s1)):
        start = pl.multiple_of(way_of("gy", odd)[0] * W, W)
        copies.append((pot_h.at[:, pl.ds(start, W)], out.at[pl.ds(Y_POT, BX)]))
        copies.append((eps_h.at[:, pl.ds(start, W)], out.at[pl.ds(Y_EPS, BX)]))
    copies += [(pot_h, pot), (eps_h, eps), (arrive_h, arrive)]
    copies = [pltpu.make_async_copy(a, b, sems.at[n]) for n, (a, b) in enumerate(copies)]
    for copy in copies:
        copy.start()
    acc[...] = jnp.zeros_like(acc)

    def clear(c, _):
        gone[c] = 0
        return 0

    lax.fori_loop(0, SLOTS, clear, 0, unroll=16)
    for copy in copies[:2]:
        copy.wait()
    for way in range(4):
        number = counts[0, way]
        for k in range(MOVERS):
            gone[jnp.where(k < number, slots[0, way, k], SLOTS)] = 1
    live = count[0]
    for copy in copies[2:4]:
        copy.wait()

    def gather(c, found):
        rows[found] = rec[c]
        cells[found] = nodes[pl.ds(c, 1), :]
        stays = jnp.logical_and(c < live, gone[c] == 0)
        return found + stays.astype(jnp.int32)

    found = lax.fori_loop(0, SLOTS, gather, 0, unroll=16)
    state[...] = jnp.full((8, NZ), found.astype(F32))
    copies[4].wait()
    for odd in range(2):
        up, way = way_of("gx", odd)
        number = counts[0, way]
        pack_records(xr.at[odd], rec, slots, number, way)
        xr[odd, X_CONC:X_NUM] = conc[:, up * (BX - 1)].reshape(X_NUM - X_CONC, NZ)
        xr[odd, X_NUM:X_POT] = jnp.full((8, NZ), number.astype(F32))
    for odd, out in enumerate((s0, s1)):
        up, way = way_of("gy", odd)
        number = counts[0, way]
        pack_records(out, rec, slots, number, way)
        out[Y_NUM] = jnp.full((8, NZ), number.astype(F32))
        for s in range(3):
            face = jnp.where(up == 1, conc[s, :, BY - 1], conc[s, :, 0])
            out[Y_CONC + 2 * s : Y_CONC + 2 * s + 2] = face.reshape(2, 8, NZ)
    for copy in copies[5:]:
        copy.wait()


def kept_kernel(acc_in, rows, cells, state, state_out, acc):
    del acc_in
    state_out[...] = state[...]
    spread_groups(0, jnp.minimum(EARLY, number_in(state[...]) // GROUP), rows, cells, acc)


def pack_x_kernel(xr, pot, eps, y1, y0, state, s1, s0):
    del state
    px, py = parity("gx"), parity("gy")
    for n, (out, up) in enumerate(((s0, 1 - px), (s1, px))):
        out[0:X_POT] = xr[n]
        for first, own, tile in ((X_POT, pot, Y_POT), (X_EPS, eps, Y_EPS)):
            for d in range(1, W + 1):
                x = jnp.where(up == 1, BX - d, d - 1)
                a, b = y0[tile + x], y1[tile + x]
                low, high = jnp.where(py == 1, a, b), jnp.where(py == 1, b, a)
                at = first + X_AT[d]
                if d < W:
                    out[at : at + W - d] = low[d:]
                    out[at + W - d + BY : at + 2 * (W - d) + BY] = high[: W - d]
                out[at + W - d : at + W - d + BY] = own[x]


def arrive_y_kernel(acc_in, rows_in, cells_in, state, y0, y1, nodes, rows, cells, state_out, acc):
    del acc_in, rows_in, cells_in
    py = parity("gy")
    found = number_in(state[...])
    total = append(found, y0, y0[Y_NUM], 3 - py, nodes, rows, cells)
    total = append(total, y1, y1[Y_NUM], 2 + py, nodes, rows, cells)
    spread_groups(jnp.minimum(EARLY, found // GROUP), total // GROUP, rows, cells, acc)
    state_out[...] = jnp.full((8, NZ), total.astype(F32))


def spread_rows(acc, channel, ex, first, number):
    half, row = divmod(ex, WIDE // 2)
    base = (row * WIDE + first) * 8 + channel
    return acc[half, pl.ds(base, number, stride=8)] + acc[half, pl.ds(base + 4, number, stride=8)]


def arrive_x_kernel(
    acc_in, rows_in, cells_in, state, x1, x0, y0, y1, nodes, conc, pot,
    conc_next, acc, dens, s1, s0, rows, cells,
    wide,
):
    del acc_in, rows_in, cells_in
    px, py = parity("gx"), parity("gy")
    x_low_first, y_low_first = px == 1, py == 1
    before = number_in(state[...])
    total = append(before, x0, x0[X_NUM:X_POT], 1 - px, nodes, rows, cells)
    total = append(total, x1, x1[X_NUM:X_POT], px, nodes, rows, cells)
    for g in range(GROUP):
        rows[total + g] = jnp.zeros((CHANNELS, NODES), F32)
        cells[total + g] = jnp.zeros((1, NODES), jnp.int32)
    spread_groups(before // GROUP, (total + GROUP - 1) // GROUP, rows, cells, acc)

    for f in range(4):
        wide[f, 1 : BX + 1, 8 : 8 + BY] = conc[f] if f < 3 else pot[...]
        if f < 3:
            xa, xb = (x[X_CONC + BY * f : X_CONC + BY * f + BY] for x in (x0, x1))
            x_low, x_high = jnp.where(x_low_first, xa, xb), jnp.where(x_low_first, xb, xa)
            ya, yb = (y[Y_CONC + 2 * f : Y_CONC + 2 * f + 2].reshape(BX, NZ) for y in (y0, y1))
            y_low, y_high = jnp.where(y_low_first, ya, yb), jnp.where(y_low_first, yb, ya)
        else:
            xa, xb = (x[X_POT + W - 1 : X_POT + W - 1 + BY] for x in (x0, x1))
            x_low, x_high = jnp.where(x_low_first, xa, xb), jnp.where(x_low_first, xb, xa)
            y_low = jnp.where(y_low_first, y0[Y_POT:Y_EPS, 7], y1[Y_POT:Y_EPS, 7])
            y_high = jnp.where(y_low_first, y1[Y_POT:Y_EPS, 0], y0[Y_POT:Y_EPS, 0])
        wide[f, 0, 8 : 8 + BY] = x_low
        wide[f, BX + 1, 8 : 8 + BY] = x_high
        wide[f, 1 : BX + 1, 7] = y_low
        wide[f, 1 : BX + 1, 8 + BY] = y_high

    dens[...] = jnp.zeros_like(dens)
    for ex in range(WIDE):
        dens[ex, 7 : 7 + WIDE] = spread_rows(acc, 0, ex, 0, WIDE)

    def around(f, x):
        c = wide[f, x + 1, 8:24]
        beside = (wide[f, x + 2, 8:24], wide[f, x, 8:24], wide[f, x + 1, 9:25], wide[f, x + 1, 7:23])
        return c, (*beside, pltpu.roll(c, NZ - 1, 1), pltpu.roll(c, 1, 1))

    def total_of(terms):
        return ((terms[0] + terms[1]) + (terms[2] + terms[3])) + (terms[4] + terms[5])

    for x in range(BX):
        p, steps = around(3, x)
        steps = [q - p for q in steps]
        total = dens[x + 1, 8:24]
        for s in range(3):
            c, beside = around(s, x)
            plain = total_of([n - c for n in beside])
            drift = total_of([(n + c) * q for n, q in zip(beside, steps)])
            later = c + (TIME_STEP * DIFFUSION[s]) * (plain + (VALENCE[s] * 0.5) * drift)
            conc_next[s, x] = later
            total = total + VALENCE[s] * later
        dens[x + 1, 8:24] = total

    for out, up in ((s0, 1 - py), (s1, py)):
        for ex in range(WIDE):
            out[ex * 8 : ex * 8 + 8] = jnp.where(up == 1, dens[ex, 17:25], dens[ex, 7:15])
        for a in range(3):
            for half in range(2):
                rims = []
                for ey in (0, WIDE - 1):
                    base = ey * 8 + a + 1
                    lead = acc[half, pl.ds(base, WIDE // 2, stride=WIDE * 8)]
                    rims.append(lead + acc[half, pl.ds(base + 4, WIDE // 2, stride=WIDE * 8)])
                r = DY_FORCE + a * WIDE + half * (WIDE // 2)
                out[r : r + WIDE // 2] = jnp.where(up == 1, rims[1], rims[0])
        out[DY_FORCE + 54 : DY_END] = jnp.zeros((2, NZ), F32)


def coefficient_kernel(acc, x0, x1, y0, y1, pot, eps, conc_next, conc_out, force, base, xp, xm, yp, ym, zp, zm, inv, phi, ew, sem):
    copy = pltpu.make_async_copy(conc_next, conc_out, sem)
    copy.start()
    px, y_low_first = parity("gx"), parity("gy") == 1
    for c in range(3):
        for ex in range(WIDE):
            force[c, ex] = spread_rows(acc, c + 1, ex, 1, BY)
    for buf, own, x_tile, y_tile in ((phi, pot, X_POT, Y_POT), (ew, eps, X_EPS, Y_EPS)):
        for n in range(BX):
            x = mirrored(px, n, BX - 1 - n)
            a, b = y0[y_tile + x], y1[y_tile + x]
            buf[W + n, 0:W] = jnp.where(y_low_first, a, b)
            buf[W + n, W : W + BY] = own[x]
            buf[W + n, W + BY : EXT] = jnp.where(y_low_first, b, a)
        for n in (*range(W), *range(W + BX, EXT)):
            buf[n] = jnp.ones((EXT, NZ), F32)
        for d in range(1, W + 1):
            at = slice(x_tile + X_AT[d], x_tile + X_AT[d + 1])
            buf[W - d, d : EXT - d] = x1[at]
            buf[W + BX - 1 + d, d : EXT - d] = x0[at]
    for x in range(1, EXT - 1):
        e = ew[x]
        up, down = e + ew[x + 1], e + ew[x - 1]
        north, south = e + pltpu.roll(e, EXT - 1, 0), e + pltpu.roll(e, 1, 0)
        over = e + pltpu.roll(e, NZ - 1, 1)
        under = pltpu.roll(over, 1, 1)
        scale = 1.0 / ((((up + down) + (north + south)) + (over + under)) + 2.0 * SCREENING)
        xp[x], xm[x] = up * scale, down * scale
        yp[x], ym[x] = north * scale, south * scale
        zp[x], zm[x] = over * scale, under * scale
        inv[x] = 2.0 * scale
    for buf in (xp, xm, yp, ym, zp, zm, inv, base):
        buf[0] = jnp.zeros((EXT, NZ), F32)
        buf[EXT - 1] = jnp.zeros((EXT, NZ), F32)
    for x in range(1, EXT - 1):
        base[x] = sweep_plane(1, x, phi.at[x - 1], phi.at[x], phi.at[x + 1], (xp, xm, yp, ym, zp, zm), None)
    copy.wait()


def join_y_kernel(dens, force, r1, r0, dext, fcore, s1, s0):
    px, py = parity("gx"), parity("gy")
    low_first = py == 1
    dext[0:7] = jnp.zeros((7, EXT, NZ), F32)
    dext[25:32] = jnp.zeros((7, EXT, NZ), F32)
    for n in range(WIDE):
        ex = mirrored(px, n, WIDE - 1 - n)
        dext[n + 7] = dens[ex]
        at = pl.ds(pl.multiple_of(ex * 8, 8), 8)
        a, b = r0[at], r1[at]
        dext[n + 7, 1:9] += jnp.where(low_first, a, b)
        dext[n + 7, 23:31] += jnp.where(low_first, b, a)
    fcore[...] = force[...]
    for c in range(3):
        r = DY_FORCE + c * WIDE
        a, b = r0[r : r + WIDE], r1[r : r + WIDE]
        fcore[c, :, 0] += jnp.where(low_first, a, b)
        fcore[c, :, BY - 1] += jnp.where(low_first, b, a)
    pack_rims(dext, fcore, s1, px, 7, 1)
    pack_rims(dext, fcore, s0, 1 - px, 24, -1)


def pack_rims(dext, fcore, out, up, first, way):
    for d in range(W):
        out[DX_AT[d] : DX_AT[d + 1]] = dext[first + way * d, d + 1 : 31 - d]
    for c in range(3):
        out[DX_FORCE + c * BY : DX_FORCE + (c + 1) * BY] = fcore[c, up * (WIDE - 1)]


def sweep_plane(k, x, west, here, east, weights, rhs):
    xp, xm, yp, ym, zp, zm = weights
    if k < SWEEPS:
        f = slice(0, EXT)
        north, south = pltpu.roll(here[...], EXT - 1, 0), pltpu.roll(here[...], 1, 0)
    else:
        f = slice(W, W + BY)
        north, south = here[W + 1 : W + BY + 1], here[W - 1 : W + BY - 1]
    centre = here[f]
    total = (xp[x, f] * east[f] + xm[x, f] * west[f]) + (yp[x, f] * north + ym[x, f] * south)
    along = zp[x, f] * pltpu.roll(centre, NZ - 1, 1) + zm[x, f] * pltpu.roll(centre, 1, 1)
    return total + (along if rhs is None else along + rhs[x, f])


def near_kernel(dext, r0, base, xp, xm, yp, ym, zp, zm, inv, near, edges, phi_a, phi_b, rhs):
    weights, other = (xp, xm, yp, ym, zp, zm), 1 - parity("gx")
    rhs[9 : EXT - 1] = dext[9 : EXT - 1]
    for d in range(W):
        rhs[23 + d, d + 1 : 31 - d] += r0[other, DX_AT[d] : DX_AT[d + 1]]
    rhs[9 : EXT - 1] = rhs[9 : EXT - 1] * inv[9 : EXT - 1]
    for k in range(1, SWEEPS + 1):
        old, new = (phi_a, phi_b)[k % 2], (phi_a, phi_b)[(k + 1) % 2]
        for x in range(W + k, EXT - k):
            if k == 1:
                total = base[x] + rhs[x]
            else:
                total = sweep_plane(k, x, old.at[x - 1], old.at[x], old.at[x + 1], weights, rhs)
            if k == SWEEPS:
                near[x - 16] = total
                continue
            new[x] = total
            if x < W + k + 2:
                edges[2 * k - 2 + x - W - k] = total


def far_kernel(
    dext, r1, r0, fcore, base, xp, xm, yp, ym, zp, zm, inv, near, edges,
    pot_next, force_out,
    phi_a, phi_b, rhs, force, lower, upper, sems,
):
    px = parity("gx")
    weights = (xp, xm, yp, ym, zp, zm)
    low_first = px == 1
    force[...] = fcore[:, 1 : BX + 1]
    a, b = (r[DX_FORCE:DX_END].reshape(3, BY, NZ) for r in (r0.at[1 - px], r1))
    force[:, 0] += jnp.where(low_first, a, b)
    force[:, BX - 1] += jnp.where(low_first, b, a)
    for n in range(W):
        upper[n] = near[mirrored(px, n, W - 1 - n)]
    copies = [
        pltpu.make_async_copy(force, force_out, sems.at[0]),
        pltpu.make_async_copy(upper, pot_next.at[pl.ds(mirrored(px, W, 0), W)], sems.at[1]),
        pltpu.make_async_copy(lower, pot_next.at[pl.ds(mirrored(px, 0, W), W)], sems.at[2]),
    ]
    copies[0].start()
    copies[1].start()

    rhs[1:16] = dext[1:16]
    for d in range(W):
        rhs[8 - d, d + 1 : 31 - d] += r1[DX_AT[d] : DX_AT[d + 1]]
    rhs[1:16] = rhs[1:16] * inv[1:16]

    def plane(k, x):
        return edges.at[2 * k - 2 + x - W - k] if x >= W + k else (phi_a, phi_b)[(k + 1) % 2].at[x]

    for k in range(1, SWEEPS + 1):
        for x in range(k, W + k):
            if k == 1:
                total = base[x] + rhs[x]
            else:
                total = sweep_plane(k, x, plane(k - 1, x - 1), plane(k - 1, x), plane(k - 1, x + 1), weights, rhs)
            if k < SWEEPS:
                plane(k, x)[...] = total
            else:
                lower[mirrored(px, x - W, 15 - x)] = total
    copies[2].start()
    for copy in copies:
        copy.wait()


def shape(*dims):
    return jax.ShapeDtypeStruct(dims, F32)


def call(kernel, name, ins, outs, scratch=(), flops=0, aliases=None, far_outs=()):
    moved = 4 * sum(int(o.size) for o in outs)
    return pl.pallas_call(
        kernel,
        name=name,
        in_specs=ins,
        out_specs=[HBM if n in far_outs else VMEM for n in range(len(outs))],
        out_shape=outs,
        scratch_shapes=scratch,
        input_output_aliases=aliases or {},
        compiler_params=pltpu.CompilerParams(vmem_limit_bytes=32 << 20),
        cost_estimate=pl.CostEstimate(flops=flops, bytes_accessed=moved, transcendentals=0),
    )


def body(conc, pot, eps, records, count, slots, counts, own_nodes, arrive_nodes):
    def store(number, kind=pltpu.VMEM):
        return [kind((number, CHANNELS, NODES), F32), kind((number, 1, NODES), jnp.int32)]

    sums = shape(2, ROWS, NZ)
    row_flops = 2 * ROWS * 2 * NZ * NODES
    field = shape(EXT, EXT, NZ)
    core = shape(BX, BY, NZ)

    ins = [pltpu.with_memory_space_constraint(x, pltpu.HBM) for x in (conc, pot, eps, records)]
    lists = [pltpu.with_memory_space_constraint(x, pltpu.HBM) for x in (slots, counts)]
    more = [pltpu.with_memory_space_constraint(x, pltpu.HBM) for x in (own_nodes, arrive_nodes)]
    small = [pltpu.SMEM((1, 4, MOVERS), jnp.int32), pltpu.SMEM((1, 4), jnp.int32)]
    rec = pltpu.VMEM((SLOTS, CHANNELS, NODES), F32)
    a1, a0, conc_v, pot_v, eps_v, arrive_v, xr, rows, cells, state, acc = call(
        first_kernel,
        "first",
        [HBM] * 8 + [SMEM],
        [
            shape(Y_END, 8, NZ), shape(Y_END, 8, NZ), shape(3, BX, BY, NZ), core, core,
            jax.ShapeDtypeStruct((1, 4, MOVERS, NODES), jnp.int32),
            shape(2, X_POT, NZ), *store(STORE, jax.ShapeDtypeStruct), shape(8, NZ), sums,
        ],
        [rec, pltpu.VMEM((SLOTS, NODES), jnp.int32), *small, pltpu.SMEM((SLOTS + 1,), jnp.int32), pltpu.SemaphoreType.DMA((12,))],
    )(*ins, *more, *lists, count)
    y0, y1 = swap(a0, "gy", 0), swap(a1, "gy", 1)
    late, acc = call(
        kept_kernel, "spread_kept", [VMEM] * 4, [shape(8, NZ), sums], flops=row_flops * EARLY * GROUP, aliases={0: 1}
    )(acc, rows, cells, state)
    b1, b0 = call(pack_x_kernel, "pack_x", [VMEM] * 6, [shape(X_END, NZ)] * 2)(xr, pot_v, eps_v, y1, y0, late)
    x1, x0 = swap(b1, "gx", 1), swap(b0, "gx", 0)
    rows, cells, state, acc = call(
        arrive_y_kernel,
        "spread_y",
        [VMEM] * 7,
        [*store(STORE, jax.ShapeDtypeStruct), shape(8, NZ), sums],
        flops=row_flops * 48,
        aliases={0: 3, 1: 0, 2: 1},
    )(acc, rows, cells, state, y0, y1, arrive_v)
    conc_near, acc, dens, c1, c0, _, _ = call(
        arrive_x_kernel,
        "spread_x",
        [VMEM] * 11,
        [shape(3, BX, BY, NZ), sums, shape(WIDE, EXT, NZ), shape(DY_END, NZ), shape(DY_END, NZ), *store(STORE, jax.ShapeDtypeStruct)],
        [pltpu.VMEM((4, WIDE, 32, NZ), F32)],
        flops=row_flops * 2 * MOVERS,
        aliases={0: 1, 1: 5, 2: 6},
    )(acc, rows, cells, state, x1, x0, y0, y1, arrive_v, conc_v, pot_v)
    r0, r1 = swap(c0, "gy", 0), swap(c1, "gy", 1)
    conc_next, force, base, *weights = call(
        coefficient_kernel,
        "coefficients",
        [VMEM] * 8,
        [shape(3, BX, BY, NZ), shape(3, WIDE, BY, NZ)] + [field] * 8,
        [pltpu.VMEM((EXT, EXT, NZ), F32)] * 2 + [pltpu.SemaphoreType.DMA],
        flops=row_flops * 8,
        far_outs=(0,),
    )(acc, x0, x1, y0, y1, pot_v, eps_v, conc_near)
    dext, fcore, e1, e0 = call(
        join_y_kernel, "join_y", [VMEM] * 4, [field, shape(3, WIDE, BY, NZ), shape(DX_END, NZ), shape(DX_END, NZ)]
    )(dens, force, r1, r0)
    g1, g0 = swap(e1, "gx", 1), chip_pair(e0)
    scratch = [pltpu.VMEM((EXT, EXT, NZ), F32)] * 3
    near, edges = call(
        near_kernel,
        "sweeps_near",
        [VMEM] * 10,
        [shape(BX // 2, BY, NZ), shape(2 * SWEEPS - 2, EXT, NZ)],
        scratch,
        flops=12 * SWEEPS * EXT * EXT * NZ,
    )(dext, g0, base, *weights)
    pot_next, body_force = call(
        far_kernel,
        "sweeps_far",
        [VMEM] * 14,
        [core, shape(3, BX, BY, NZ)],
        scratch + [pltpu.VMEM((3, BX, BY, NZ), F32)] + [pltpu.VMEM((W, BY, NZ), F32)] * 2 + [pltpu.SemaphoreType.DMA((3,))],
        flops=8 * SWEEPS * EXT * EXT * NZ,
        far_outs=(0, 1),
    )(dext, g1, g0, fcore, base, *weights, near, edges)
    return conc_next, pot_next, body_force


def solution(mesh):
    placed = (
        P(None, "gx", "gy", None),
        P("gx", "gy", None),
        P("gx", "gy", None),
        P(("gx", "gy"), None, None),
        P(("gx", "gy")),
        P(("gx", "gy"), None, None),
        P(("gx", "gy"), None),
        P(("gx", "gy"), None),
        P(("gx", "gy"), None, None, None),
    )
    return jax.shard_map(
        body,
        mesh=mesh,
        in_specs=placed,
        out_specs=(P(None, "gx", "gy", None), P("gx", "gy", None), P(None, "gx", "gy", None)),
        check_vma=False,
    )
```
